32 devices in a mesh: grp: 2 (over y), exp: 8 (over z, x), hid: 2 (over core).
Axes of the slice: x: 2, y: 2, z: 4, core: 2. Of those that a mesh axis runs over, the one named last changes fastest.
Arguments:
- tokens: bfloat16 [64, 4096], P(('grp', 'exp')), parts along dimension 0, may hold values from -6 to 6
- w_gate: bfloat16 [4096, 32768], P(None, ('exp', 'hid')), may hold values from -0.09375 to 0.09375
- w_up: bfloat16 [4096, 32768], P(None, ('exp', 'hid')), may hold values from -0.09375 to 0.09375
- w_down: bfloat16 [32768, 4096], P(('exp', 'hid')), may hold values from -0.0625 to 0.0625
- block_counts: int32 [8], P('grp'), parts along dimension 0, may hold values from 1 to 1, as said below
- block_rows: int32 [8, 128], P('grp'), parts along dimension 0, may hold values from -1 to 31, as said below
- row_gates: float32 [8, 128], P('grp'), parts along dimension 0, may hold values from 0.1 to 1
Outputs:
- mixed: bfloat16 [64, 4096], P(('grp', 'exp'), 'hid'), parts along dimension 0
The draws below stay inside these ranges and needn't reach their ends.
There are 2 independent parts, one for each index of `grp`. The reference program is written for one: setup_inputs(seed, part) draws one part's arguments, and reference() takes and returns one part's arrays. A program takes and returns all parts, laid end to end along the dimension named above; an argument that names none is the same for every part. Nothing has to cross between parts.
Inputs may be any that keep to these rules, and one draw needn't show every extreme that they name: `block_rows`: in the first block_counts[e] * 128 slots of expert e, the entries other than -1 fill its first slots and are distinct; the slots after them hold stale token indices, which are not live. Every token stands among the live entries of exactly 2 experts. Of one expert's live entries at most 3 name tokens of one aligned block of 4 tokens, and some expert has exactly 3 from every such block in every draw. block_counts[e] is the number of blocks of 128 slots of expert e that hold a live entry; some expert has 1 in every draw.
All inputs are finite; a program needn't handle non-finite values.
Results may differ from the reference program's by a relative error of at most 0.0058.
Values may be sent and summed in bfloat16 or wider, within the bound.
No kernel may reach another device: no remote copies, remote signals or barrier semaphores. Data moves between devices by JAX's collectives and lax.ppermute only.
A program may use at most 128 MiB of HBM per device.

```python
import math
import jax
import jax.numpy as jnp
from jax import lax

D = 4096
FF = 8192
EXPERTS = 4
TOP = 2
BLOCK = 128
TOK_DEV = 4
CAP = 3
TOKENS = 32
MAXB = 1
N_EXP = 8


def routing_tables(key):
    source_count = TOKENS // TOK_DEV
    slot_count = MAXB * BLOCK
    key_fav, key_swing, key_order, key_pair, key_slot, key_stale = jax.random.split(key, 6)
    favourite = jax.random.randint(key_fav, (), 0, EXPERTS).astype(jnp.int32)
    remaining = TOP * TOK_DEV - CAP
    base_share = remaining // (EXPERTS - 1)
    leftover = remaining - base_share * (EXPERTS - 1)
    swing = jax.random.randint(key_swing, (source_count,), 0, 2).astype(jnp.int32)
    extra_share = (jnp.arange(EXPERTS - 1) < leftover).astype(jnp.int32)
    others_counts = base_share + extra_share[None, :] + jnp.zeros((source_count, EXPERTS - 1), jnp.int32)
    others_counts = others_counts.at[:, 0].add(swing).at[:, 1].add(-swing)
    scores = jax.random.randint(key_order, (source_count, EXPERTS - 1), 0, 1024) * 8 + jnp.arange(EXPERTS - 1)[None, :]
    others_order = jnp.argsort(scores, axis=1).astype(jnp.int32)
    others_ids = (favourite + 1 + others_order) % EXPERTS
    ordered_ids = jnp.concatenate([jnp.zeros((source_count, 1), jnp.int32) + favourite, others_ids], axis=1)
    ordered_counts = jnp.concatenate([jnp.zeros((source_count, 1), jnp.int32) + CAP, others_counts], axis=1)
    bounds = jnp.cumsum(ordered_counts, axis=1)
    spots = jnp.arange(TOP * TOK_DEV, dtype=jnp.int32)
    which = jnp.sum((spots[None, :, None] >= bounds[:, None, :]).astype(jnp.int32), axis=2)
    labels = jnp.take_along_axis(ordered_ids, which, axis=1)
    pair_scores = jax.random.randint(key_pair, (source_count, TOK_DEV), 0, 4096) * TOK_DEV + jnp.arange(TOK_DEV)[None, :]
    shuffle = jnp.argsort(pair_scores, axis=1).astype(jnp.int32)
    first = jnp.take_along_axis(labels[:, :TOK_DEV], shuffle, axis=1).reshape(TOKENS)
    second = jnp.take_along_axis(labels[:, TOK_DEV:], shuffle, axis=1).reshape(TOKENS)
    expert_ids = jnp.arange(EXPERTS, dtype=jnp.int32)[:, None]
    chosen = ((first[None, :] == expert_ids) | (second[None, :] == expert_ids)).astype(jnp.int32)
    visit = jax.random.permutation(key_slot, TOKENS).astype(jnp.int32)
    chosen_visit = chosen[:, visit]
    slot_pos = jnp.cumsum(chosen_visit, axis=1) - 1
    target = jnp.where(chosen_visit > 0, slot_pos, slot_count).astype(jnp.int32)
    filled = jnp.full((EXPERTS, slot_count + 1), -1, jnp.int32)
    filled = filled.at[expert_ids + jnp.zeros_like(target), target].set(visit[None, :] + jnp.zeros_like(target))
    block_counts = ((jnp.sum(chosen, axis=1) + BLOCK - 1) // BLOCK).astype(jnp.int32)
    position = jnp.arange(slot_count, dtype=jnp.int32)
    counted_slots = position[None, :] < block_counts[:, None] * BLOCK
    stale_rows = jax.random.randint(key_stale, (EXPERTS, slot_count), 0, TOKENS).astype(jnp.int32)
    block_rows = jnp.where(counted_slots, filled[:, :slot_count], stale_rows).astype(jnp.int32)
    return (block_counts, block_rows)


def draw_block_counts(key, part):
    block_counts, block_rows = routing_tables(key)
    return block_counts


def draw_block_rows(key, part):
    block_counts, block_rows = routing_tables(key)
    return block_rows


def block_scale(rng, shape, cuts, smallest, top_value):
    level, own = 1.0, jax.random.fold_in(rng, 6)
    for dim, blocks in cuts:
        heights = jnp.exp(jax.random.uniform(jax.random.fold_in(own, dim), (blocks,), jnp.float32, smallest / len(cuts), top_value / len(cuts)))
        level = level * jnp.repeat(heights, shape[dim] // blocks).reshape([-1 if axis == dim else 1 for axis in range(len(shape))])
    return level


def bell_draw(rng, extent, scale, bound, cuts=(), kind=jnp.bfloat16):
    drawn = scale * jax.random.normal(rng, extent, jnp.float32)
    if cuts:
        drawn = drawn * block_scale(rng, extent, cuts, -0.22, 0.18)
    return jnp.clip(drawn, -bound, bound).astype(kind)


def setup_inputs(seed: int = 0, part: int = 0) -> dict:
    seeds = jax.random.split(jax.random.key(seed), 8)
    part_keys = jax.random.split(jax.random.fold_in(seeds[7], part), 8)
    tokens = bell_draw(part_keys[0], (TOKENS, D), 1.0, 6.0, ((0, 8),))
    w_gate = bell_draw(seeds[1], (D, EXPERTS * FF), D ** -0.5, 0.09375, ((1, 16),))
    w_up = bell_draw(seeds[2], (D, EXPERTS * FF), D ** -0.5, 0.09375, ((1, 16),))
    w_down = bell_draw(seeds[3], (EXPERTS * FF, D), FF ** -0.5, 0.0625, ((0, 16),))
    block_counts = draw_block_counts(jax.random.fold_in(jax.random.fold_in(seeds[7], part), 71), part)
    block_rows = draw_block_rows(jax.random.fold_in(jax.random.fold_in(seeds[7], part), 71), part)
    row_gates = jnp.clip(jnp.exp(jax.random.uniform(part_keys[6], (EXPERTS, MAXB * BLOCK), jnp.float32, math.log(0.1), math.log(1.0))), 0.1, 1.0)
    return dict(tokens=tokens, w_gate=w_gate, w_up=w_up, w_down=w_down, block_counts=block_counts, block_rows=block_rows, row_gates=row_gates)


def reference(tokens, w_gate, w_up, w_down, block_counts, block_rows, row_gates):
    groups = 2 * N_EXP // EXPERTS
    group_width = FF // groups
    slot_count = MAXB * BLOCK
    position = jnp.arange(slot_count, dtype=jnp.int32)
    padded = jnp.concatenate([tokens, jnp.zeros((1, D), tokens.dtype)], axis=0)
    combined = jnp.zeros((TOKENS + 1, D), jnp.float32)
    for expert in range(EXPERTS):
        is_live = (position < block_counts[expert] * BLOCK) & (block_rows[expert] >= 0)
        slot_index = jnp.where(is_live, block_rows[expert], TOKENS).astype(jnp.int32)
        routed = padded[slot_index]
        gate_act = jnp.dot(routed, w_gate[:, expert * FF:(expert + 1) * FF], preferred_element_type=jnp.float32)
        up_act = jnp.dot(routed, w_up[:, expert * FF:(expert + 1) * FF], preferred_element_type=jnp.float32)
        hidden = (jax.nn.silu(gate_act) * up_act).astype(jnp.bfloat16)
        hidden_groups = jnp.transpose(hidden.reshape(slot_count, groups, group_width), (1, 0, 2))
        down_rows = w_down[expert * FF:(expert + 1) * FF].reshape(groups, group_width, D)

        def add_group(running, operands):
            hidden_part, weight_part = operands
            term = jnp.dot(hidden_part, weight_part, preferred_element_type=jnp.float32)
            rounded = lax.optimization_barrier(term.astype(jnp.bfloat16))
            return running + rounded.astype(jnp.float32), None

        expert_out, _ = lax.scan(add_group, jnp.zeros((slot_count, D), jnp.float32), (hidden_groups, down_rows))
        weights = jnp.where(is_live, row_gates[expert], 0.0).astype(jnp.float32)
        combined = combined.at[slot_index].add(weights[:, None] * expert_out)
    return combined[:TOKENS].astype(jnp.bfloat16)
```

```python
import functools

import jax
import jax.numpy as jnp
from jax import lax
from jax.experimental import pallas as pl
from jax.experimental.pallas import tpu as pltpu
from jax.sharding import PartitionSpec as P

BLOCK = 128
CAP = 3
TILE = 256
CHUNKS = 8
MIB = 1 << 20
HBM = pl.BlockSpec(memory_space=pltpu.HBM)
VMEM = pl.BlockSpec(memory_space=pltpu.VMEM)
SMEM = pl.BlockSpec(memory_space=pltpu.SMEM)


def chunk_copies(src, dst, sems):
    step = src.shape[0] // CHUNKS
    return [
        pltpu.make_async_copy(
            src.at[pl.ds(c * step, step)], dst.at[pl.ds(c * step, step)], sems.at[c]
        )
        for c in range(CHUNKS)
    ]


def fetch_kernel(wg_ref, wu_ref, wg_out, wu_out, sems):
    copies = chunk_copies(wg_ref, wg_out, sems.at[0]) + chunk_copies(wu_ref, wu_out, sems.at[1])
    for c in copies:
        c.start()
    for c in copies:
        c.wait()


def fetch(w_gate, w_up):
    return pl.pallas_call(
        fetch_kernel,
        out_shape=(pltpu.VMEM(w_gate.shape, w_gate.dtype), pltpu.VMEM(w_up.shape, w_up.dtype)),
        in_specs=[HBM, HBM],
        out_specs=(VMEM, VMEM),
        scratch_shapes=[pltpu.SemaphoreType.DMA((2, CHUNKS))],
        compiler_params=pltpu.CompilerParams(vmem_limit_bytes=1 * MIB),
        cost_estimate=pl.CostEstimate(
            flops=0, bytes_accessed=2 * (w_gate.size + w_up.size), transcendentals=0
        ),
    )(in_hbm(w_gate), in_hbm(w_up))


def token_gates(own, sources, per_expert, token_count, counts_ref, rows_ref, gates_ref):
    experts, slots = rows_ref.shape
    expert = own // per_expert
    mine = lax.broadcasted_iota(jnp.int32, (experts, slots), 0) == expert
    rows = jnp.sum(jnp.where(mine, rows_ref[...], 0), axis=0, keepdims=True)
    gates = jnp.sum(jnp.where(mine, gates_ref[...], 0.0), axis=0, keepdims=True)
    position = lax.broadcasted_iota(jnp.int32, (1, slots), 1)
    live = (position < counts_ref[expert] * BLOCK) & (rows >= 0)
    rows = jnp.where(live, rows, -1)
    total = sources * token_count
    line = lax.broadcasted_iota(jnp.int32, (total, slots), 0)
    start = lax.rem(own - line // token_count + sources, sources) * token_count
    token = start + lax.rem(line, token_count)
    return jnp.sum(jnp.where(rows == token, gates, 0.0), axis=1, keepdims=True)


def hidden_kernel(sources, per_expert, *refs):
    pieces = refs[:sources]
    (wg_ref, wu_ref, wd_ref, counts_ref, rows_ref, gates_ref, h_out, g_out, wd_out, wide, x_ref, sems) = refs[sources:]
    copies = chunk_copies(wd_ref, wd_out, sems)
    for c in copies:
        c.start()
    token_count = pieces[0].shape[0]
    for k, piece in enumerate(pieces):
        wide[pl.ds(k * token_count, token_count), :] = piece[...].astype(jnp.float32)
    x_ref[...] = wide[...].astype(jnp.bfloat16)
    own = lax.axis_index("exp")
    g = token_gates(own, sources, per_expert, token_count, counts_ref, rows_ref, gates_ref)
    g_out[...] = jnp.broadcast_to(g, g_out.shape)

    @pl.loop(0, wg_ref.shape[1] // TILE)
    def _(n):
        cols = pl.ds(pl.multiple_of(n * TILE, TILE), TILE)
        gate = jnp.dot(x_ref[...], wg_ref[:, cols], preferred_element_type=jnp.float32)
        up = jnp.dot(x_ref[...], wu_ref[:, cols], preferred_element_type=jnp.float32)
        h_out[:, cols] = (gate / (1.0 + jnp.exp(-gate)) * up).astype(jnp.bfloat16)

    for c in copies:
        c.wait()


def hidden_rows(pieces, wg, wu, w_down, block_counts, block_rows, row_gates, per_expert):
    sources = len(pieces)
    total = sources * pieces[0].shape[0]
    depth, width = wg.shape
    return pl.pallas_call(
        functools.partial(hidden_kernel, sources, per_expert),
        out_shape=(
            pltpu.VMEM((total, width), jnp.bfloat16),
            pltpu.VMEM((total, 128), jnp.float32),
            pltpu.VMEM(w_down.shape, w_down.dtype),
        ),
        in_specs=[VMEM] * sources + [VMEM, VMEM, HBM, SMEM, VMEM, VMEM],
        out_specs=(VMEM, VMEM, VMEM),
        scratch_shapes=[
            pltpu.VMEM((total, depth), jnp.float32),
            pltpu.VMEM((total, depth), jnp.bfloat16),
            pltpu.SemaphoreType.DMA((CHUNKS,)),
        ],
        compiler_params=pltpu.CompilerParams(vmem_limit_bytes=2 * MIB),
        cost_estimate=pl.CostEstimate(
            flops=4 * total * depth * width, bytes_accessed=2 * w_down.size, transcendentals=total * width
        ),
    )(*pieces, in_vmem(wg), in_vmem(wu), in_hbm(w_down), block_counts, block_rows, row_gates)


def in_hbm(x):
    return pltpu.with_memory_space_constraint(x, pltpu.HBM)


def in_vmem(x):
    return pltpu.with_memory_space_constraint(x, pltpu.VMEM)


def down_kernel(other, h_ref, g_ref, wd_ref, out_ref):
    half = wd_ref.shape[1] // 2
    side = lax.axis_index("hid")
    base = (1 - side if other else side) * half
    for n in range(half // TILE):
        cols = pl.ds(pl.multiple_of(base + n * TILE, TILE), TILE)
        part = jnp.dot(h_ref[...], wd_ref[:, cols], preferred_element_type=jnp.float32)
        out_ref[:, pl.ds(n * TILE, TILE)] = (part * g_ref[:, :1]).astype(out_ref.dtype)


def down_half(hidden, g, wd, other, dtype):
    rows, depth = hidden.shape
    half = wd.shape[1] // 2
    return pl.pallas_call(
        functools.partial(down_kernel, other),
        out_shape=jax.ShapeDtypeStruct((rows, half), dtype),
        in_specs=[VMEM, VMEM, VMEM],
        out_specs=VMEM,
        compiler_params=pltpu.CompilerParams(vmem_limit_bytes=2 * MIB),
        cost_estimate=pl.CostEstimate(flops=2 * rows * depth * half, bytes_accessed=0, transcendentals=0),
    )(in_vmem(hidden), in_vmem(g), in_vmem(wd))


def merge_kernel(keep_ref, got_ref, own_ref, *out_refs):
    both = keep_ref[...] + got_ref[...].astype(jnp.float32)
    count = own_ref.shape[0]
    own_ref[...] = both[:count]
    for k, out_ref in enumerate(out_refs):
        out_ref[...] = both[(k + 1) * count : (k + 2) * count].astype(out_ref.dtype)


def merge(keep, got, sources):
    rows, width = keep.shape
    count = rows // sources
    return pl.pallas_call(
        merge_kernel,
        out_shape=(jax.ShapeDtypeStruct((count, width), jnp.float32),)
        + (jax.ShapeDtypeStruct((count, width), jnp.bfloat16),) * (sources - 1),
        in_specs=[VMEM, VMEM],
        out_specs=(VMEM,) * sources,
        compiler_params=pltpu.CompilerParams(vmem_limit_bytes=2 * MIB),
    )(keep, got)


def sum_kernel(own_ref, *refs):
    total = own_ref[...]
    for ref in refs[:-1]:
        total = total + ref[...].astype(jnp.float32)
    refs[-1][...] = total.astype(jnp.bfloat16)


def final_sum(own, got):
    return pl.pallas_call(
        sum_kernel,
        out_shape=jax.ShapeDtypeStruct(own.shape, jnp.bfloat16),
        in_specs=[VMEM] * (1 + len(got)),
        out_specs=VMEM,
        compiler_params=pltpu.CompilerParams(vmem_limit_bytes=2 * MIB),
    )(own, *got)


def shifted(x, k, sources):
    return lax.ppermute(x, "exp", [(i, (i + k) % sources) for i in range(sources)])


def local(tokens, w_gate, w_up, w_down, block_counts, block_rows, row_gates):
    sources = lax.axis_size("exp")
    per_expert = sources // block_rows.shape[0]
    pieces = [tokens] + [shifted(tokens, k, sources) for k in range(1, sources)]
    wg, wu = fetch(w_gate, w_up)
    hidden, g, wd = hidden_rows(pieces, wg, wu, w_down, block_counts, block_rows, row_gates, per_expert)
    send = down_half(hidden, g, wd, True, jnp.bfloat16)
    keep = down_half(hidden, g, wd, False, jnp.float32)
    got = lax.ppermute(send, "hid", [(0, 1), (1, 0)])
    own, *outgoing = merge(keep, got, sources)
    returned = [shifted(piece, -(k + 1), sources) for k, piece in enumerate(outgoing)]
    return final_sum(own, returned)


def expert_block(segment, w_gate, w_up, w_down):
    gate_act = jnp.dot(segment, w_gate, preferred_element_type=jnp.float32)
    up_act = jnp.dot(segment, w_up, preferred_element_type=jnp.float32)
    hidden = (jax.nn.silu(gate_act) * up_act).astype(jnp.bfloat16)
    return jnp.dot(hidden, w_down, preferred_element_type=jnp.float32).astype(jnp.bfloat16)


def local_wide(tokens, w_gate, w_up, w_down, block_counts, block_rows, row_gates):
    sources = lax.axis_size("exp")
    own_index = lax.axis_index("exp")
    token_count = tokens.shape[0]
    model_width = tokens.shape[1]
    experts = block_rows.shape[0]
    slot_count = block_rows.shape[1]
    per_expert = sources // experts
    my_expert = own_index // per_expert
    position = jnp.arange(slot_count, dtype=jnp.int32)
    is_live = (position[None, :] < block_counts[:, None] * BLOCK) & (block_rows >= 0)
    source = jnp.where(is_live, block_rows // token_count, sources)
    matches = (source[:, :, None] == jnp.arange(sources, dtype=jnp.int32)[None, None, :]).astype(
        jnp.int32
    )
    order_rank = jnp.sum(jnp.cumsum(matches, axis=1) * matches, axis=2) - 1
    is_mine = is_live & (source == own_index)
    slot_target = jnp.where(
        is_mine, jnp.arange(experts, dtype=jnp.int32)[:, None] * CAP + order_rank, experts * CAP
    )
    local_values = jnp.where(is_mine, block_rows - own_index * token_count, token_count)
    local_row = (
        jnp.full((experts * CAP + 1,), token_count, jnp.int32)
        .at[slot_target.ravel()]
        .set(local_values.ravel())[: experts * CAP]
    )
    gate_mine = (
        jnp.zeros((experts * CAP + 1,), jnp.float32)
        .at[slot_target.ravel()]
        .set(jnp.where(is_mine, row_gates, 0.0).ravel())[: experts * CAP]
    )
    live_mine = lax.dynamic_index_in_dim(is_live, my_expert, 0, keepdims=False)
    rows_mine = lax.dynamic_index_in_dim(block_rows, my_expert, 0, keepdims=False)
    source_mine = lax.dynamic_index_in_dim(source, my_expert, 0, keepdims=False)
    rank_mine = lax.dynamic_index_in_dim(order_rank, my_expert, 0, keepdims=False)
    back_index = jnp.where(live_mine, source_mine * CAP + rank_mine, sources * CAP)
    blank_row = jnp.zeros((1, model_width), jnp.bfloat16)
    everyone = lax.all_gather(tokens, "exp", axis=0, tiled=True)
    row_pool = jnp.concatenate([everyone, blank_row], axis=0)
    routed = row_pool[jnp.where(live_mine, rows_mine, sources * token_count)]
    partial_rows = expert_block(routed, w_gate, w_up, w_down)
    outbound = (
        jnp.zeros((sources * CAP + 1, model_width), jnp.bfloat16).at[back_index].set(partial_rows)
    )
    outbound = outbound[: sources * CAP].reshape(sources, CAP, model_width)
    returned = lax.all_to_all(outbound, "exp", split_axis=0, concat_axis=0, tiled=True)
    summed = jnp.sum(
        returned.reshape(experts, per_expert, CAP, model_width), axis=1, dtype=jnp.float32
    )
    weighted = (summed * gate_mine.reshape(experts, CAP, 1)).reshape(experts * CAP, model_width)
    selector = (local_row[:, None] == jnp.arange(token_count, dtype=jnp.int32)[None, :]).astype(
        jnp.float32
    )
    gathered_sum = jnp.einsum("st,sd->td", selector, weighted, precision=lax.Precision.HIGHEST)
    share = lax.psum_scatter(gathered_sum, "hid", scatter_dimension=1, tiled=True)
    return share.astype(jnp.bfloat16)


def solution(mesh):
    return jax.shard_map(
        local if mesh.shape["exp"] <= 16 else local_wide,
        mesh=mesh,
        in_specs=(
            P(("grp", "exp"), None),
            P(None, ("exp", "hid")),
            P(None, ("exp", "hid")),
            P(("exp", "hid"), None),
            P("grp"),
            P("grp", None),
            P("grp", None),
        ),
        out_specs=P(("grp", "exp"), "hid"),
        check_vma=False,
    )
```

```python
import functools

import jax
import jax.numpy as jnp
from jax import lax
from jax.experimental import pallas as pl
from jax.experimental.pallas import tpu as pltpu
from jax.sharding import PartitionSpec as P

BLOCK = 128
CAP = 3
TILE = 512
MIB = 1 << 20
AHEAD = 20_000_000_000
VMEM = pl.BlockSpec(memory_space=pltpu.VMEM)
SMEM = pl.BlockSpec(memory_space=pltpu.SMEM)


def token_gates(own, sources, per_expert, token_count, counts_ref, rows_ref, gates_ref):
    experts, slots = rows_ref.shape
    expert = own // per_expert
    mine = lax.broadcasted_iota(jnp.int32, (experts, slots), 0) == expert
    rows = jnp.sum(jnp.where(mine, rows_ref[...], 0), axis=0, keepdims=True)
    gates = jnp.sum(jnp.where(mine, gates_ref[...], 0.0), axis=0, keepdims=True)
    position = lax.broadcasted_iota(jnp.int32, (1, slots), 1)
    live = (position < counts_ref[expert] * BLOCK) & (rows >= 0)
    rows = jnp.where(live, rows, -1)
    total = sources * token_count
    line = lax.broadcasted_iota(jnp.int32, (total, slots), 0)
    start = lax.rem(own - line // token_count + sources, sources) * token_count
    token = start + lax.rem(line, token_count)
    return jnp.sum(jnp.where(rows == token, gates, 0.0), axis=1, keepdims=True)


def route_kernel(sources, per_expert, tokens_ref, counts_ref, rows_ref, gates_ref, tokens_out, g_out):
    tokens_out[...] = tokens_ref[...]
    g = token_gates(
        lax.axis_index("exp"), sources, per_expert, tokens_ref.shape[0], counts_ref, rows_ref, gates_ref
    )
    g_out[...] = jnp.broadcast_to(g, g_out.shape)


def route(tokens, block_counts, block_rows, row_gates, sources, per_expert):
    return pl.pallas_call(
        functools.partial(route_kernel, sources, per_expert),
        out_shape=(
            jax.ShapeDtypeStruct(tokens.shape, tokens.dtype),
            jax.ShapeDtypeStruct((sources * tokens.shape[0], 128), jnp.float32),
        ),
        in_specs=[VMEM, SMEM, VMEM, VMEM],
        out_specs=(VMEM, VMEM),
        compiler_params=pltpu.CompilerParams(vmem_limit_bytes=2 * MIB),
        cost_estimate=pl.CostEstimate(flops=AHEAD, bytes_accessed=0, transcendentals=0),
    )(tokens, block_counts, block_rows, row_gates)


def hidden_kernel(sources, *refs):
    pieces = refs[:sources]
    wg_ref, wu_ref, h_out, wide, x_ref = refs[sources:]
    token_count = pieces[0].shape[0]
    for k, piece in enumerate(pieces):
        wide[pl.ds(k * token_count, token_count), :] = piece[...].astype(jnp.float32)
    x_ref[...] = wide[...].astype(jnp.bfloat16)

    @pl.loop(0, wg_ref.shape[1] // TILE)
    def _(n):
        cols = pl.ds(pl.multiple_of(n * TILE, TILE), TILE)
        gate = jnp.dot(x_ref[...], wg_ref[:, cols], preferred_element_type=jnp.float32)
        up = jnp.dot(x_ref[...], wu_ref[:, cols], preferred_element_type=jnp.float32)
        h_out[:, cols] = (gate / (1.0 + jnp.exp(-gate)) * up).astype(jnp.bfloat16)


def hidden_rows(pieces, wg, wu):
    sources = len(pieces)
    total = sources * pieces[0].shape[0]
    depth, width = wg.shape
    return pl.pallas_call(
        functools.partial(hidden_kernel, sources),
        out_shape=jax.ShapeDtypeStruct((total, width), jnp.bfloat16),
        in_specs=[VMEM] * (sources + 2),
        out_specs=VMEM,
        scratch_shapes=[
            pltpu.VMEM((total, depth), jnp.float32),
            pltpu.VMEM((total, depth), jnp.bfloat16),
        ],
        compiler_params=pltpu.CompilerParams(vmem_limit_bytes=2 * MIB),
        cost_estimate=pl.CostEstimate(
            flops=4 * total * depth * width, bytes_accessed=0, transcendentals=total * width
        ),
    )(*pieces, in_vmem(wg), in_vmem(wu))


def in_vmem(x):
    return pltpu.with_memory_space_constraint(x, pltpu.VMEM)


def down_kernel(other, h_ref, g_ref, wd_ref, out_ref):
    half = wd_ref.shape[1] // 2
    side = lax.axis_index("hid")
    base = (1 - side if other else side) * half
    for n in range(half // TILE):
        cols = pl.ds(pl.multiple_of(base + n * TILE, TILE), TILE)
        part = jnp.dot(h_ref[...], wd_ref[:, cols], preferred_element_type=jnp.float32)
        out_ref[:, pl.ds(n * TILE, TILE)] = (part * g_ref[:, :1]).astype(out_ref.dtype)


def down_half(hidden, g, wd, other, dtype):
    rows, depth = hidden.shape
    half = wd.shape[1] // 2
    return pl.pallas_call(
        functools.partial(down_kernel, other),
        out_shape=jax.ShapeDtypeStruct((rows, half), dtype),
        in_specs=[VMEM, VMEM, VMEM],
        out_specs=VMEM,
        compiler_params=pltpu.CompilerParams(vmem_limit_bytes=2 * MIB),
        cost_estimate=pl.CostEstimate(flops=2 * rows * depth * half, bytes_accessed=0, transcendentals=0),
    )(hidden, g, in_vmem(wd))


def merge_kernel(keep_ref, got_ref, own_ref, *out_refs):
    both = keep_ref[...] + got_ref[...].astype(jnp.float32)
    count = own_ref.shape[0]
    own_ref[...] = both[:count]
    for k, out_ref in enumerate(out_refs):
        out_ref[...] = both[(k + 1) * count : (k + 2) * count].astype(out_ref.dtype)


def merge(keep, got, sources):
    rows, width = keep.shape
    count = rows // sources
    return pl.pallas_call(
        merge_kernel,
        out_shape=(jax.ShapeDtypeStruct((count, width), jnp.float32),)
        + (jax.ShapeDtypeStruct((count, width), jnp.bfloat16),) * (sources - 1),
        in_specs=[VMEM, VMEM],
        out_specs=(VMEM,) * sources,
        compiler_params=pltpu.CompilerParams(vmem_limit_bytes=2 * MIB),
    )(keep, got)


def sum_kernel(own_ref, *refs):
    total = own_ref[...]
    for ref in refs[:-1]:
        total = total + ref[...].astype(jnp.float32)
    refs[-1][...] = total.astype(jnp.bfloat16)


def final_sum(own, got):
    return pl.pallas_call(
        sum_kernel,
        out_shape=jax.ShapeDtypeStruct(own.shape, jnp.bfloat16),
        in_specs=[VMEM] * (1 + len(got)),
        out_specs=VMEM,
        compiler_params=pltpu.CompilerParams(vmem_limit_bytes=2 * MIB),
    )(own, *got)


def shifted(x, k, sources):
    return lax.ppermute(x, "exp", [(i, (i + k) % sources) for i in range(sources)])


def local(tokens, w_gate, w_up, w_down, block_counts, block_rows, row_gates):
    sources = lax.axis_size("exp")
    per_expert = sources // block_rows.shape[0]
    tokens, g = route(tokens, block_counts, block_rows, row_gates, sources, per_expert)
    pieces = [tokens] + [shifted(tokens, k, sources) for k in range(1, sources)]
    hidden = hidden_rows(pieces, w_gate, w_up)
    send = down_half(hidden, g, w_down, True, jnp.bfloat16)
    keep = down_half(hidden, g, w_down, False, jnp.float32)
    got = lax.ppermute(send, "hid", [(0, 1), (1, 0)])
    own, *outgoing = merge(keep, got, sources)
    returned = [shifted(piece, -(k + 1), sources) for k, piece in enumerate(outgoing)]
    return final_sum(own, returned)


def expert_block(segment, w_gate, w_up, w_down):
    gate_act = jnp.dot(segment, w_gate, preferred_element_type=jnp.float32)
    up_act = jnp.dot(segment, w_up, preferred_element_type=jnp.float32)
    hidden = (jax.nn.silu(gate_act) * up_act).astype(jnp.bfloat16)
    return jnp.dot(hidden, w_down, preferred_element_type=jnp.float32).astype(jnp.bfloat16)


def local_wide(tokens, w_gate, w_up, w_down, block_counts, block_rows, row_gates):
    sources = lax.axis_size("exp")
    own_index = lax.axis_index("exp")
    token_count = tokens.shape[0]
    model_width = tokens.shape[1]
    experts = block_rows.shape[0]
    slot_count = block_rows.shape[1]
    per_expert = sources // experts
    my_expert = own_index // per_expert
    position = jnp.arange(slot_count, dtype=jnp.int32)
    is_live = (position[None, :] < block_counts[:, None] * BLOCK) & (block_rows >= 0)
    source = jnp.where(is_live, block_rows // token_count, sources)
    matches = (source[:, :, None] == jnp.arange(sources, dtype=jnp.int32)[None, None, :]).astype(
        jnp.int32
    )
    order_rank = jnp.sum(jnp.cumsum(matches, axis=1) * matches, axis=2) - 1
    is_mine = is_live & (source == own_index)
    slot_target = jnp.where(
        is_mine, jnp.arange(experts, dtype=jnp.int32)[:, None] * CAP + order_rank, experts * CAP
    )
    local_values = jnp.where(is_mine, block_rows - own_index * token_count, token_count)
    local_row = (
        jnp.full((experts * CAP + 1,), token_count, jnp.int32)
        .at[slot_target.ravel()]
        .set(local_values.ravel())[: experts * CAP]
    )
    gate_mine = (
        jnp.zeros((experts * CAP + 1,), jnp.float32)
        .at[slot_target.ravel()]
        .set(jnp.where(is_mine, row_gates, 0.0).ravel())[: experts * CAP]
    )
    live_mine = lax.dynamic_index_in_dim(is_live, my_expert, 0, keepdims=False)
    rows_mine = lax.dynamic_index_in_dim(block_rows, my_expert, 0, keepdims=False)
    source_mine = lax.dynamic_index_in_dim(source, my_expert, 0, keepdims=False)
    rank_mine = lax.dynamic_index_in_dim(order_rank, my_expert, 0, keepdims=False)
    back_index = jnp.where(live_mine, source_mine * CAP + rank_mine, sources * CAP)
    blank_row = jnp.zeros((1, model_width), jnp.bfloat16)
    everyone = lax.all_gather(tokens, "exp", axis=0, tiled=True)
    row_pool = jnp.concatenate([everyone, blank_row], axis=0)
    routed = row_pool[jnp.where(live_mine, rows_mine, sources * token_count)]
    partial_rows = expert_block(routed, w_gate, w_up, w_down)
    outbound = (
        jnp.zeros((sources * CAP + 1, model_width), jnp.bfloat16).at[back_index].set(partial_rows)
    )
    outbound = outbound[: sources * CAP].reshape(sources, CAP, model_width)
    returned = lax.all_to_all(outbound, "exp", split_axis=0, concat_axis=0, tiled=True)
    summed = jnp.sum(
        returned.reshape(experts, per_expert, CAP, model_width), axis=1, dtype=jnp.float32
    )
    weighted = (summed * gate_mine.reshape(experts, CAP, 1)).reshape(experts * CAP, model_width)
    selector = (local_row[:, None] == jnp.arange(token_count, dtype=jnp.int32)[None, :]).astype(
        jnp.float32
    )
    gathered_sum = jnp.einsum("st,sd->td", selector, weighted, precision=lax.Precision.HIGHEST)
    share = lax.psum_scatter(gathered_sum, "hid", scatter_dimension=1, tiled=True)
    return share.astype(jnp.bfloat16)


def solution(mesh):
    return jax.shard_map(
        local if mesh.shape["exp"] <= 16 else local_wide,
        mesh=mesh,
        in_specs=(
            P(("grp", "exp"), None),
            P(None, ("exp", "hid")),
            P(None, ("exp", "hid")),
            P(("exp", "hid"), None),
            P("grp"),
            P("grp", None),
            P("grp", None),
        ),
        out_specs=P(("grp", "exp"), "hid"),
        check_vma=False,
    )
```

```python
import functools

import jax
import jax.numpy as jnp
from jax import lax
from jax.experimental import pallas as pl
from jax.experimental.pallas import tpu as pltpu
from jax.sharding import PartitionSpec as P

BLOCK = 128
CAP = 3
TILE = 512
MIB = 1 << 20
AHEAD = 20_000_000_000
HBM = pl.BlockSpec(memory_space=pltpu.HBM)
VMEM = pl.BlockSpec(memory_space=pltpu.VMEM)
SMEM = pl.BlockSpec(memory_space=pltpu.SMEM)


def pass_kernel(tokens_ref, out_ref, sem):
    copy = pltpu.make_async_copy(tokens_ref, out_ref, sem)
    copy.start()
    copy.wait()


def pass_on(tokens):
    return pl.pallas_call(
        pass_kernel,
        out_shape=jax.ShapeDtypeStruct(tokens.shape, tokens.dtype),
        in_specs=[HBM],
        out_specs=VMEM,
        scratch_shapes=[pltpu.SemaphoreType.DMA],
        compiler_params=pltpu.CompilerParams(vmem_limit_bytes=2 * MIB),
        cost_estimate=pl.CostEstimate(flops=AHEAD, bytes_accessed=0, transcendentals=0),
    )(pltpu.with_memory_space_constraint(tokens, pltpu.HBM))


def route_kernel(count, per_expert, counts_ref, rows_ref, gates_ref, out_ref):
    experts, slots = rows_ref.shape
    total = out_ref.shape[0]
    line = lax.broadcasted_iota(jnp.int32, (total, slots), 0)
    position = lax.broadcasted_iota(jnp.int32, (total, slots), 1)
    token = lax.axis_index("exp") * count + lax.rem(line, count)
    expert = line // (count * per_expert)
    found = jnp.zeros((total, slots), jnp.float32)
    for e in range(experts):
        rows = rows_ref[pl.ds(e, 1), :]
        here = (expert == e) & (rows == token) & (position < counts_ref[e] * BLOCK)
        found = jnp.where(here, gates_ref[pl.ds(e, 1), :], found)
    out_ref[...] = jnp.broadcast_to(jnp.sum(found, axis=1, keepdims=True), out_ref.shape)


def route(block_counts, block_rows, row_gates, sources, count):
    return pl.pallas_call(
        functools.partial(route_kernel, count, sources // block_rows.shape[0]),
        out_shape=jax.ShapeDtypeStruct((sources * count, 128), jnp.float32),
        in_specs=[SMEM, VMEM, VMEM],
        out_specs=VMEM,
        compiler_params=pltpu.CompilerParams(vmem_limit_bytes=2 * MIB),
    )(block_counts, block_rows, row_gates)


def hidden_kernel(sources, *refs):
    pieces = refs[:sources]
    wg_ref, wu_ref, h_out, wide, x_ref = refs[sources:]
    token_count = pieces[0].shape[0]
    for k, piece in enumerate(pieces):
        wide[pl.ds(k * token_count, token_count), :] = piece[...].astype(jnp.float32)
    x_ref[...] = wide[...].astype(jnp.bfloat16)

    @pl.loop(0, wg_ref.shape[1] // TILE)
    def _(n):
        cols = pl.ds(pl.multiple_of(n * TILE, TILE), TILE)
        gate = jnp.dot(x_ref[...], wg_ref[:, cols], preferred_element_type=jnp.float32)
        up = jnp.dot(x_ref[...], wu_ref[:, cols], preferred_element_type=jnp.float32)
        h_out[:, cols] = (gate / (1.0 + jnp.exp(-gate)) * up).astype(jnp.bfloat16)


def hidden_rows(pieces, wg, wu):
    sources = len(pieces)
    total = sources * pieces[0].shape[0]
    depth, width = wg.shape
    return pl.pallas_call(
        functools.partial(hidden_kernel, sources),
        out_shape=jax.ShapeDtypeStruct((total, width), jnp.bfloat16),
        in_specs=[VMEM] * (sources + 2),
        out_specs=VMEM,
        scratch_shapes=[
            pltpu.VMEM((total, depth), jnp.float32),
            pltpu.VMEM((total, depth), jnp.bfloat16),
        ],
        compiler_params=pltpu.CompilerParams(vmem_limit_bytes=2 * MIB),
        cost_estimate=pl.CostEstimate(
            flops=4 * total * depth * width, bytes_accessed=0, transcendentals=total * width
        ),
    )(*pieces, in_vmem(wg), in_vmem(wu))


def in_vmem(x):
    return pltpu.with_memory_space_constraint(x, pltpu.VMEM)


def down_kernel(other, h_ref, wd_ref, out_ref):
    half = wd_ref.shape[1] // 2
    side = lax.axis_index("hid")
    base = (1 - side if other else side) * half
    for n in range(half // TILE):
        cols = pl.ds(pl.multiple_of(base + n * TILE, TILE), TILE)
        part = jnp.dot(h_ref[...], wd_ref[:, cols], preferred_element_type=jnp.float32)
        out_ref[:, pl.ds(n * TILE, TILE)] = part.astype(out_ref.dtype)


def down_half(hidden, wd, other, dtype):
    rows, depth = hidden.shape
    half = wd.shape[1] // 2
    return pl.pallas_call(
        functools.partial(down_kernel, other),
        out_shape=jax.ShapeDtypeStruct((rows, half), dtype),
        in_specs=[VMEM, VMEM],
        out_specs=VMEM,
        compiler_params=pltpu.CompilerParams(vmem_limit_bytes=2 * MIB),
        cost_estimate=pl.CostEstimate(flops=2 * rows * depth * half, bytes_accessed=0, transcendentals=0),
    )(hidden, in_vmem(wd))


def merge_kernel(keep_ref, got_ref, out_ref):
    sources, count, _ = out_ref.shape
    own = lax.axis_index("exp")
    both = (keep_ref[...] + got_ref[...].astype(jnp.float32)).astype(out_ref.dtype)
    for k in range(sources):
        out_ref[lax.rem(own - k + sources, sources)] = both[k * count : (k + 1) * count]


def merge(keep, got, sources):
    rows, width = keep.shape
    return pl.pallas_call(
        merge_kernel,
        out_shape=jax.ShapeDtypeStruct((sources, rows // sources, width), jnp.bfloat16),
        in_specs=[VMEM, VMEM],
        out_specs=VMEM,
        compiler_params=pltpu.CompilerParams(vmem_limit_bytes=2 * MIB),
    )(keep, got)


def sum_kernel(got_ref, gates_ref, out_ref):
    sources, count, _ = got_ref.shape
    total = jnp.zeros(out_ref.shape, jnp.float32)
    for s in range(sources):
        total = total + got_ref[s].astype(jnp.float32) * gates_ref[pl.ds(s * count, count), :1]
    out_ref[...] = total.astype(out_ref.dtype)


def weighted_sum(got, gates):
    return pl.pallas_call(
        sum_kernel,
        out_shape=jax.ShapeDtypeStruct(got.shape[1:], jnp.bfloat16),
        in_specs=[VMEM, VMEM],
        out_specs=VMEM,
        compiler_params=pltpu.CompilerParams(vmem_limit_bytes=2 * MIB),
    )(got, gates)


def shifted(x, k, sources):
    return lax.ppermute(x, "exp", [(i, (i + k) % sources) for i in range(sources)])


def local(tokens, w_gate, w_up, w_down, block_counts, block_rows, row_gates):
    sources = lax.axis_size("exp")
    tokens = pass_on(tokens)
    pieces = [tokens] + [shifted(tokens, k, sources) for k in range(1, sources)]
    hidden = hidden_rows(pieces, w_gate, w_up)
    send = down_half(hidden, w_down, True, jnp.bfloat16)
    keep = down_half(hidden, w_down, False, jnp.float32)
    got = lax.ppermute(send, "hid", [(0, 1), (1, 0)])
    outgoing = merge(keep, got, sources)
    returned = lax.all_to_all(outgoing, "exp", split_axis=0, concat_axis=0, tiled=True)
    gates = route(block_counts, block_rows, row_gates, sources, tokens.shape[0])
    return weighted_sum(returned, gates)


def expert_block(segment, w_gate, w_up, w_down):
    gate_act = jnp.dot(segment, w_gate, preferred_element_type=jnp.float32)
    up_act = jnp.dot(segment, w_up, preferred_element_type=jnp.float32)
    hidden = (jax.nn.silu(gate_act) * up_act).astype(jnp.bfloat16)
    return jnp.dot(hidden, w_down, preferred_element_type=jnp.float32).astype(jnp.bfloat16)


def local_wide(tokens, w_gate, w_up, w_down, block_counts, block_rows, row_gates):
    sources = lax.axis_size("exp")
    own_index = lax.axis_index("exp")
    token_count = tokens.shape[0]
    model_width = tokens.shape[1]
    experts = block_rows.shape[0]
    slot_count = block_rows.shape[1]
    per_expert = sources // experts
    my_expert = own_index // per_expert
    position = jnp.arange(slot_count, dtype=jnp.int32)
    is_live = (position[None, :] < block_counts[:, None] * BLOCK) & (block_rows >= 0)
    source = jnp.where(is_live, block_rows // token_count, sources)
    matches = (source[:, :, None] == jnp.arange(sources, dtype=jnp.int32)[None, None, :]).astype(
        jnp.int32
    )
    order_rank = jnp.sum(jnp.cumsum(matches, axis=1) * matches, axis=2) - 1
    is_mine = is_live & (source == own_index)
    slot_target = jnp.where(
        is_mine, jnp.arange(experts, dtype=jnp.int32)[:, None] * CAP + order_rank, experts * CAP
    )
    local_values = jnp.where(is_mine, block_rows - own_index * token_count, token_count)
    local_row = (
        jnp.full((experts * CAP + 1,), token_count, jnp.int32)
        .at[slot_target.ravel()]
        .set(local_values.ravel())[: experts * CAP]
    )
    gate_mine = (
        jnp.zeros((experts * CAP + 1,), jnp.float32)
        .at[slot_target.ravel()]
        .set(jnp.where(is_mine, row_gates, 0.0).ravel())[: experts * CAP]
    )
    live_mine = lax.dynamic_index_in_dim(is_live, my_expert, 0, keepdims=False)
    rows_mine = lax.dynamic_index_in_dim(block_rows, my_expert, 0, keepdims=False)
    source_mine = lax.dynamic_index_in_dim(source, my_expert, 0, keepdims=False)
    rank_mine = lax.dynamic_index_in_dim(order_rank, my_expert, 0, keepdims=False)
    back_index = jnp.where(live_mine, source_mine * CAP + rank_mine, sources * CAP)
    blank_row = jnp.zeros((1, model_width), jnp.bfloat16)
    everyone = lax.all_gather(tokens, "exp", axis=0, tiled=True)
    row_pool = jnp.concatenate([everyone, blank_row], axis=0)
    routed = row_pool[jnp.where(live_mine, rows_mine, sources * token_count)]
    partial_rows = expert_block(routed, w_gate, w_up, w_down)
    outbound = (
        jnp.zeros((sources * CAP + 1, model_width), jnp.bfloat16).at[back_index].set(partial_rows)
    )
    outbound = outbound[: sources * CAP].reshape(sources, CAP, model_width)
    returned = lax.all_to_all(outbound, "exp", split_axis=0, concat_axis=0, tiled=True)
    summed = jnp.sum(
        returned.reshape(experts, per_expert, CAP, model_width), axis=1, dtype=jnp.float32
    )
    weighted = (summed * gate_mine.reshape(experts, CAP, 1)).reshape(experts * CAP, model_width)
    selector = (local_row[:, None] == jnp.arange(token_count, dtype=jnp.int32)[None, :]).astype(
        jnp.float32
    )
    gathered_sum = jnp.einsum("st,sd->td", selector, weighted, precision=lax.Precision.HIGHEST)
    share = lax.psum_scatter(gathered_sum, "hid", scatter_dimension=1, tiled=True)
    return share.astype(jnp.bfloat16)


def solution(mesh):
    return jax.shard_map(
        local if mesh.shape["exp"] <= 16 else local_wide,
        mesh=mesh,
        in_specs=(
            P(("grp", "exp"), None),
            P(None, ("exp", "hid")),
            P(None, ("exp", "hid")),
            P(("exp", "hid"), None),
            P("grp"),
            P("grp", None),
            P("grp", None),
        ),
        out_specs=P(("grp", "exp"), "hid"),
        check_vma=False,
    )
```

```python
import functools

import jax
import jax.numpy as jnp
from jax import lax
from jax.experimental import pallas as pl
from jax.experimental.pallas import tpu as pltpu
from jax.sharding import PartitionSpec as P

BLOCK = 128
CAP = 3
TILE = 512
MIB = 1 << 20
AHEAD = 20_000_000_000
HBM = pl.BlockSpec(memory_space=pltpu.HBM)
VMEM = pl.BlockSpec(memory_space=pltpu.VMEM)
SMEM = pl.BlockSpec(memory_space=pltpu.SMEM)


def pass_kernel(tokens_ref, out_ref, side_ref, sem):
    copy = pltpu.make_async_copy(tokens_ref, out_ref, sem)
    copy.start()
    side_ref[0] = lax.axis_index("hid")
    copy.wait()


def pass_on(tokens):
    return pl.pallas_call(
        pass_kernel,
        out_shape=(jax.ShapeDtypeStruct(tokens.shape, tokens.dtype), pltpu.SMEM((1,), jnp.int32)),
        in_specs=[HBM],
        out_specs=(VMEM, SMEM),
        scratch_shapes=[pltpu.SemaphoreType.DMA],
        compiler_params=pltpu.CompilerParams(vmem_limit_bytes=2 * MIB),
        cost_estimate=pl.CostEstimate(flops=AHEAD, bytes_accessed=0, transcendentals=0),
    )(pltpu.with_memory_space_constraint(tokens, pltpu.HBM))


def route_kernel(count, per_expert, counts_ref, rows_ref, gates_ref, out_ref):
    experts, slots = rows_ref.shape
    total = out_ref.shape[0]
    line = lax.broadcasted_iota(jnp.int32, (total, slots), 0)
    position = lax.broadcasted_iota(jnp.int32, (total, slots), 1)
    own = lax.axis_index("exp")
    token = own * count + lax.rem(line, count)
    expert = (own ^ (line // count)) // per_expert
    found = jnp.zeros((total, slots), jnp.float32)
    for e in range(experts):
        rows = rows_ref[pl.ds(e, 1), :]
        here = (expert == e) & (rows == token) & (position < counts_ref[e] * BLOCK)
        found = jnp.where(here, gates_ref[pl.ds(e, 1), :], found)
    out_ref[...] = jnp.broadcast_to(jnp.sum(found, axis=1, keepdims=True), out_ref.shape)


def route(block_counts, block_rows, row_gates, sources, count):
    return pl.pallas_call(
        functools.partial(route_kernel, count, sources // block_rows.shape[0]),
        out_shape=jax.ShapeDtypeStruct((sources * count, 128), jnp.float32),
        in_specs=[SMEM, VMEM, VMEM],
        out_specs=VMEM,
        compiler_params=pltpu.CompilerParams(vmem_limit_bytes=2 * MIB),
    )(block_counts, block_rows, row_gates)


def hidden_kernel(sources, *refs):
    pieces = refs[:sources]
    wg_ref, wu_ref, h_out, wide, x_ref = refs[sources:]
    token_count = pieces[0].shape[0]
    for k, piece in enumerate(pieces):
        wide[pl.ds(k * token_count, token_count), :] = piece[...].astype(jnp.float32)
    x_ref[...] = wide[...].astype(jnp.bfloat16)

    @pl.loop(0, wg_ref.shape[1] // TILE)
    def _(n):
        cols = pl.ds(pl.multiple_of(n * TILE, TILE), TILE)
        gate = jnp.dot(x_ref[...], wg_ref[:, cols], preferred_element_type=jnp.float32)
        up = jnp.dot(x_ref[...], wu_ref[:, cols], preferred_element_type=jnp.float32)
        h_out[:, cols] = (gate / (1.0 + jnp.exp(-gate)) * up).astype(jnp.bfloat16)


def hidden_rows(pieces, wg, wu):
    sources = len(pieces)
    total = sources * pieces[0].shape[0]
    depth, width = wg.shape
    return pl.pallas_call(
        functools.partial(hidden_kernel, sources),
        out_shape=jax.ShapeDtypeStruct((total, width), jnp.bfloat16),
        in_specs=[VMEM] * (sources + 2),
        out_specs=VMEM,
        scratch_shapes=[
            pltpu.VMEM((total, depth), jnp.float32),
            pltpu.VMEM((total, depth), jnp.bfloat16),
        ],
        compiler_params=pltpu.CompilerParams(vmem_limit_bytes=2 * MIB),
        cost_estimate=pl.CostEstimate(
            flops=4 * total * depth * width, bytes_accessed=0, transcendentals=total * width
        ),
    )(*pieces, in_vmem(wg), in_vmem(wu))


def in_vmem(x):
    return pltpu.with_memory_space_constraint(x, pltpu.VMEM)


def down_kernel(other, side_ref, h_ref, wd_ref, out_ref):
    half = wd_ref.shape[1] // 2
    side = side_ref[0]
    base = (1 - side if other else side) * half
    for n in range(half // TILE):
        cols = pl.ds(pl.multiple_of(base + n * TILE, TILE), TILE)
        part = jnp.dot(h_ref[...], wd_ref[:, cols], preferred_element_type=jnp.float32)
        out_ref[:, pl.ds(n * TILE, TILE)] = part.astype(out_ref.dtype)


def down_half(side, hidden, wd, other, dtype):
    rows, depth = hidden.shape
    half = wd.shape[1] // 2
    return pl.pallas_call(
        functools.partial(down_kernel, other),
        out_shape=jax.ShapeDtypeStruct((rows, half), dtype),
        in_specs=[SMEM, VMEM, VMEM],
        out_specs=VMEM,
        compiler_params=pltpu.CompilerParams(vmem_limit_bytes=2 * MIB),
        cost_estimate=pl.CostEstimate(flops=2 * rows * depth * half, bytes_accessed=0, transcendentals=0),
    )(pltpu.with_memory_space_constraint(side, pltpu.SMEM), hidden, in_vmem(wd))


def merge_kernel(keep_ref, got_ref, own_ref, *out_refs):
    both = keep_ref[...] + got_ref[...].astype(jnp.float32)
    count = own_ref.shape[0]
    own_ref[...] = both[:count]
    for k, out_ref in enumerate(out_refs):
        out_ref[...] = both[(k + 1) * count : (k + 2) * count].astype(out_ref.dtype)


def merge(keep, got, sources):
    rows, width = keep.shape
    count = rows // sources
    return pl.pallas_call(
        merge_kernel,
        out_shape=(jax.ShapeDtypeStruct((count, width), jnp.float32),)
        + (jax.ShapeDtypeStruct((count, width), jnp.bfloat16),) * (sources - 1),
        in_specs=[VMEM, VMEM],
        out_specs=(VMEM,) * sources,
        compiler_params=pltpu.CompilerParams(vmem_limit_bytes=2 * MIB),
    )(keep, got)


def sum_kernel(gates_ref, *refs):
    total = jnp.zeros(refs[-1].shape, jnp.float32)
    count = total.shape[0]
    for k, ref in enumerate(refs[:-1]):
        total = total + ref[...].astype(jnp.float32) * gates_ref[pl.ds(k * count, count), :1]
    refs[-1][...] = total.astype(jnp.bfloat16)


def weighted_sum(gates, own, got):
    return pl.pallas_call(
        sum_kernel,
        out_shape=jax.ShapeDtypeStruct(own.shape, jnp.bfloat16),
        in_specs=[VMEM] * (2 + len(got)),
        out_specs=VMEM,
        compiler_params=pltpu.CompilerParams(vmem_limit_bytes=2 * MIB),
    )(gates, own, *got)


def swapped(x, k, sources):
    return lax.ppermute(x, "exp", [(i, i ^ k) for i in range(sources)])


def local(tokens, w_gate, w_up, w_down, block_counts, block_rows, row_gates):
    sources = lax.axis_size("exp")
    tokens, side = pass_on(tokens)
    pieces = [tokens] + [swapped(tokens, k, sources) for k in range(1, sources)]
    hidden = hidden_rows(pieces, w_gate, w_up)
    send = down_half(side, hidden, w_down, True, jnp.bfloat16)
    keep = down_half(side, hidden, w_down, False, jnp.float32)
    got = lax.ppermute(send, "hid", [(0, 1), (1, 0)])
    own, *outgoing = merge(keep, got, sources)
    returned = [swapped(piece, k + 1, sources) for k, piece in enumerate(outgoing)]
    gates = route(block_counts, block_rows, row_gates, sources, tokens.shape[0])
    return weighted_sum(gates, own, returned)


def expert_block(segment, w_gate, w_up, w_down):
    gate_act = jnp.dot(segment, w_gate, preferred_element_type=jnp.float32)
    up_act = jnp.dot(segment, w_up, preferred_element_type=jnp.float32)
    hidden = (jax.nn.silu(gate_act) * up_act).astype(jnp.bfloat16)
    return jnp.dot(hidden, w_down, preferred_element_type=jnp.float32).astype(jnp.bfloat16)


def local_wide(tokens, w_gate, w_up, w_down, block_counts, block_rows, row_gates):
    sources = lax.axis_size("exp")
    own_index = lax.axis_index("exp")
    token_count = tokens.shape[0]
    model_width = tokens.shape[1]
    experts = block_rows.shape[0]
    slot_count = block_rows.shape[1]
    per_expert = sources // experts
    my_expert = own_index // per_expert
    position = jnp.arange(slot_count, dtype=jnp.int32)
    is_live = (position[None, :] < block_counts[:, None] * BLOCK) & (block_rows >= 0)
    source = jnp.where(is_live, block_rows // token_count, sources)
    matches = (source[:, :, None] == jnp.arange(sources, dtype=jnp.int32)[None, None, :]).astype(
        jnp.int32
    )
    order_rank = jnp.sum(jnp.cumsum(matches, axis=1) * matches, axis=2) - 1
    is_mine = is_live & (source == own_index)
    slot_target = jnp.where(
        is_mine, jnp.arange(experts, dtype=jnp.int32)[:, None] * CAP + order_rank, experts * CAP
    )
    local_values = jnp.where(is_mine, block_rows - own_index * token_count, token_count)
    local_row = (
        jnp.full((experts * CAP + 1,), token_count, jnp.int32)
        .at[slot_target.ravel()]
        .set(local_values.ravel())[: experts * CAP]
    )
    gate_mine = (
        jnp.zeros((experts * CAP + 1,), jnp.float32)
        .at[slot_target.ravel()]
        .set(jnp.where(is_mine, row_gates, 0.0).ravel())[: experts * CAP]
    )
    live_mine = lax.dynamic_index_in_dim(is_live, my_expert, 0, keepdims=False)
    rows_mine = lax.dynamic_index_in_dim(block_rows, my_expert, 0, keepdims=False)
    source_mine = lax.dynamic_index_in_dim(source, my_expert, 0, keepdims=False)
    rank_mine = lax.dynamic_index_in_dim(order_rank, my_expert, 0, keepdims=False)
    back_index = jnp.where(live_mine, source_mine * CAP + rank_mine, sources * CAP)
    blank_row = jnp.zeros((1, model_width), jnp.bfloat16)
    everyone = lax.all_gather(tokens, "exp", axis=0, tiled=True)
    row_pool = jnp.concatenate([everyone, blank_row], axis=0)
    routed = row_pool[jnp.where(live_mine, rows_mine, sources * token_count)]
    partial_rows = expert_block(routed, w_gate, w_up, w_down)
    outbound = (
        jnp.zeros((sources * CAP + 1, model_width), jnp.bfloat16).at[back_index].set(partial_rows)
    )
    outbound = outbound[: sources * CAP].reshape(sources, CAP, model_width)
    returned = lax.all_to_all(outbound, "exp", split_axis=0, concat_axis=0, tiled=True)
    summed = jnp.sum(
        returned.reshape(experts, per_expert, CAP, model_width), axis=1, dtype=jnp.float32
    )
    weighted = (summed * gate_mine.reshape(experts, CAP, 1)).reshape(experts * CAP, model_width)
    selector = (local_row[:, None] == jnp.arange(token_count, dtype=jnp.int32)[None, :]).astype(
        jnp.float32
    )
    gathered_sum = jnp.einsum("st,sd->td", selector, weighted, precision=lax.Precision.HIGHEST)
    share = lax.psum_scatter(gathered_sum, "hid", scatter_dimension=1, tiled=True)
    return share.astype(jnp.bfloat16)


def solution(mesh):
    sources = mesh.shape["exp"]
    return jax.shard_map(
        local if sources in (4, 8, 16) and mesh.shape["hid"] == 2 else local_wide,
        mesh=mesh,
        in_specs=(
            P(("grp", "exp"), None),
            P(None, ("exp", "hid")),
            P(None, ("exp", "hid")),
            P(("exp", "hid"), None),
            P("grp"),
            P("grp", None),
            P("grp", None),
        ),
        out_specs=P(("grp", "exp"), "hid"),
        check_vma=False,
    )
```

```python
import functools

import jax
import jax.numpy as jnp
from jax import lax
from jax.experimental import pallas as pl
from jax.experimental.pallas import tpu as pltpu
from jax.sharding import PartitionSpec as P

BLOCK = 128
CAP = 3
TILE = 512
MIB = 1 << 20
ORDER = (0, 1, 2, 3, 7, 4, 5, 6)
AHEAD = 20_000_000_000
HBM = pl.BlockSpec(memory_space=pltpu.HBM)
VMEM = pl.BlockSpec(memory_space=pltpu.VMEM)
SMEM = pl.BlockSpec(memory_space=pltpu.SMEM)


def pass_kernel(tokens_ref, out_ref, side_ref, sem):
    copy = pltpu.make_async_copy(tokens_ref, out_ref, sem)
    copy.start()
    side_ref[0] = lax.axis_index("hid")
    copy.wait()


def pass_on(tokens):
    return pl.pallas_call(
        pass_kernel,
        out_shape=(jax.ShapeDtypeStruct(tokens.shape, tokens.dtype), pltpu.SMEM((1,), jnp.int32)),
        in_specs=[HBM],
        out_specs=(VMEM, SMEM),
        scratch_shapes=[pltpu.SemaphoreType.DMA],
        compiler_params=pltpu.CompilerParams(vmem_limit_bytes=2 * MIB),
        cost_estimate=pl.CostEstimate(flops=AHEAD, bytes_accessed=0, transcendentals=0),
    )(pltpu.with_memory_space_constraint(tokens, pltpu.HBM))


def route_kernel(count, per_expert, counts_ref, rows_ref, gates_ref, out_ref):
    experts, slots = rows_ref.shape
    total = out_ref.shape[0]
    line = lax.broadcasted_iota(jnp.int32, (total, slots), 0)
    position = lax.broadcasted_iota(jnp.int32, (total, slots), 1)
    own = lax.axis_index("exp")
    token = own * count + lax.rem(line, count)
    expert = (own // per_expert) ^ (line // count)
    found = jnp.zeros((total, slots), jnp.float32)
    for e in range(experts):
        rows = rows_ref[pl.ds(e, 1), :]
        here = (expert == e) & (rows == token) & (position < counts_ref[e] * BLOCK)
        found = jnp.where(here, gates_ref[pl.ds(e, 1), :], found)
    out_ref[...] = jnp.broadcast_to(jnp.sum(found, axis=1, keepdims=True), out_ref.shape)


def route(block_counts, block_rows, row_gates, sources, count):
    return pl.pallas_call(
        functools.partial(route_kernel, count, sources // block_rows.shape[0]),
        out_shape=jax.ShapeDtypeStruct((block_rows.shape[0] * count, 128), jnp.float32),
        in_specs=[SMEM, VMEM, VMEM],
        out_specs=VMEM,
        compiler_params=pltpu.CompilerParams(vmem_limit_bytes=2 * MIB),
    )(block_counts, block_rows, row_gates)


def pack_kernel(side_ref, tokens_ref, last_ref, *refs):
    out_ref = refs[-1]
    out_ref[0] = jnp.where(side_ref[0] == 0, tokens_ref[...], last_ref[...])
    for r, ref in enumerate(refs[:-1]):
        out_ref[r + 1] = ref[...]


def pack(side, tokens, last, pieces):
    return pl.pallas_call(
        pack_kernel,
        out_shape=jax.ShapeDtypeStruct((1 + len(pieces), *tokens.shape), tokens.dtype),
        in_specs=[SMEM] + [VMEM] * (2 + len(pieces)),
        out_specs=VMEM,
        compiler_params=pltpu.CompilerParams(vmem_limit_bytes=2 * MIB),
    )(in_smem(side), tokens, last, *pieces)


def hidden_kernel(side_ref, mine_ref, got_ref, wg_ref, wu_ref, h_out, wide, x_ref):
    sets, count, _ = mine_ref.shape
    first = side_ref[0] == 0
    for j in range(sets):
        mine = mine_ref[j].astype(jnp.float32)
        got = got_ref[j].astype(jnp.float32)
        wide[pl.ds(j * count, count), :] = jnp.where(first, mine, got)
        wide[pl.ds((sets + j) * count, count), :] = jnp.where(first, got, mine)
    x_ref[...] = wide[...].astype(jnp.bfloat16)

    @pl.loop(0, wg_ref.shape[1] // TILE)
    def _(n):
        cols = pl.ds(pl.multiple_of(n * TILE, TILE), TILE)
        gate = jnp.dot(x_ref[...], wg_ref[:, cols], preferred_element_type=jnp.float32)
        up = jnp.dot(x_ref[...], wu_ref[:, cols], preferred_element_type=jnp.float32)
        h_out[:, cols] = (gate / (1.0 + jnp.exp(-gate)) * up).astype(jnp.bfloat16)


def hidden_rows(side, mine, got, wg, wu):
    total = 2 * mine.shape[0] * mine.shape[1]
    depth, width = wg.shape
    return pl.pallas_call(
        hidden_kernel,
        out_shape=jax.ShapeDtypeStruct((total, width), jnp.bfloat16),
        in_specs=[SMEM] + [VMEM] * 4,
        out_specs=VMEM,
        scratch_shapes=[
            pltpu.VMEM((total, depth), jnp.float32),
            pltpu.VMEM((total, depth), jnp.bfloat16),
        ],
        compiler_params=pltpu.CompilerParams(vmem_limit_bytes=2 * MIB),
        cost_estimate=pl.CostEstimate(
            flops=AHEAD, bytes_accessed=0, transcendentals=total * width
        ),
    )(in_smem(side), mine, got, in_vmem(wg), in_vmem(wu))


def in_smem(x):
    return pltpu.with_memory_space_constraint(x, pltpu.SMEM)


def in_vmem(x):
    return pltpu.with_memory_space_constraint(x, pltpu.VMEM)


def down_kernel(other, side_ref, h_ref, wd_ref, out_ref):
    half = wd_ref.shape[1] // 2
    side = side_ref[0]
    base = (1 - side if other else side) * half
    for n in range(half // TILE):
        cols = pl.ds(pl.multiple_of(base + n * TILE, TILE), TILE)
        part = jnp.dot(h_ref[...], wd_ref[:, cols], preferred_element_type=jnp.float32)
        out_ref[:, pl.ds(n * TILE, TILE)] = part.astype(out_ref.dtype)


def down_half(side, hidden, wd, other, dtype):
    rows, depth = hidden.shape
    half = wd.shape[1] // 2
    return pl.pallas_call(
        functools.partial(down_kernel, other),
        out_shape=jax.ShapeDtypeStruct((rows, half), dtype),
        in_specs=[SMEM, VMEM, VMEM],
        out_specs=VMEM,
        compiler_params=pltpu.CompilerParams(vmem_limit_bytes=2 * MIB),
        cost_estimate=pl.CostEstimate(flops=2 * rows * depth * half, bytes_accessed=0, transcendentals=0),
    )(in_smem(side), hidden, in_vmem(wd))


def near_kernel(keep_ref, got_ref, even_ref, odd_ref):
    both = keep_ref[...] + got_ref[...].astype(jnp.float32)
    pairs, count, _ = odd_ref.shape
    for at, k in enumerate(ORDER):
        rows = both[at * count : (at + 1) * count]
        if k % 2:
            odd_ref[k // 2] = rows.astype(odd_ref.dtype)
        else:
            even_ref[k // 2] = rows


def near(keep, got):
    rows, width = keep.shape
    shape = (len(ORDER) // 2, rows // len(ORDER), width)
    return pl.pallas_call(
        near_kernel,
        out_shape=(jax.ShapeDtypeStruct(shape, jnp.float32), jax.ShapeDtypeStruct(shape, jnp.bfloat16)),
        in_specs=[VMEM, VMEM],
        out_specs=(VMEM, VMEM),
        compiler_params=pltpu.CompilerParams(vmem_limit_bytes=2 * MIB),
    )(keep, got)


def far_kernel(even_ref, got_ref, own_ref, *out_refs):
    for j, out_ref in enumerate((own_ref, *out_refs)):
        out_ref[...] = (even_ref[j] + got_ref[j].astype(jnp.float32)).astype(out_ref.dtype)


def far(even, got):
    sets, count, width = even.shape
    return pl.pallas_call(
        far_kernel,
        out_shape=(jax.ShapeDtypeStruct((count, width), jnp.float32),)
        + (jax.ShapeDtypeStruct((count, width), jnp.bfloat16),) * (sets - 1),
        in_specs=[VMEM, VMEM],
        out_specs=(VMEM,) * sets,
        compiler_params=pltpu.CompilerParams(vmem_limit_bytes=2 * MIB),
    )(even, got)


def sum_kernel(gates_ref, *refs):
    total = jnp.zeros(refs[-1].shape, jnp.float32)
    count = total.shape[0]
    for k, ref in enumerate(refs[:-1]):
        total = total + ref[...].astype(jnp.float32) * gates_ref[pl.ds(k * count, count), :1]
    refs[-1][...] = total.astype(jnp.bfloat16)


def weighted_sum(gates, own, got):
    return pl.pallas_call(
        sum_kernel,
        out_shape=jax.ShapeDtypeStruct(own.shape, jnp.bfloat16),
        in_specs=[VMEM] * (2 + len(got)),
        out_specs=VMEM,
        compiler_params=pltpu.CompilerParams(vmem_limit_bytes=2 * MIB),
    )(gates, own, *got)


def swapped(x, k, sources):
    return lax.ppermute(x, "exp", [(i, i ^ k) for i in range(sources)])


def fetched(x, first, second, sources):
    pairs = []
    for side, k in enumerate((first, second)):
        if k is not None:
            pairs += [(2 * i + side, 2 * (i ^ k) + side) for i in range(sources)]
    return lax.ppermute(x, ("exp", "hid"), pairs)


def swap_cores(x):
    return lax.ppermute(x, "hid", [(0, 1), (1, 0)])


def local(tokens, w_gate, w_up, w_down, block_counts, block_rows, row_gates):
    sources = lax.axis_size("exp")
    tokens, side = pass_on(tokens)
    half = len(ORDER) // 2
    pieces = [fetched(tokens, ORDER[b], ORDER[half + b], sources) for b in range(1, half)]
    last = fetched(tokens, None, ORDER[half], sources)
    mine = pack(side, tokens, last, pieces)
    hidden = hidden_rows(side, mine, swap_cores(mine), w_gate, w_up)
    send = down_half(side, hidden, w_down, True, jnp.bfloat16)
    keep = down_half(side, hidden, w_down, False, jnp.float32)
    even, odd = near(keep, swap_cores(send))
    own, *outgoing = far(even, swapped(odd, 1, sources))
    returned = [swapped(piece, 2 * (j + 1), sources) for j, piece in enumerate(outgoing)]
    gates = route(block_counts, block_rows, row_gates, sources, tokens.shape[0])
    return weighted_sum(gates, own, returned)


def expert_block(segment, w_gate, w_up, w_down):
    gate_act = jnp.dot(segment, w_gate, preferred_element_type=jnp.float32)
    up_act = jnp.dot(segment, w_up, preferred_element_type=jnp.float32)
    hidden = (jax.nn.silu(gate_act) * up_act).astype(jnp.bfloat16)
    return jnp.dot(hidden, w_down, preferred_element_type=jnp.float32).astype(jnp.bfloat16)


def local_wide(tokens, w_gate, w_up, w_down, block_counts, block_rows, row_gates):
    sources = lax.axis_size("exp")
    own_index = lax.axis_index("exp")
    token_count = tokens.shape[0]
    model_width = tokens.shape[1]
    experts = block_rows.shape[0]
    slot_count = block_rows.shape[1]
    per_expert = sources // experts
    my_expert = own_index // per_expert
    position = jnp.arange(slot_count, dtype=jnp.int32)
    is_live = (position[None, :] < block_counts[:, None] * BLOCK) & (block_rows >= 0)
    source = jnp.where(is_live, block_rows // token_count, sources)
    matches = (source[:, :, None] == jnp.arange(sources, dtype=jnp.int32)[None, None, :]).astype(
        jnp.int32
    )
    order_rank = jnp.sum(jnp.cumsum(matches, axis=1) * matches, axis=2) - 1
    is_mine = is_live & (source == own_index)
    slot_target = jnp.where(
        is_mine, jnp.arange(experts, dtype=jnp.int32)[:, None] * CAP + order_rank, experts * CAP
    )
    local_values = jnp.where(is_mine, block_rows - own_index * token_count, token_count)
    local_row = (
        jnp.full((experts * CAP + 1,), token_count, jnp.int32)
        .at[slot_target.ravel()]
        .set(local_values.ravel())[: experts * CAP]
    )
    gate_mine = (
        jnp.zeros((experts * CAP + 1,), jnp.float32)
        .at[slot_target.ravel()]
        .set(jnp.where(is_mine, row_gates, 0.0).ravel())[: experts * CAP]
    )
    live_mine = lax.dynamic_index_in_dim(is_live, my_expert, 0, keepdims=False)
    rows_mine = lax.dynamic_index_in_dim(block_rows, my_expert, 0, keepdims=False)
    source_mine = lax.dynamic_index_in_dim(source, my_expert, 0, keepdims=False)
    rank_mine = lax.dynamic_index_in_dim(order_rank, my_expert, 0, keepdims=False)
    back_index = jnp.where(live_mine, source_mine * CAP + rank_mine, sources * CAP)
    blank_row = jnp.zeros((1, model_width), jnp.bfloat16)
    everyone = lax.all_gather(tokens, "exp", axis=0, tiled=True)
    row_pool = jnp.concatenate([everyone, blank_row], axis=0)
    routed = row_pool[jnp.where(live_mine, rows_mine, sources * token_count)]
    partial_rows = expert_block(routed, w_gate, w_up, w_down)
    outbound = (
        jnp.zeros((sources * CAP + 1, model_width), jnp.bfloat16).at[back_index].set(partial_rows)
    )
    outbound = outbound[: sources * CAP].reshape(sources, CAP, model_width)
    returned = lax.all_to_all(outbound, "exp", split_axis=0, concat_axis=0, tiled=True)
    summed = jnp.sum(
        returned.reshape(experts, per_expert, CAP, model_width), axis=1, dtype=jnp.float32
    )
    weighted = (summed * gate_mine.reshape(experts, CAP, 1)).reshape(experts * CAP, model_width)
    selector = (local_row[:, None] == jnp.arange(token_count, dtype=jnp.int32)[None, :]).astype(
        jnp.float32
    )
    gathered_sum = jnp.einsum("st,sd->td", selector, weighted, precision=lax.Precision.HIGHEST)
    share = lax.psum_scatter(gathered_sum, "hid", scatter_dimension=1, tiled=True)
    return share.astype(jnp.bfloat16)


def solution(mesh):
    small = mesh.shape["exp"] == len(ORDER) and mesh.shape["hid"] == 2

    def chosen(*args):
        return (local if small and args[5].shape[0] * 2 == len(ORDER) else local_wide)(*args)

    return jax.shard_map(
        chosen,
        mesh=mesh,
        in_specs=(
            P(("grp", "exp"), None),
            P(None, ("exp", "hid")),
            P(None, ("exp", "hid")),
            P(("exp", "hid"), None),
            P("grp"),
            P("grp", None),
            P("grp", None),
        ),
        out_specs=P(("grp", "exp"), "hid"),
        check_vma=False,
    )
```

```python
import functools

import jax
import jax.numpy as jnp
from jax import lax
from jax.experimental import pallas as pl
from jax.experimental.pallas import tpu as pltpu
from jax.sharding import PartitionSpec as P

BLOCK = 128
CAP = 3
TILE = 512
MIB = 1 << 20
SOURCES = 8
GATE = 2_000_000_000
UP = 2_000_000_000
AHEAD = 20_000_000_000
HBM = pl.BlockSpec(memory_space=pltpu.HBM)
VMEM = pl.BlockSpec(memory_space=pltpu.VMEM)
SMEM = pl.BlockSpec(memory_space=pltpu.SMEM)


def in_hbm(x):
    return pltpu.with_memory_space_constraint(x, pltpu.HBM)


def in_smem(x):
    return pltpu.with_memory_space_constraint(x, pltpu.SMEM)


def in_vmem(x):
    return pltpu.with_memory_space_constraint(x, pltpu.VMEM)


def take_kernel(tokens_ref, half_ref, side_ref, sem):
    side = lax.axis_index("hid")
    width = half_ref.shape[1]
    columns = pl.ds(pl.multiple_of(side * width, width), width)
    copy = pltpu.make_async_copy(tokens_ref.at[:, columns], half_ref, sem)
    copy.start()
    side_ref[0] = side
    copy.wait()


def take_half(tokens):
    count, width = tokens.shape
    return pl.pallas_call(
        take_kernel,
        out_shape=(jax.ShapeDtypeStruct((count, width // 2), tokens.dtype), pltpu.SMEM((1,), jnp.int32)),
        in_specs=[HBM],
        out_specs=(VMEM, SMEM),
        scratch_shapes=[pltpu.SemaphoreType.DMA],
        compiler_params=pltpu.CompilerParams(vmem_limit_bytes=2 * MIB),
        cost_estimate=pl.CostEstimate(flops=AHEAD, bytes_accessed=0, transcendentals=0),
    )(in_hbm(tokens))


def route_kernel(count, per_expert, counts_ref, rows_ref, gates_ref, out_ref):
    experts, slots = rows_ref.shape
    total = out_ref.shape[0]
    line = lax.broadcasted_iota(jnp.int32, (total, slots), 0)
    position = lax.broadcasted_iota(jnp.int32, (total, slots), 1)
    own = lax.axis_index("exp")
    token = own * count + lax.rem(line, count)
    expert = (own // per_expert) ^ (line // count)
    found = jnp.zeros((total, slots), jnp.float32)
    for e in range(experts):
        rows = rows_ref[pl.ds(e, 1), :]
        here = (expert == e) & (rows == token) & (position < counts_ref[e] * BLOCK)
        found = jnp.where(here, gates_ref[pl.ds(e, 1), :], found)
    out_ref[...] = jnp.broadcast_to(jnp.sum(found, axis=1, keepdims=True), out_ref.shape)


def route(block_counts, block_rows, row_gates, sources, count):
    return pl.pallas_call(
        functools.partial(route_kernel, count, sources // block_rows.shape[0]),
        out_shape=jax.ShapeDtypeStruct((block_rows.shape[0] * count, 128), jnp.float32),
        in_specs=[SMEM, VMEM, VMEM],
        out_specs=VMEM,
        compiler_params=pltpu.CompilerParams(vmem_limit_bytes=2 * MIB),
    )(block_counts, block_rows, row_gates)


def stack_kernel(*refs):
    out_ref = refs[-1]
    for i, ref in enumerate(refs[:-1]):
        out_ref[i] = ref[...]


def stack(*parts):
    return pl.pallas_call(
        stack_kernel,
        out_shape=jax.ShapeDtypeStruct((len(parts), *parts[0].shape), parts[0].dtype),
        in_specs=[VMEM] * len(parts),
        out_specs=VMEM,
        compiler_params=pltpu.CompilerParams(vmem_limit_bytes=2 * MIB),
    )(*parts)


def gate_kernel(side_ref, mine_ref, got_ref, wg_ref, x_ref, act_ref, wide):
    far, near, count, width = mine_ref.shape
    first = side_ref[0] == 0
    for j in range(far):
        for i in range(near):
            rows = pl.ds((j * near + i) * count, count)
            mine = mine_ref[j, i].astype(jnp.float32)
            got = got_ref[j, i].astype(jnp.float32)
            wide[rows, :width] = jnp.where(first, mine, got)
            wide[rows, width:] = jnp.where(first, got, mine)
    x_ref[...] = wide[...].astype(jnp.bfloat16)

    @pl.loop(0, wg_ref.shape[1] // TILE)
    def _(n):
        cols = pl.ds(pl.multiple_of(n * TILE, TILE), TILE)
        gate = jnp.dot(x_ref[...], wg_ref[:, cols], preferred_element_type=jnp.float32)
        act_ref[:, cols] = gate / (1.0 + jnp.exp(-gate))


def gate_rows(side, mine, got, wg):
    total = mine.shape[0] * mine.shape[1] * mine.shape[2]
    depth, width = wg.shape
    return pl.pallas_call(
        gate_kernel,
        out_shape=(
            jax.ShapeDtypeStruct((total, depth), jnp.bfloat16),
            jax.ShapeDtypeStruct((total, width), jnp.float32),
        ),
        in_specs=[SMEM] + [VMEM] * 3,
        out_specs=(VMEM, VMEM),
        scratch_shapes=[pltpu.VMEM((total, depth), jnp.float32)],
        compiler_params=pltpu.CompilerParams(vmem_limit_bytes=2 * MIB),
        cost_estimate=pl.CostEstimate(flops=GATE, bytes_accessed=0, transcendentals=total * width),
    )(in_smem(side), mine, got, in_vmem(wg))


def up_kernel(x_ref, act_ref, wu_ref, h_out):
    @pl.loop(0, wu_ref.shape[1] // TILE)
    def _(n):
        cols = pl.ds(pl.multiple_of(n * TILE, TILE), TILE)
        up = jnp.dot(x_ref[...], wu_ref[:, cols], preferred_element_type=jnp.float32)
        h_out[:, cols] = (act_ref[:, cols] * up).astype(jnp.bfloat16)


def hidden_rows(x, act, wu):
    return pl.pallas_call(
        up_kernel,
        out_shape=jax.ShapeDtypeStruct(act.shape, jnp.bfloat16),
        in_specs=[VMEM] * 3,
        out_specs=VMEM,
        compiler_params=pltpu.CompilerParams(vmem_limit_bytes=2 * MIB),
        cost_estimate=pl.CostEstimate(flops=UP, bytes_accessed=0, transcendentals=0),
    )(x, act, in_vmem(wu))


def down_kernel(other, side_ref, h_ref, wd_ref, out_ref):
    half = wd_ref.shape[1] // 2
    side = side_ref[0]
    base = (1 - side if other else side) * half
    for n in range(half // TILE):
        cols = pl.ds(pl.multiple_of(base + n * TILE, TILE), TILE)
        part = jnp.dot(h_ref[...], wd_ref[:, cols], preferred_element_type=jnp.float32)
        out_ref[:, pl.ds(n * TILE, TILE)] = part.astype(out_ref.dtype)


def down_half(side, hidden, wd, other, dtype):
    rows, depth = hidden.shape
    half = wd.shape[1] // 2
    return pl.pallas_call(
        functools.partial(down_kernel, other),
        out_shape=jax.ShapeDtypeStruct((rows, half), dtype),
        in_specs=[SMEM, VMEM, VMEM],
        out_specs=VMEM,
        compiler_params=pltpu.CompilerParams(vmem_limit_bytes=2 * MIB),
        cost_estimate=pl.CostEstimate(flops=2 * rows * depth * half, bytes_accessed=0, transcendentals=0),
    )(in_smem(side), hidden, in_vmem(wd))


def near_kernel(keep_ref, got_ref, even_ref, odd_ref):
    both = keep_ref[...] + got_ref[...].astype(jnp.float32)
    sets, count, _ = odd_ref.shape
    for j in range(sets):
        even_ref[j] = both[2 * j * count : (2 * j + 1) * count]
        odd_ref[j] = both[(2 * j + 1) * count : (2 * j + 2) * count].astype(odd_ref.dtype)


def near(keep, got):
    rows, width = keep.shape
    shape = (SOURCES // 2, rows // SOURCES, width)
    return pl.pallas_call(
        near_kernel,
        out_shape=(jax.ShapeDtypeStruct(shape, jnp.float32), jax.ShapeDtypeStruct(shape, jnp.bfloat16)),
        in_specs=[VMEM, VMEM],
        out_specs=(VMEM, VMEM),
        compiler_params=pltpu.CompilerParams(vmem_limit_bytes=2 * MIB),
    )(keep, got)


def far_kernel(even_ref, got_ref, own_ref, *out_refs):
    for j, out_ref in enumerate((own_ref, *out_refs)):
        out_ref[...] = (even_ref[j] + got_ref[j].astype(jnp.float32)).astype(out_ref.dtype)


def far(even, got):
    sets, count, width = even.shape
    return pl.pallas_call(
        far_kernel,
        out_shape=(jax.ShapeDtypeStruct((count, width), jnp.float32),)
        + (jax.ShapeDtypeStruct((count, width), jnp.bfloat16),) * (sets - 1),
        in_specs=[VMEM, VMEM],
        out_specs=(VMEM,) * sets,
        compiler_params=pltpu.CompilerParams(vmem_limit_bytes=2 * MIB),
    )(even, got)


def sum_kernel(gates_ref, *refs):
    total = jnp.zeros(refs[-1].shape, jnp.float32)
    count = total.shape[0]
    for k, ref in enumerate(refs[:-1]):
        total = total + ref[...].astype(jnp.float32) * gates_ref[pl.ds(k * count, count), :1]
    refs[-1][...] = total.astype(jnp.bfloat16)


def weighted_sum(gates, own, got):
    return pl.pallas_call(
        sum_kernel,
        out_shape=jax.ShapeDtypeStruct(own.shape, jnp.bfloat16),
        in_specs=[VMEM] * (2 + len(got)),
        out_specs=VMEM,
        compiler_params=pltpu.CompilerParams(vmem_limit_bytes=2 * MIB),
    )(gates, own, *got)


def swapped(x, k):
    return lax.ppermute(x, "exp", [(i, i ^ k) for i in range(SOURCES)])


def swap_cores(x):
    return lax.ppermute(x, "hid", [(0, 1), (1, 0)])


def local(tokens, w_gate, w_up, w_down, block_counts, block_rows, row_gates):
    half, side = take_half(tokens)
    pair = stack(half, swapped(half, 1))
    mine = stack(pair, *[swapped(pair, 2 * j) for j in range(1, SOURCES // 2)])
    x, act = gate_rows(side, mine, swap_cores(mine), w_gate)
    hidden = hidden_rows(x, act, w_up)
    send = down_half(side, hidden, w_down, True, jnp.bfloat16)
    keep = down_half(side, hidden, w_down, False, jnp.float32)
    even, odd = near(keep, swap_cores(send))
    own, *outgoing = far(even, swapped(odd, 1))
    returned = [swapped(piece, 2 * (j + 1)) for j, piece in enumerate(outgoing)]
    gates = route(block_counts, block_rows, row_gates, SOURCES, tokens.shape[0])
    return weighted_sum(gates, own, returned)


def expert_block(segment, w_gate, w_up, w_down):
    gate_act = jnp.dot(segment, w_gate, preferred_element_type=jnp.float32)
    up_act = jnp.dot(segment, w_up, preferred_element_type=jnp.float32)
    hidden = (jax.nn.silu(gate_act) * up_act).astype(jnp.bfloat16)
    return jnp.dot(hidden, w_down, preferred_element_type=jnp.float32).astype(jnp.bfloat16)


def local_wide(tokens, w_gate, w_up, w_down, block_counts, block_rows, row_gates):
    sources = lax.axis_size("exp")
    own_index = lax.axis_index("exp")
    token_count = tokens.shape[0]
    model_width = tokens.shape[1]
    experts = block_rows.shape[0]
    slot_count = block_rows.shape[1]
    per_expert = sources // experts
    my_expert = own_index // per_expert
    position = jnp.arange(slot_count, dtype=jnp.int32)
    is_live = (position[None, :] < block_counts[:, None] * BLOCK) & (block_rows >= 0)
    source = jnp.where(is_live, block_rows // token_count, sources)
    matches = (source[:, :, None] == jnp.arange(sources, dtype=jnp.int32)[None, None, :]).astype(
        jnp.int32
    )
    order_rank = jnp.sum(jnp.cumsum(matches, axis=1) * matches, axis=2) - 1
    is_mine = is_live & (source == own_index)
    slot_target = jnp.where(
        is_mine, jnp.arange(experts, dtype=jnp.int32)[:, None] * CAP + order_rank, experts * CAP
    )
    local_values = jnp.where(is_mine, block_rows - own_index * token_count, token_count)
    local_row = (
        jnp.full((experts * CAP + 1,), token_count, jnp.int32)
        .at[slot_target.ravel()]
        .set(local_values.ravel())[: experts * CAP]
    )
    gate_mine = (
        jnp.zeros((experts * CAP + 1,), jnp.float32)
        .at[slot_target.ravel()]
        .set(jnp.where(is_mine, row_gates, 0.0).ravel())[: experts * CAP]
    )
    live_mine = lax.dynamic_index_in_dim(is_live, my_expert, 0, keepdims=False)
    rows_mine = lax.dynamic_index_in_dim(block_rows, my_expert, 0, keepdims=False)
    source_mine = lax.dynamic_index_in_dim(source, my_expert, 0, keepdims=False)
    rank_mine = lax.dynamic_index_in_dim(order_rank, my_expert, 0, keepdims=False)
    back_index = jnp.where(live_mine, source_mine * CAP + rank_mine, sources * CAP)
    blank_row = jnp.zeros((1, model_width), jnp.bfloat16)
    everyone = lax.all_gather(tokens, "exp", axis=0, tiled=True)
    row_pool = jnp.concatenate([everyone, blank_row], axis=0)
    routed = row_pool[jnp.where(live_mine, rows_mine, sources * token_count)]
    partial_rows = expert_block(routed, w_gate, w_up, w_down)
    outbound = (
        jnp.zeros((sources * CAP + 1, model_width), jnp.bfloat16).at[back_index].set(partial_rows)
    )
    outbound = outbound[: sources * CAP].reshape(sources, CAP, model_width)
    returned = lax.all_to_all(outbound, "exp", split_axis=0, concat_axis=0, tiled=True)
    summed = jnp.sum(
        returned.reshape(experts, per_expert, CAP, model_width), axis=1, dtype=jnp.float32
    )
    weighted = (summed * gate_mine.reshape(experts, CAP, 1)).reshape(experts * CAP, model_width)
    selector = (local_row[:, None] == jnp.arange(token_count, dtype=jnp.int32)[None, :]).astype(
        jnp.float32
    )
    gathered_sum = jnp.einsum("st,sd->td", selector, weighted, precision=lax.Precision.HIGHEST)
    share = lax.psum_scatter(gathered_sum, "hid", scatter_dimension=1, tiled=True)
    return share.astype(jnp.bfloat16)


def solution(mesh):
    small = mesh.shape["exp"] == SOURCES and mesh.shape["hid"] == 2

    def chosen(*args):
        return (local if small and args[5].shape[0] * 2 == SOURCES else local_wide)(*args)

    return jax.shard_map(
        chosen,
        mesh=mesh,
        in_specs=(
            P(("grp", "exp"), None),
            P(None, ("exp", "hid")),
            P(None, ("exp", "hid")),
            P(("exp", "hid"), None),
            P("grp"),
            P("grp", None),
            P("grp", None),
        ),
        out_specs=P(("grp", "exp"), "hid"),
        check_vma=False,
    )
```

```python
import functools

import jax
import jax.numpy as jnp
from jax import lax
from jax.experimental import pallas as pl
from jax.experimental.pallas import tpu as pltpu
from jax.sharding import PartitionSpec as P

BLOCK = 128
CAP = 3
TILE = 512
MIB = 1 << 20
ORDER = (0, 7, 6, 1, 2, 5, 4, 3)
SOURCES = len(ORDER)
GATE = 5_000_000_000
UP = 2_000_000_000
AHEAD = 20_000_000_000
HBM = pl.BlockSpec(memory_space=pltpu.HBM)
VMEM = pl.BlockSpec(memory_space=pltpu.VMEM)
SMEM = pl.BlockSpec(memory_space=pltpu.SMEM)


def in_hbm(x):
    return pltpu.with_memory_space_constraint(x, pltpu.HBM)


def in_smem(x):
    return pltpu.with_memory_space_constraint(x, pltpu.SMEM)


def in_vmem(x):
    return pltpu.with_memory_space_constraint(x, pltpu.VMEM)


def pass_kernel(tokens_ref, out_ref, side_ref, sem):
    copy = pltpu.make_async_copy(tokens_ref, out_ref, sem)
    copy.start()
    side_ref[0] = lax.axis_index("hid")
    copy.wait()


def pass_on(tokens):
    return pl.pallas_call(
        pass_kernel,
        out_shape=(jax.ShapeDtypeStruct(tokens.shape, tokens.dtype), pltpu.SMEM((1,), jnp.int32)),
        in_specs=[HBM],
        out_specs=(VMEM, SMEM),
        scratch_shapes=[pltpu.SemaphoreType.DMA],
        compiler_params=pltpu.CompilerParams(vmem_limit_bytes=2 * MIB),
        cost_estimate=pl.CostEstimate(flops=AHEAD, bytes_accessed=0, transcendentals=0),
    )(in_hbm(tokens))


def route_kernel(count, per_expert, counts_ref, rows_ref, gates_ref, out_ref):
    experts, slots = rows_ref.shape
    total = out_ref.shape[0]
    line = lax.broadcasted_iota(jnp.int32, (total, slots), 0)
    position = lax.broadcasted_iota(jnp.int32, (total, slots), 1)
    own = lax.axis_index("exp")
    block = line // count
    token = (own ^ lax.rem(block, per_expert)) * count + lax.rem(line, count)
    expert = (own // per_expert) ^ (block // per_expert)
    found = jnp.zeros((total, slots), jnp.float32)
    for e in range(experts):
        rows = rows_ref[pl.ds(e, 1), :]
        here = (expert == e) & (rows == token) & (position < counts_ref[e] * BLOCK)
        found = jnp.where(here, gates_ref[pl.ds(e, 1), :], found)
    out_ref[...] = jnp.broadcast_to(jnp.sum(found, axis=1, keepdims=True), out_ref.shape)


def route(block_counts, block_rows, row_gates, count):
    return pl.pallas_call(
        functools.partial(route_kernel, count, SOURCES // block_rows.shape[0]),
        out_shape=jax.ShapeDtypeStruct((SOURCES * count, 128), jnp.float32),
        in_specs=[SMEM, VMEM, VMEM],
        out_specs=VMEM,
        compiler_params=pltpu.CompilerParams(vmem_limit_bytes=2 * MIB),
    )(block_counts, block_rows, row_gates)


def pack_kernel(side_ref, tokens_ref, *refs):
    *pieces, last_ref, out_ref = refs
    for r, ref in enumerate(pieces):
        out_ref[r + 1] = ref[...]
    out_ref[0] = jnp.where(side_ref[0] == 0, tokens_ref[...], last_ref[...])


def pack(side, tokens, pieces):
    return pl.pallas_call(
        pack_kernel,
        out_shape=jax.ShapeDtypeStruct((len(pieces), *tokens.shape), tokens.dtype),
        in_specs=[SMEM] + [VMEM] * (1 + len(pieces)),
        out_specs=VMEM,
        compiler_params=pltpu.CompilerParams(vmem_limit_bytes=2 * MIB),
    )(in_smem(side), tokens, *pieces)


def gate_kernel(side_ref, mine_ref, got_ref, wg_ref, x_ref, act_ref, wide):
    sets, count, _ = mine_ref.shape
    first = side_ref[0] == 0
    for j in range(sets):
        mine = mine_ref[j].astype(jnp.float32)
        got = got_ref[j].astype(jnp.float32)
        wide[pl.ds(j * count, count), :] = jnp.where(first, mine, got)
        wide[pl.ds((sets + j) * count, count), :] = jnp.where(first, got, mine)
    x_ref[...] = wide[...].astype(jnp.bfloat16)

    @pl.loop(0, wg_ref.shape[1] // TILE)
    def _(n):
        cols = pl.ds(pl.multiple_of(n * TILE, TILE), TILE)
        gate = jnp.dot(x_ref[...], wg_ref[:, cols], preferred_element_type=jnp.float32)
        act_ref[:, cols] = gate / (1.0 + jnp.exp(-gate))


def gate_rows(side, mine, got, wg):
    total = 2 * mine.shape[0] * mine.shape[1]
    depth, width = wg.shape
    return pl.pallas_call(
        gate_kernel,
        out_shape=(
            jax.ShapeDtypeStruct((total, depth), jnp.bfloat16),
            jax.ShapeDtypeStruct((total, width), jnp.float32),
        ),
        in_specs=[SMEM] + [VMEM] * 3,
        out_specs=(VMEM, VMEM),
        scratch_shapes=[pltpu.VMEM((total, depth), jnp.float32)],
        compiler_params=pltpu.CompilerParams(vmem_limit_bytes=2 * MIB),
        cost_estimate=pl.CostEstimate(flops=GATE, bytes_accessed=0, transcendentals=total * width),
    )(in_smem(side), mine, got, in_vmem(wg))


def up_kernel(x_ref, act_ref, wu_ref, h_out):
    @pl.loop(0, wu_ref.shape[1] // TILE)
    def _(n):
        cols = pl.ds(pl.multiple_of(n * TILE, TILE), TILE)
        up = jnp.dot(x_ref[...], wu_ref[:, cols], preferred_element_type=jnp.float32)
        h_out[:, cols] = (act_ref[:, cols] * up).astype(jnp.bfloat16)


def hidden_rows(x, act, wu):
    return pl.pallas_call(
        up_kernel,
        out_shape=jax.ShapeDtypeStruct(act.shape, jnp.bfloat16),
        in_specs=[VMEM] * 3,
        out_specs=VMEM,
        compiler_params=pltpu.CompilerParams(vmem_limit_bytes=2 * MIB),
        cost_estimate=pl.CostEstimate(flops=UP, bytes_accessed=0, transcendentals=0),
    )(x, act, in_vmem(wu))


def down_kernel(other, side_ref, h_ref, wd_ref, out_ref):
    half = wd_ref.shape[1] // 2
    side = side_ref[0]
    base = (1 - side if other else side) * half
    for n in range(half // TILE):
        cols = pl.ds(pl.multiple_of(base + n * TILE, TILE), TILE)
        part = jnp.dot(h_ref[...], wd_ref[:, cols], preferred_element_type=jnp.float32)
        out_ref[:, pl.ds(n * TILE, TILE)] = part.astype(out_ref.dtype)


def down_half(side, hidden, wd, other, dtype):
    rows, depth = hidden.shape
    half = wd.shape[1] // 2
    return pl.pallas_call(
        functools.partial(down_kernel, other),
        out_shape=jax.ShapeDtypeStruct((rows, half), dtype),
        in_specs=[SMEM, VMEM, VMEM],
        out_specs=VMEM,
        compiler_params=pltpu.CompilerParams(vmem_limit_bytes=2 * MIB),
        cost_estimate=pl.CostEstimate(flops=2 * rows * depth * half, bytes_accessed=0, transcendentals=0),
    )(in_smem(side), hidden, in_vmem(wd))


def near_kernel(keep_ref, got_ref, own_ref, *out_refs):
    near, count, _ = own_ref.shape
    both = keep_ref[...] + got_ref[...].astype(jnp.float32)
    for at, k in enumerate(ORDER):
        out_ref = (own_ref, *out_refs)[k // near]
        out_ref[k % near] = both[at * count : (at + 1) * count].astype(out_ref.dtype)


def near(keep, got, per_expert):
    rows, width = keep.shape
    shape = (per_expert, rows // SOURCES, width)
    others = SOURCES // per_expert - 1
    return pl.pallas_call(
        near_kernel,
        out_shape=(jax.ShapeDtypeStruct(shape, jnp.float32),)
        + (jax.ShapeDtypeStruct(shape, jnp.bfloat16),) * others,
        in_specs=[VMEM, VMEM],
        out_specs=(VMEM,) * (1 + others),
        compiler_params=pltpu.CompilerParams(vmem_limit_bytes=2 * MIB),
    )(keep, got)


def weigh_kernel(gates_ref, *refs):
    *parts, own_ref, next_ref = refs
    near, count, _ = parts[0].shape
    for i, out_ref in enumerate((own_ref, next_ref)):
        total = jnp.zeros(out_ref.shape, jnp.float32)
        for at, part_ref in enumerate(parts):
            j = (len(parts) - at) % len(parts)
            gates = gates_ref[pl.ds((j * near + i) * count, count), :1]
            total = total + part_ref[i].astype(jnp.float32) * gates
        out_ref[...] = total.astype(out_ref.dtype)


def weigh(gates, parts):
    shape = parts[0].shape[1:]
    return pl.pallas_call(
        weigh_kernel,
        out_shape=(jax.ShapeDtypeStruct(shape, jnp.float32), jax.ShapeDtypeStruct(shape, jnp.bfloat16)),
        in_specs=[VMEM] * (1 + len(parts)),
        out_specs=(VMEM, VMEM),
        compiler_params=pltpu.CompilerParams(vmem_limit_bytes=2 * MIB),
    )(gates, *parts)


def sum_kernel(own_ref, got_ref, out_ref):
    out_ref[...] = (own_ref[...] + got_ref[...].astype(jnp.float32)).astype(out_ref.dtype)


def final_sum(own, got):
    return pl.pallas_call(
        sum_kernel,
        out_shape=jax.ShapeDtypeStruct(own.shape, jnp.bfloat16),
        in_specs=[VMEM, VMEM],
        out_specs=VMEM,
        compiler_params=pltpu.CompilerParams(vmem_limit_bytes=2 * MIB),
    )(own, got)


def swapped(x, k):
    return lax.ppermute(x, "exp", [(i, i ^ k) for i in range(SOURCES)])


def fetched(x, first, second):
    pairs = []
    for side, k in enumerate((first, second)):
        if k is not None:
            pairs += [(2 * i + side, 2 * (i ^ k) + side) for i in range(SOURCES)]
    return lax.ppermute(x, ("exp", "hid"), pairs)


def swap_cores(x):
    return lax.ppermute(x, "hid", [(0, 1), (1, 0)])


def local(tokens, w_gate, w_up, w_down, block_counts, block_rows, row_gates):
    per_expert = SOURCES // block_rows.shape[0]
    tokens, side = pass_on(tokens)
    half = SOURCES // 2
    pieces = [fetched(tokens, ORDER[b], ORDER[half + b]) for b in range(1, half)]
    pieces += [fetched(tokens, None, ORDER[half])]
    mine = pack(side, tokens, pieces)
    x, act = gate_rows(side, mine, swap_cores(mine), w_gate)
    hidden = hidden_rows(x, act, w_up)
    send = down_half(side, hidden, w_down, True, jnp.bfloat16)
    keep = down_half(side, hidden, w_down, False, jnp.float32)
    parts = near(keep, swap_cores(send), per_expert)
    returned = [swapped(parts[j], per_expert * j) for j in range(len(parts) - 1, 0, -1)]
    gates = route(block_counts, block_rows, row_gates, tokens.shape[0])
    own, other = weigh(gates, [parts[0], *returned])
    return final_sum(own, swapped(other, 1))


def expert_block(segment, w_gate, w_up, w_down):
    gate_act = jnp.dot(segment, w_gate, preferred_element_type=jnp.float32)
    up_act = jnp.dot(segment, w_up, preferred_element_type=jnp.float32)
    hidden = (jax.nn.silu(gate_act) * up_act).astype(jnp.bfloat16)
    return jnp.dot(hidden, w_down, preferred_element_type=jnp.float32).astype(jnp.bfloat16)


def local_wide(tokens, w_gate, w_up, w_down, block_counts, block_rows, row_gates):
    sources = lax.axis_size("exp")
    own_index = lax.axis_index("exp")
    token_count = tokens.shape[0]
    model_width = tokens.shape[1]
    experts = block_rows.shape[0]
    slot_count = block_rows.shape[1]
    per_expert = sources // experts
    my_expert = own_index // per_expert
    position = jnp.arange(slot_count, dtype=jnp.int32)
    is_live = (position[None, :] < block_counts[:, None] * BLOCK) & (block_rows >= 0)
    source = jnp.where(is_live, block_rows // token_count, sources)
    matches = (source[:, :, None] == jnp.arange(sources, dtype=jnp.int32)[None, None, :]).astype(
        jnp.int32
    )
    order_rank = jnp.sum(jnp.cumsum(matches, axis=1) * matches, axis=2) - 1
    is_mine = is_live & (source == own_index)
    slot_target = jnp.where(
        is_mine, jnp.arange(experts, dtype=jnp.int32)[:, None] * CAP + order_rank, experts * CAP
    )
    local_values = jnp.where(is_mine, block_rows - own_index * token_count, token_count)
    local_row = (
        jnp.full((experts * CAP + 1,), token_count, jnp.int32)
        .at[slot_target.ravel()]
        .set(local_values.ravel())[: experts * CAP]
    )
    gate_mine = (
        jnp.zeros((experts * CAP + 1,), jnp.float32)
        .at[slot_target.ravel()]
        .set(jnp.where(is_mine, row_gates, 0.0).ravel())[: experts * CAP]
    )
    live_mine = lax.dynamic_index_in_dim(is_live, my_expert, 0, keepdims=False)
    rows_mine = lax.dynamic_index_in_dim(block_rows, my_expert, 0, keepdims=False)
    source_mine = lax.dynamic_index_in_dim(source, my_expert, 0, keepdims=False)
    rank_mine = lax.dynamic_index_in_dim(order_rank, my_expert, 0, keepdims=False)
    back_index = jnp.where(live_mine, source_mine * CAP + rank_mine, sources * CAP)
    blank_row = jnp.zeros((1, model_width), jnp.bfloat16)
    everyone = lax.all_gather(tokens, "exp", axis=0, tiled=True)
    row_pool = jnp.concatenate([everyone, blank_row], axis=0)
    routed = row_pool[jnp.where(live_mine, rows_mine, sources * token_count)]
    partial_rows = expert_block(routed, w_gate, w_up, w_down)
    outbound = (
        jnp.zeros((sources * CAP + 1, model_width), jnp.bfloat16).at[back_index].set(partial_rows)
    )
    outbound = outbound[: sources * CAP].reshape(sources, CAP, model_width)
    returned = lax.all_to_all(outbound, "exp", split_axis=0, concat_axis=0, tiled=True)
    summed = jnp.sum(
        returned.reshape(experts, per_expert, CAP, model_width), axis=1, dtype=jnp.float32
    )
    weighted = (summed * gate_mine.reshape(experts, CAP, 1)).reshape(experts * CAP, model_width)
    selector = (local_row[:, None] == jnp.arange(token_count, dtype=jnp.int32)[None, :]).astype(
        jnp.float32
    )
    gathered_sum = jnp.einsum("st,sd->td", selector, weighted, precision=lax.Precision.HIGHEST)
    share = lax.psum_scatter(gathered_sum, "hid", scatter_dimension=1, tiled=True)
    return share.astype(jnp.bfloat16)


def solution(mesh):
    small = mesh.shape["exp"] == SOURCES and mesh.shape["hid"] == 2

    def chosen(*args):
        return (local if small and args[5].shape[0] * 2 == SOURCES else local_wide)(*args)

    return jax.shard_map(
        chosen,
        mesh=mesh,
        in_specs=(
            P(("grp", "exp"), None),
            P(None, ("exp", "hid")),
            P(None, ("exp", "hid")),
            P(("exp", "hid"), None),
            P("grp"),
            P("grp", None),
            P("grp", None),
        ),
        out_specs=P(("grp", "exp"), "hid"),
        check_vma=False,
    )
```

```python
import functools

import jax
import jax.numpy as jnp
from jax import lax
from jax.experimental import pallas as pl
from jax.experimental.pallas import tpu as pltpu
from jax.sharding import PartitionSpec as P

BLOCK = 128
CAP = 3
TILE = 512
MIB = 1 << 20
ORDER = (0, 7, 6, 1, 2, 5, 4, 3)
SOURCES = len(ORDER)
GATE = 5_000_000_000
UP = 2_000_000_000
AHEAD = 20_000_000_000
HBM = pl.BlockSpec(memory_space=pltpu.HBM)
VMEM = pl.BlockSpec(memory_space=pltpu.VMEM)
SMEM = pl.BlockSpec(memory_space=pltpu.SMEM)


def in_hbm(x):
    return pltpu.with_memory_space_constraint(x, pltpu.HBM)


def in_smem(x):
    return pltpu.with_memory_space_constraint(x, pltpu.SMEM)


def in_vmem(x):
    return pltpu.with_memory_space_constraint(x, pltpu.VMEM)


def pass_kernel(tokens_ref, out_ref, place_ref, sem):
    copy = pltpu.make_async_copy(tokens_ref, out_ref, sem)
    copy.start()
    place_ref[0] = lax.axis_index("hid")
    place_ref[1] = lax.axis_index("exp")
    copy.wait()


def pass_on(tokens):
    return pl.pallas_call(
        pass_kernel,
        out_shape=(jax.ShapeDtypeStruct(tokens.shape, tokens.dtype), pltpu.SMEM((2,), jnp.int32)),
        in_specs=[HBM],
        out_specs=(VMEM, SMEM),
        scratch_shapes=[pltpu.SemaphoreType.DMA],
        compiler_params=pltpu.CompilerParams(vmem_limit_bytes=2 * MIB),
        cost_estimate=pl.CostEstimate(flops=AHEAD, bytes_accessed=0, transcendentals=0),
    )(in_hbm(tokens))


def route_kernel(count, per_expert, counts_ref, rows_ref, gates_ref, out_ref):
    experts, slots = rows_ref.shape
    total = out_ref.shape[0]
    line = lax.broadcasted_iota(jnp.int32, (total, slots), 0)
    position = lax.broadcasted_iota(jnp.int32, (total, slots), 1)
    own = lax.axis_index("exp")
    block = line // count
    token = (own ^ lax.rem(block, per_expert)) * count + lax.rem(line, count)
    expert = block // per_expert
    found = jnp.zeros((total, slots), jnp.float32)
    for e in range(experts):
        rows = rows_ref[pl.ds(e, 1), :]
        here = (expert == e) & (rows == token) & (position < counts_ref[e] * BLOCK)
        found = jnp.where(here, gates_ref[pl.ds(e, 1), :], found)
    out_ref[...] = jnp.broadcast_to(jnp.sum(found, axis=1, keepdims=True), out_ref.shape)


def route(block_counts, block_rows, row_gates, count):
    return pl.pallas_call(
        functools.partial(route_kernel, count, SOURCES // block_rows.shape[0]),
        out_shape=jax.ShapeDtypeStruct((SOURCES * count, 128), jnp.float32),
        in_specs=[SMEM, VMEM, VMEM],
        out_specs=VMEM,
        compiler_params=pltpu.CompilerParams(vmem_limit_bytes=2 * MIB),
    )(block_counts, block_rows, row_gates)


def pack_kernel(place_ref, tokens_ref, *refs):
    *pieces, last_ref, out_ref = refs
    for r, ref in enumerate(pieces):
        out_ref[r + 1] = ref[...]
    out_ref[0] = jnp.where(place_ref[0] == 0, tokens_ref[...], last_ref[...])


def pack(place, tokens, pieces):
    return pl.pallas_call(
        pack_kernel,
        out_shape=jax.ShapeDtypeStruct((len(pieces), *tokens.shape), tokens.dtype),
        in_specs=[SMEM] + [VMEM] * (1 + len(pieces)),
        out_specs=VMEM,
        compiler_params=pltpu.CompilerParams(vmem_limit_bytes=2 * MIB),
    )(in_smem(place), tokens, *pieces)


def gate_kernel(place_ref, mine_ref, got_ref, wg_ref, x_ref, act_ref, wide):
    sets, count, _ = mine_ref.shape
    for j in range(sets):
        rows = pl.ds(j * count, count)
        wide[place_ref[0], rows, :] = mine_ref[j].astype(jnp.float32)
        wide[1 - place_ref[0], rows, :] = got_ref[j].astype(jnp.float32)
    x_ref[...] = wide[...].reshape(x_ref.shape).astype(jnp.bfloat16)

    for n in range(wg_ref.shape[1] // TILE):
        cols = pl.ds(n * TILE, TILE)
        gate = jnp.dot(x_ref[...], wg_ref[:, cols], preferred_element_type=jnp.float32)
        act_ref[:, cols] = gate / (1.0 + jnp.exp(-gate))


def gate_rows(place, mine, got, wg):
    total = 2 * mine.shape[0] * mine.shape[1]
    depth, width = wg.shape
    return pl.pallas_call(
        gate_kernel,
        out_shape=(
            jax.ShapeDtypeStruct((total, depth), jnp.bfloat16),
            jax.ShapeDtypeStruct((total, width), jnp.float32),
        ),
        in_specs=[SMEM] + [VMEM] * 3,
        out_specs=(VMEM, VMEM),
        scratch_shapes=[pltpu.VMEM((2, total // 2, depth), jnp.float32)],
        compiler_params=pltpu.CompilerParams(vmem_limit_bytes=2 * MIB),
        cost_estimate=pl.CostEstimate(flops=GATE, bytes_accessed=0, transcendentals=total * width),
    )(in_smem(place), mine, got, in_vmem(wg))


def up_kernel(x_ref, act_ref, wu_ref, h_out):
    for n in range(wu_ref.shape[1] // TILE):
        cols = pl.ds(n * TILE, TILE)
        up = jnp.dot(x_ref[...], wu_ref[:, cols], preferred_element_type=jnp.float32)
        h_out[:, cols] = (act_ref[:, cols] * up).astype(jnp.bfloat16)


def hidden_rows(x, act, wu):
    return pl.pallas_call(
        up_kernel,
        out_shape=jax.ShapeDtypeStruct(act.shape, jnp.bfloat16),
        in_specs=[VMEM] * 3,
        out_specs=VMEM,
        compiler_params=pltpu.CompilerParams(vmem_limit_bytes=2 * MIB),
        cost_estimate=pl.CostEstimate(flops=UP, bytes_accessed=0, transcendentals=0),
    )(x, act, in_vmem(wu))


def down_kernel(other, place_ref, h_ref, wd_ref, out_ref):
    half = wd_ref.shape[1] // 2
    side = place_ref[0]
    base = (1 - side if other else side) * half
    for n in range(half // TILE):
        cols = pl.ds(pl.multiple_of(base + n * TILE, TILE), TILE)
        part = jnp.dot(h_ref[...], wd_ref[:, cols], preferred_element_type=jnp.float32)
        out_ref[:, pl.ds(n * TILE, TILE)] = part.astype(out_ref.dtype)


def down_half(place, hidden, wd, other, dtype):
    rows, depth = hidden.shape
    half = wd.shape[1] // 2
    return pl.pallas_call(
        functools.partial(down_kernel, other),
        out_shape=jax.ShapeDtypeStruct((rows, half), dtype),
        in_specs=[SMEM, VMEM, VMEM],
        out_specs=VMEM,
        compiler_params=pltpu.CompilerParams(vmem_limit_bytes=2 * MIB),
        cost_estimate=pl.CostEstimate(flops=2 * rows * depth * half, bytes_accessed=0, transcendentals=0),
    )(in_smem(place), hidden, in_vmem(wd))


def near_kernel(place_ref, keep_ref, got_ref, out_ref):
    _, near, count, _ = out_ref.shape
    both = keep_ref[...] + got_ref[...].astype(jnp.float32)
    expert = place_ref[1] // near
    for at, k in enumerate(ORDER):
        out_ref[expert ^ (k // near), k % near] = both[at * count : (at + 1) * count].astype(out_ref.dtype)


def near(place, keep, got, per_expert):
    rows, width = keep.shape
    return pl.pallas_call(
        near_kernel,
        out_shape=jax.ShapeDtypeStruct(
            (SOURCES // per_expert, per_expert, rows // SOURCES, width), jnp.bfloat16
        ),
        in_specs=[SMEM, VMEM, VMEM],
        out_specs=VMEM,
        compiler_params=pltpu.CompilerParams(vmem_limit_bytes=2 * MIB),
    )(in_smem(place), keep, got)


def weigh_kernel(gates_ref, parts_ref, own_ref, next_ref):
    experts, near, count, _ = parts_ref.shape
    for i, out_ref in enumerate((own_ref, next_ref)):
        total = jnp.zeros(out_ref.shape, jnp.float32)
        for e in range(experts):
            gates = gates_ref[pl.ds((e * near + i) * count, count), :1]
            total = total + parts_ref[e, i].astype(jnp.float32) * gates
        out_ref[...] = total.astype(out_ref.dtype)


def weigh(gates, parts):
    shape = parts.shape[2:]
    return pl.pallas_call(
        weigh_kernel,
        out_shape=(jax.ShapeDtypeStruct(shape, jnp.float32), jax.ShapeDtypeStruct(shape, jnp.bfloat16)),
        in_specs=[VMEM, VMEM],
        out_specs=(VMEM, VMEM),
        compiler_params=pltpu.CompilerParams(vmem_limit_bytes=2 * MIB),
    )(gates, parts)


def sum_kernel(own_ref, got_ref, out_ref):
    out_ref[...] = (own_ref[...] + got_ref[...].astype(jnp.float32)).astype(out_ref.dtype)


def final_sum(own, got):
    return pl.pallas_call(
        sum_kernel,
        out_shape=jax.ShapeDtypeStruct(own.shape, jnp.bfloat16),
        in_specs=[VMEM, VMEM],
        out_specs=VMEM,
        compiler_params=pltpu.CompilerParams(vmem_limit_bytes=2 * MIB),
    )(own, got)


def swapped(x, k):
    return lax.ppermute(x, "exp", [(i, i ^ k) for i in range(SOURCES)])


def fetched(x, first, second):
    pairs = []
    for side, k in enumerate((first, second)):
        if k is not None:
            pairs += [(2 * i + side, 2 * (i ^ k) + side) for i in range(SOURCES)]
    return lax.ppermute(x, ("exp", "hid"), pairs)


def swap_cores(x):
    return lax.ppermute(x, "hid", [(0, 1), (1, 0)])


def local(tokens, w_gate, w_up, w_down, block_counts, block_rows, row_gates):
    per_expert = SOURCES // block_rows.shape[0]
    tokens, place = pass_on(tokens)
    half = SOURCES // 2
    pieces = [fetched(tokens, ORDER[b], ORDER[half + b]) for b in range(1, half)]
    pieces += [fetched(tokens, None, ORDER[half])]
    mine = pack(place, tokens, pieces)
    x, act = gate_rows(place, mine, swap_cores(mine), w_gate)
    hidden = hidden_rows(x, act, w_up)
    send = down_half(place, hidden, w_down, True, jnp.bfloat16)
    keep = down_half(place, hidden, w_down, False, jnp.float32)
    parts = near(place, keep, swap_cores(send), per_expert)
    lines = [[i + per_expert * e for e in range(SOURCES // per_expert)] for i in range(per_expert)]
    returned = lax.all_to_all(
        parts, "exp", split_axis=0, concat_axis=0, tiled=True, axis_index_groups=lines
    )
    gates = route(block_counts, block_rows, row_gates, tokens.shape[0])
    own, other = weigh(gates, returned)
    return final_sum(own, swapped(other, 1))


def expert_block(segment, w_gate, w_up, w_down):
    gate_act = jnp.dot(segment, w_gate, preferred_element_type=jnp.float32)
    up_act = jnp.dot(segment, w_up, preferred_element_type=jnp.float32)
    hidden = (jax.nn.silu(gate_act) * up_act).astype(jnp.bfloat16)
    return jnp.dot(hidden, w_down, preferred_element_type=jnp.float32).astype(jnp.bfloat16)


def local_wide(tokens, w_gate, w_up, w_down, block_counts, block_rows, row_gates):
    sources = lax.axis_size("exp")
    own_index = lax.axis_index("exp")
    token_count = tokens.shape[0]
    model_width = tokens.shape[1]
    experts = block_rows.shape[0]
    slot_count = block_rows.shape[1]
    per_expert = sources // experts
    my_expert = own_index // per_expert
    position = jnp.arange(slot_count, dtype=jnp.int32)
    is_live = (position[None, :] < block_counts[:, None] * BLOCK) & (block_rows >= 0)
    source = jnp.where(is_live, block_rows // token_count, sources)
    matches = (source[:, :, None] == jnp.arange(sources, dtype=jnp.int32)[None, None, :]).astype(
        jnp.int32
    )
    order_rank = jnp.sum(jnp.cumsum(matches, axis=1) * matches, axis=2) - 1
    is_mine = is_live & (source == own_index)
    slot_target = jnp.where(
        is_mine, jnp.arange(experts, dtype=jnp.int32)[:, None] * CAP + order_rank, experts * CAP
    )
    local_values = jnp.where(is_mine, block_rows - own_index * token_count, token_count)
    local_row = (
        jnp.full((experts * CAP + 1,), token_count, jnp.int32)
        .at[slot_target.ravel()]
        .set(local_values.ravel())[: experts * CAP]
    )
    gate_mine = (
        jnp.zeros((experts * CAP + 1,), jnp.float32)
        .at[slot_target.ravel()]
        .set(jnp.where(is_mine, row_gates, 0.0).ravel())[: experts * CAP]
    )
    live_mine = lax.dynamic_index_in_dim(is_live, my_expert, 0, keepdims=False)
    rows_mine = lax.dynamic_index_in_dim(block_rows, my_expert, 0, keepdims=False)
    source_mine = lax.dynamic_index_in_dim(source, my_expert, 0, keepdims=False)
    rank_mine = lax.dynamic_index_in_dim(order_rank, my_expert, 0, keepdims=False)
    back_index = jnp.where(live_mine, source_mine * CAP + rank_mine, sources * CAP)
    blank_row = jnp.zeros((1, model_width), jnp.bfloat16)
    everyone = lax.all_gather(tokens, "exp", axis=0, tiled=True)
    row_pool = jnp.concatenate([everyone, blank_row], axis=0)
    routed = row_pool[jnp.where(live_mine, rows_mine, sources * token_count)]
    partial_rows = expert_block(routed, w_gate, w_up, w_down)
    outbound = (
        jnp.zeros((sources * CAP + 1, model_width), jnp.bfloat16).at[back_index].set(partial_rows)
    )
    outbound = outbound[: sources * CAP].reshape(sources, CAP, model_width)
    returned = lax.all_to_all(outbound, "exp", split_axis=0, concat_axis=0, tiled=True)
    summed = jnp.sum(
        returned.reshape(experts, per_expert, CAP, model_width), axis=1, dtype=jnp.float32
    )
    weighted = (summed * gate_mine.reshape(experts, CAP, 1)).reshape(experts * CAP, model_width)
    selector = (local_row[:, None] == jnp.arange(token_count, dtype=jnp.int32)[None, :]).astype(
        jnp.float32
    )
    gathered_sum = jnp.einsum("st,sd->td", selector, weighted, precision=lax.Precision.HIGHEST)
    share = lax.psum_scatter(gathered_sum, "hid", scatter_dimension=1, tiled=True)
    return share.astype(jnp.bfloat16)


def solution(mesh):
    small = mesh.shape["exp"] == SOURCES and mesh.shape["hid"] == 2

    def chosen(*args):
        return (local if small and args[5].shape[0] * 2 == SOURCES else local_wide)(*args)

    return jax.shard_map(
        chosen,
        mesh=mesh,
        in_specs=(
            P(("grp", "exp"), None),
            P(None, ("exp", "hid")),
            P(None, ("exp", "hid")),
            P(("exp", "hid"), None),
            P("grp"),
            P("grp", None),
            P("grp", None),
        ),
        out_specs=P(("grp", "exp"), "hid"),
        check_vma=False,
    )
```

```python
import functools

import jax
import jax.numpy as jnp
from jax import lax
from jax.experimental import pallas as pl
from jax.experimental.pallas import tpu as pltpu
from jax.sharding import PartitionSpec as P

BLOCK = 128
CAP = 3
TILE = 512
MIB = 1 << 20
ORDER = (0, 7, 6, 1, 2, 5, 4, 3)
SOURCES = len(ORDER)
GATE = 5_000_000_000
UP = 2_000_000_000
AHEAD = 20_000_000_000
HBM = pl.BlockSpec(memory_space=pltpu.HBM)
VMEM = pl.BlockSpec(memory_space=pltpu.VMEM)
SMEM = pl.BlockSpec(memory_space=pltpu.SMEM)


def in_hbm(x):
    return pltpu.with_memory_space_constraint(x, pltpu.HBM)


def in_smem(x):
    return pltpu.with_memory_space_constraint(x, pltpu.SMEM)


def in_vmem(x):
    return pltpu.with_memory_space_constraint(x, pltpu.VMEM)


def pass_kernel(tokens_ref, counts_ref, out_ref, counts_out, place_ref, sems):
    copy = pltpu.make_async_copy(tokens_ref, out_ref, sems.at[0])
    copy.start()
    small = pltpu.make_async_copy(counts_ref, counts_out, sems.at[1])
    small.start()
    place_ref[0] = lax.axis_index("hid")
    place_ref[1] = lax.axis_index("exp")
    copy.wait()
    small.wait()


def pass_on(tokens, counts):
    return pl.pallas_call(
        pass_kernel,
        out_shape=(
            jax.ShapeDtypeStruct(tokens.shape, tokens.dtype),
            pltpu.SMEM(counts.shape, counts.dtype),
            pltpu.SMEM((2,), jnp.int32),
        ),
        in_specs=[HBM, HBM],
        out_specs=(VMEM, SMEM, SMEM),
        scratch_shapes=[pltpu.SemaphoreType.DMA((2,))],
        compiler_params=pltpu.CompilerParams(vmem_limit_bytes=2 * MIB),
        cost_estimate=pl.CostEstimate(flops=AHEAD, bytes_accessed=0, transcendentals=0),
    )(in_hbm(tokens), in_hbm(counts))


def routed_gates(own, per_expert, count, counts_ref, rows_ref, gates_ref):
    experts, slots = rows_ref.shape
    expert = own // per_expert
    mine = lax.broadcasted_iota(jnp.int32, (experts, slots), 0) == expert
    rows = jnp.sum(jnp.where(mine, rows_ref[...], 0), axis=0, keepdims=True)
    gates = jnp.sum(jnp.where(mine, gates_ref[...], 0.0), axis=0, keepdims=True)
    position = lax.broadcasted_iota(jnp.int32, (1, slots), 1)
    rows = jnp.where(position < counts_ref[expert] * BLOCK, rows, -1)
    line = lax.broadcasted_iota(jnp.int32, (SOURCES * count, slots), 0)
    block = line // count
    source = jnp.zeros_like(line)
    for at, k in enumerate(ORDER):
        source = jnp.where(block == at, own ^ k, source)
    token = source * count + lax.rem(line, count)
    return jnp.sum(jnp.where(rows == token, gates, 0.0), axis=1, keepdims=True)


def pack_kernel(place_ref, tokens_ref, last_ref, *refs):
    *pieces, out_ref = refs
    for r, ref in enumerate(pieces[::-1]):
        out_ref[r + 1] = ref[...]
    out_ref[0] = jnp.where(place_ref[0] == 0, tokens_ref[...], last_ref[...])


def pack(place, tokens, pieces):
    return pl.pallas_call(
        pack_kernel,
        out_shape=jax.ShapeDtypeStruct((len(pieces), *tokens.shape), tokens.dtype),
        in_specs=[SMEM] + [VMEM] * (1 + len(pieces)),
        out_specs=VMEM,
        compiler_params=pltpu.CompilerParams(vmem_limit_bytes=2 * MIB),
    )(in_smem(place), tokens, *pieces)


def gate_kernel(
    per_expert, place_ref, counts_ref, mine_ref, got_ref, rows_ref, gates_ref, wg_ref, x_ref, act_ref, g_ref, wide
):
    sets, count, _ = mine_ref.shape
    g = routed_gates(place_ref[1], per_expert, count, counts_ref, rows_ref, gates_ref)
    g_ref[...] = jnp.broadcast_to(g, g_ref.shape)
    for j in range(sets):
        rows = pl.ds(j * count, count)
        wide[place_ref[0], rows, :] = mine_ref[j].astype(jnp.float32)
        wide[1 - place_ref[0], rows, :] = got_ref[j].astype(jnp.float32)
    x_ref[...] = wide[...].reshape(x_ref.shape).astype(jnp.bfloat16)

    for n in range(wg_ref.shape[1] // TILE):
        cols = pl.ds(n * TILE, TILE)
        gate = jnp.dot(x_ref[...], wg_ref[:, cols], preferred_element_type=jnp.float32)
        act_ref[:, cols] = gate / (1.0 + jnp.exp(-gate))


def gate_rows(place, counts, mine, got, block_rows, row_gates, wg):
    total = 2 * mine.shape[0] * mine.shape[1]
    depth, width = wg.shape
    return pl.pallas_call(
        functools.partial(gate_kernel, SOURCES // block_rows.shape[0]),
        out_shape=(
            jax.ShapeDtypeStruct((total, depth), jnp.bfloat16),
            jax.ShapeDtypeStruct((total, width), jnp.float32),
            jax.ShapeDtypeStruct((total, 128), jnp.float32),
        ),
        in_specs=[SMEM] * 2 + [VMEM] * 5,
        out_specs=(VMEM,) * 3,
        scratch_shapes=[pltpu.VMEM((2, total // 2, depth), jnp.float32)],
        compiler_params=pltpu.CompilerParams(vmem_limit_bytes=2 * MIB),
        cost_estimate=pl.CostEstimate(flops=GATE, bytes_accessed=0, transcendentals=total * width),
    )(in_smem(place), in_smem(counts), mine, got, block_rows, row_gates, in_vmem(wg))


def up_kernel(x_ref, act_ref, wu_ref, h_out):
    for n in range(wu_ref.shape[1] // TILE):
        cols = pl.ds(n * TILE, TILE)
        up = jnp.dot(x_ref[...], wu_ref[:, cols], preferred_element_type=jnp.float32)
        h_out[:, cols] = (act_ref[:, cols] * up).astype(jnp.bfloat16)


def hidden_rows(x, act, wu):
    return pl.pallas_call(
        up_kernel,
        out_shape=jax.ShapeDtypeStruct(act.shape, jnp.bfloat16),
        in_specs=[VMEM] * 3,
        out_specs=VMEM,
        compiler_params=pltpu.CompilerParams(vmem_limit_bytes=2 * MIB),
        cost_estimate=pl.CostEstimate(flops=UP, bytes_accessed=0, transcendentals=0),
    )(x, act, in_vmem(wu))


def down_kernel(other, place_ref, h_ref, wd_ref, out_ref):
    half = wd_ref.shape[1] // 2
    side = place_ref[0]
    base = (1 - side if other else side) * half
    for n in range(half // TILE):
        cols = pl.ds(pl.multiple_of(base + n * TILE, TILE), TILE)
        part = jnp.dot(h_ref[...], wd_ref[:, cols], preferred_element_type=jnp.float32)
        out_ref[:, pl.ds(n * TILE, TILE)] = part.astype(out_ref.dtype)


def down_half(place, hidden, wd, other, dtype):
    rows, depth = hidden.shape
    half = wd.shape[1] // 2
    return pl.pallas_call(
        functools.partial(down_kernel, other),
        out_shape=jax.ShapeDtypeStruct((rows, half), dtype),
        in_specs=[SMEM, VMEM, VMEM],
        out_specs=VMEM,
        compiler_params=pltpu.CompilerParams(vmem_limit_bytes=2 * MIB),
        cost_estimate=pl.CostEstimate(flops=2 * rows * depth * half, bytes_accessed=0, transcendentals=0),
    )(in_smem(place), hidden, in_vmem(wd))


def near_kernel(g_ref, keep_ref, got_ref, own_ref, *out_refs):
    both = (keep_ref[...] + got_ref[...].astype(jnp.float32)) * g_ref[:, :1]
    pair, count, _ = own_ref.shape
    group = SOURCES // pair
    for at, k in enumerate(ORDER):
        out_ref = (own_ref, *out_refs)[k % group]
        out_ref[k // group] = both[at * count : (at + 1) * count].astype(out_ref.dtype)


def near(g, keep, got):
    rows, width = keep.shape
    group = SOURCES // 2
    shape = (2, rows // SOURCES, width)
    return pl.pallas_call(
        near_kernel,
        out_shape=(jax.ShapeDtypeStruct(shape, jnp.float32),)
        + (jax.ShapeDtypeStruct(shape, jnp.bfloat16),) * (group - 1),
        in_specs=[VMEM] * 3,
        out_specs=(VMEM,) * group,
        compiler_params=pltpu.CompilerParams(vmem_limit_bytes=2 * MIB),
    )(g, keep, got)


def far_kernel(*refs):
    *part_refs, own_ref, next_ref = refs
    for i, out_ref in enumerate((own_ref, next_ref)):
        total = part_refs[0][i]
        for part_ref in part_refs[1:]:
            total = total + part_ref[i].astype(jnp.float32)
        out_ref[...] = total.astype(out_ref.dtype)


def far(parts):
    shape = parts[0].shape[1:]
    return pl.pallas_call(
        far_kernel,
        out_shape=(jax.ShapeDtypeStruct(shape, jnp.float32), jax.ShapeDtypeStruct(shape, jnp.bfloat16)),
        in_specs=[VMEM] * len(parts),
        out_specs=(VMEM, VMEM),
        compiler_params=pltpu.CompilerParams(vmem_limit_bytes=2 * MIB),
    )(*parts)


def sum_kernel(own_ref, got_ref, out_ref):
    out_ref[...] = (own_ref[...] + got_ref[...].astype(jnp.float32)).astype(out_ref.dtype)


def final_sum(own, got):
    return pl.pallas_call(
        sum_kernel,
        out_shape=jax.ShapeDtypeStruct(own.shape, jnp.bfloat16),
        in_specs=[VMEM, VMEM],
        out_specs=VMEM,
        compiler_params=pltpu.CompilerParams(vmem_limit_bytes=2 * MIB),
    )(own, got)


def swapped(x, k):
    return lax.ppermute(x, "exp", [(i, i ^ k) for i in range(SOURCES)])


def fetched(x, first, second):
    pairs = []
    for side, k in enumerate((first, second)):
        if k is not None:
            pairs += [(2 * i + side, 2 * (i ^ k) + side) for i in range(SOURCES)]
    return lax.ppermute(x, ("exp", "hid"), pairs)


def swap_cores(x):
    return lax.ppermute(x, "hid", [(0, 1), (1, 0)])


def local(tokens, w_gate, w_up, w_down, block_counts, block_rows, row_gates):
    tokens, counts, place = pass_on(tokens, block_counts)
    half = SOURCES // 2
    pieces = [fetched(tokens, ORDER[b], ORDER[half + b]) for b in range(1, half)]
    pieces += [fetched(tokens, None, ORDER[half])]
    mine = pack(place, tokens, pieces[::-1])
    x, act, g = gate_rows(place, counts, mine, swap_cores(mine), block_rows, row_gates, w_gate)
    hidden = hidden_rows(x, act, w_up)
    send = down_half(place, hidden, w_down, True, jnp.bfloat16)
    keep = down_half(place, hidden, w_down, False, jnp.float32)
    own, *parts = near(g, keep, swap_cores(send))
    returned = [swapped(parts[j - 1], j) for j in range(half - 1, 0, -1)]
    own, other = far([own, *returned])
    return final_sum(own, swapped(other, half))


def expert_block(segment, w_gate, w_up, w_down):
    gate_act = jnp.dot(segment, w_gate, preferred_element_type=jnp.float32)
    up_act = jnp.dot(segment, w_up, preferred_element_type=jnp.float32)
    hidden = (jax.nn.silu(gate_act) * up_act).astype(jnp.bfloat16)
    return jnp.dot(hidden, w_down, preferred_element_type=jnp.float32).astype(jnp.bfloat16)


def local_wide(tokens, w_gate, w_up, w_down, block_counts, block_rows, row_gates):
    sources = lax.axis_size("exp")
    own_index = lax.axis_index("exp")
    token_count = tokens.shape[0]
    model_width = tokens.shape[1]
    experts = block_rows.shape[0]
    slot_count = block_rows.shape[1]
    per_expert = sources // experts
    my_expert = own_index // per_expert
    position = jnp.arange(slot_count, dtype=jnp.int32)
    is_live = (position[None, :] < block_counts[:, None] * BLOCK) & (block_rows >= 0)
    source = jnp.where(is_live, block_rows // token_count, sources)
    matches = (source[:, :, None] == jnp.arange(sources, dtype=jnp.int32)[None, None, :]).astype(
        jnp.int32
    )
    order_rank = jnp.sum(jnp.cumsum(matches, axis=1) * matches, axis=2) - 1
    is_mine = is_live & (source == own_index)
    slot_target = jnp.where(
        is_mine, jnp.arange(experts, dtype=jnp.int32)[:, None] * CAP + order_rank, experts * CAP
    )
    local_values = jnp.where(is_mine, block_rows - own_index * token_count, token_count)
    local_row = (
        jnp.full((experts * CAP + 1,), token_count, jnp.int32)
        .at[slot_target.ravel()]
        .set(local_values.ravel())[: experts * CAP]
    )
    gate_mine = (
        jnp.zeros((experts * CAP + 1,), jnp.float32)
        .at[slot_target.ravel()]
        .set(jnp.where(is_mine, row_gates, 0.0).ravel())[: experts * CAP]
    )
    live_mine = lax.dynamic_index_in_dim(is_live, my_expert, 0, keepdims=False)
    rows_mine = lax.dynamic_index_in_dim(block_rows, my_expert, 0, keepdims=False)
    source_mine = lax.dynamic_index_in_dim(source, my_expert, 0, keepdims=False)
    rank_mine = lax.dynamic_index_in_dim(order_rank, my_expert, 0, keepdims=False)
    back_index = jnp.where(live_mine, source_mine * CAP + rank_mine, sources * CAP)
    blank_row = jnp.zeros((1, model_width), jnp.bfloat16)
    everyone = lax.all_gather(tokens, "exp", axis=0, tiled=True)
    row_pool = jnp.concatenate([everyone, blank_row], axis=0)
    routed = row_pool[jnp.where(live_mine, rows_mine, sources * token_count)]
    partial_rows = expert_block(routed, w_gate, w_up, w_down)
    outbound = (
        jnp.zeros((sources * CAP + 1, model_width), jnp.bfloat16).at[back_index].set(partial_rows)
    )
    outbound = outbound[: sources * CAP].reshape(sources, CAP, model_width)
    returned = lax.all_to_all(outbound, "exp", split_axis=0, concat_axis=0, tiled=True)
    summed = jnp.sum(
        returned.reshape(experts, per_expert, CAP, model_width), axis=1, dtype=jnp.float32
    )
    weighted = (summed * gate_mine.reshape(experts, CAP, 1)).reshape(experts * CAP, model_width)
    selector = (local_row[:, None] == jnp.arange(token_count, dtype=jnp.int32)[None, :]).astype(
        jnp.float32
    )
    gathered_sum = jnp.einsum("st,sd->td", selector, weighted, precision=lax.Precision.HIGHEST)
    share = lax.psum_scatter(gathered_sum, "hid", scatter_dimension=1, tiled=True)
    return share.astype(jnp.bfloat16)


def solution(mesh):
    small = mesh.shape["exp"] == SOURCES and mesh.shape["hid"] == 2

    def chosen(*args):
        return (local if small and args[5].shape[0] * 2 == SOURCES else local_wide)(*args)

    return jax.shard_map(
        chosen,
        mesh=mesh,
        in_specs=(
            P(("grp", "exp"), None),
            P(None, ("exp", "hid")),
            P(None, ("exp", "hid")),
            P(("exp", "hid"), None),
            P("grp"),
            P("grp", None),
            P("grp", None),
        ),
        out_specs=P(("grp", "exp"), "hid"),
        check_vma=False,
    )
```

```python
import functools

import jax
import jax.numpy as jnp
from jax import lax
from jax.experimental import pallas as pl
from jax.experimental.pallas import tpu as pltpu
from jax.sharding import PartitionSpec as P

BLOCK = 128
CAP = 3
TILE = 512
MIB = 1 << 20
ORDER = (0, 7, 6, 1, 2, 5, 4, 3)
SOURCES = len(ORDER)
GATE = 5_000_000_000
UP = 2_000_000_000
AHEAD = 20_000_000_000
HBM = pl.BlockSpec(memory_space=pltpu.HBM)
VMEM = pl.BlockSpec(memory_space=pltpu.VMEM)
SMEM = pl.BlockSpec(memory_space=pltpu.SMEM)


def in_hbm(x):
    return pltpu.with_memory_space_constraint(x, pltpu.HBM)


def in_smem(x):
    return pltpu.with_memory_space_constraint(x, pltpu.SMEM)


def in_vmem(x):
    return pltpu.with_memory_space_constraint(x, pltpu.VMEM)


def first_kernel(place_ref):
    place_ref[0] = lax.axis_index("hid")
    place_ref[1] = lax.axis_index("exp")


def first():
    return pl.pallas_call(
        first_kernel,
        out_shape=pltpu.SMEM((2,), jnp.int32),
        out_specs=SMEM,
        compiler_params=pltpu.CompilerParams(vmem_limit_bytes=2 * MIB),
        cost_estimate=pl.CostEstimate(flops=AHEAD, bytes_accessed=0, transcendentals=0),
    )()


def routed_gates(own, per_expert, count, counts_ref, rows_ref, gates_ref):
    experts, slots = rows_ref.shape
    expert = own // per_expert
    mine = lax.broadcasted_iota(jnp.int32, (experts, slots), 0) == expert
    rows = jnp.sum(jnp.where(mine, rows_ref[...], 0), axis=0, keepdims=True)
    gates = jnp.sum(jnp.where(mine, gates_ref[...], 0.0), axis=0, keepdims=True)
    position = lax.broadcasted_iota(jnp.int32, (1, slots), 1)
    here = lax.broadcasted_iota(jnp.int32, counts_ref.shape, 1) == expert
    blocks = jnp.sum(jnp.where(here, counts_ref[...], 0), axis=1, keepdims=True)
    rows = jnp.where(position < blocks * BLOCK, rows, -1)
    line = lax.broadcasted_iota(jnp.int32, (SOURCES * count, slots), 0)
    block = line // count
    source = jnp.zeros_like(line)
    for at, k in enumerate(ORDER):
        source = jnp.where(block == at, own ^ k, source)
    token = source * count + lax.rem(line, count)
    return jnp.sum(jnp.where(rows == token, gates, 0.0), axis=1, keepdims=True)


def pack_kernel(place_ref, tokens_ref, last_ref, *refs):
    *pieces, out_ref = refs
    for r, ref in enumerate(pieces[::-1]):
        out_ref[r + 1] = ref[...]
    out_ref[0] = jnp.where(place_ref[0] == 0, tokens_ref[...], last_ref[...])


def pack(place, tokens, pieces):
    return pl.pallas_call(
        pack_kernel,
        out_shape=jax.ShapeDtypeStruct((len(pieces), *tokens.shape), tokens.dtype),
        in_specs=[SMEM] + [VMEM] * (1 + len(pieces)),
        out_specs=VMEM,
        compiler_params=pltpu.CompilerParams(vmem_limit_bytes=2 * MIB),
    )(in_smem(place), tokens, *pieces)


def gate_kernel(
    per_expert, place_ref, counts_ref, mine_ref, got_ref, rows_ref, gates_ref, wg_ref, x_ref, act_ref, g_ref, wide
):
    sets, count, _ = mine_ref.shape
    g = routed_gates(place_ref[1], per_expert, count, counts_ref, rows_ref, gates_ref)
    g_ref[...] = jnp.broadcast_to(g, g_ref.shape)
    for j in range(sets):
        rows = pl.ds(j * count, count)
        wide[place_ref[0], rows, :] = mine_ref[j].astype(jnp.float32)
        wide[1 - place_ref[0], rows, :] = got_ref[j].astype(jnp.float32)
    x_ref[...] = wide[...].reshape(x_ref.shape).astype(jnp.bfloat16)

    for n in range(wg_ref.shape[1] // TILE):
        cols = pl.ds(n * TILE, TILE)
        gate = jnp.dot(x_ref[...], wg_ref[:, cols], preferred_element_type=jnp.float32)
        act_ref[:, cols] = gate / (1.0 + jnp.exp(-gate))


def gate_rows(place, counts, mine, got, block_rows, row_gates, wg):
    total = 2 * mine.shape[0] * mine.shape[1]
    depth, width = wg.shape
    return pl.pallas_call(
        functools.partial(gate_kernel, SOURCES // block_rows.shape[0]),
        out_shape=(
            jax.ShapeDtypeStruct((total, depth), jnp.bfloat16),
            jax.ShapeDtypeStruct((total, width), jnp.float32),
            jax.ShapeDtypeStruct((total, 128), jnp.float32),
        ),
        in_specs=[SMEM] + [VMEM] * 6,
        out_specs=(VMEM,) * 3,
        scratch_shapes=[pltpu.VMEM((2, total // 2, depth), jnp.float32)],
        compiler_params=pltpu.CompilerParams(vmem_limit_bytes=2 * MIB),
        cost_estimate=pl.CostEstimate(flops=GATE, bytes_accessed=0, transcendentals=total * width),
    )(in_smem(place), counts.reshape(1, -1), mine, got, block_rows, row_gates, in_vmem(wg))


def up_kernel(x_ref, act_ref, wu_ref, h_out):
    for n in range(wu_ref.shape[1] // TILE):
        cols = pl.ds(n * TILE, TILE)
        up = jnp.dot(x_ref[...], wu_ref[:, cols], preferred_element_type=jnp.float32)
        h_out[:, cols] = (act_ref[:, cols] * up).astype(jnp.bfloat16)


def hidden_rows(x, act, wu):
    return pl.pallas_call(
        up_kernel,
        out_shape=jax.ShapeDtypeStruct(act.shape, jnp.bfloat16),
        in_specs=[VMEM] * 3,
        out_specs=VMEM,
        compiler_params=pltpu.CompilerParams(vmem_limit_bytes=2 * MIB),
        cost_estimate=pl.CostEstimate(flops=UP, bytes_accessed=0, transcendentals=0),
    )(x, act, in_vmem(wu))


def down_kernel(other, place_ref, h_ref, wd_ref, out_ref):
    half = wd_ref.shape[1] // 2
    side = place_ref[0]
    base = (1 - side if other else side) * half
    for n in range(half // TILE):
        cols = pl.ds(pl.multiple_of(base + n * TILE, TILE), TILE)
        part = jnp.dot(h_ref[...], wd_ref[:, cols], preferred_element_type=jnp.float32)
        out_ref[:, pl.ds(n * TILE, TILE)] = part.astype(out_ref.dtype)


def down_half(place, hidden, wd, other, dtype):
    rows, depth = hidden.shape
    half = wd.shape[1] // 2
    return pl.pallas_call(
        functools.partial(down_kernel, other),
        out_shape=jax.ShapeDtypeStruct((rows, half), dtype),
        in_specs=[SMEM, VMEM, VMEM],
        out_specs=VMEM,
        compiler_params=pltpu.CompilerParams(vmem_limit_bytes=2 * MIB),
        cost_estimate=pl.CostEstimate(flops=2 * rows * depth * half, bytes_accessed=0, transcendentals=0),
    )(in_smem(place), hidden, in_vmem(wd))


def near_kernel(g_ref, keep_ref, got_ref, own_ref, *out_refs):
    both = (keep_ref[...] + got_ref[...].astype(jnp.float32)) * g_ref[:, :1]
    pair, count, _ = own_ref.shape
    group = SOURCES // pair
    for at, k in enumerate(ORDER):
        out_ref = (own_ref, *out_refs)[k % group]
        out_ref[k // group] = both[at * count : (at + 1) * count].astype(out_ref.dtype)


def near(g, keep, got):
    rows, width = keep.shape
    group = SOURCES // 2
    shape = (2, rows // SOURCES, width)
    return pl.pallas_call(
        near_kernel,
        out_shape=(jax.ShapeDtypeStruct(shape, jnp.float32),)
        + (jax.ShapeDtypeStruct(shape, jnp.bfloat16),) * (group - 1),
        in_specs=[VMEM] * 3,
        out_specs=(VMEM,) * group,
        compiler_params=pltpu.CompilerParams(vmem_limit_bytes=2 * MIB),
    )(g, keep, got)


def far_kernel(*refs):
    *part_refs, own_ref, next_ref = refs
    for i, out_ref in enumerate((own_ref, next_ref)):
        total = part_refs[0][i]
        for part_ref in part_refs[1:]:
            total = total + part_ref[i].astype(jnp.float32)
        out_ref[...] = total.astype(out_ref.dtype)


def far(parts):
    shape = parts[0].shape[1:]
    return pl.pallas_call(
        far_kernel,
        out_shape=(jax.ShapeDtypeStruct(shape, jnp.float32), jax.ShapeDtypeStruct(shape, jnp.bfloat16)),
        in_specs=[VMEM] * len(parts),
        out_specs=(VMEM, VMEM),
        compiler_params=pltpu.CompilerParams(vmem_limit_bytes=2 * MIB),
    )(*parts)


def sum_kernel(own_ref, got_ref, out_ref):
    out_ref[...] = (own_ref[...] + got_ref[...].astype(jnp.float32)).astype(out_ref.dtype)


def final_sum(own, got):
    return pl.pallas_call(
        sum_kernel,
        out_shape=jax.ShapeDtypeStruct(own.shape, jnp.bfloat16),
        in_specs=[VMEM, VMEM],
        out_specs=VMEM,
        compiler_params=pltpu.CompilerParams(vmem_limit_bytes=2 * MIB),
    )(own, got)


def swapped(x, k):
    return lax.ppermute(x, "exp", [(i, i ^ k) for i in range(SOURCES)])


def fetched(x, first, second):
    pairs = []
    for side, k in enumerate((first, second)):
        if k is not None:
            pairs += [(2 * i + 1 - side, 2 * (i ^ k) + side) for i in range(SOURCES)]
    return lax.ppermute(x, ("exp", "hid"), pairs)


def swap_cores(x):
    return lax.ppermute(x, "hid", [(0, 1), (1, 0)])


def local(tokens, w_gate, w_up, w_down, block_counts, block_rows, row_gates):
    place = first()
    tokens, place, counts = lax.optimization_barrier((tokens, place, block_counts))
    half = SOURCES // 2
    pieces = [fetched(tokens, ORDER[b], ORDER[half + b]) for b in range(1, half)]
    pieces += [fetched(tokens, None, ORDER[half])]
    mine = pack(place, tokens, pieces[::-1])
    x, act, g = gate_rows(place, counts, mine, swap_cores(mine), block_rows, row_gates, w_gate)
    hidden = hidden_rows(x, act, w_up)
    send = down_half(place, hidden, w_down, True, jnp.bfloat16)
    keep = down_half(place, hidden, w_down, False, jnp.float32)
    own, *parts = near(g, keep, swap_cores(send))
    returned = [swapped(parts[j - 1], j) for j in range(half - 1, 0, -1)]
    own, other = far([own, *returned])
    return final_sum(own, swapped(other, half))


def expert_block(segment, w_gate, w_up, w_down):
    gate_act = jnp.dot(segment, w_gate, preferred_element_type=jnp.float32)
    up_act = jnp.dot(segment, w_up, preferred_element_type=jnp.float32)
    hidden = (jax.nn.silu(gate_act) * up_act).astype(jnp.bfloat16)
    return jnp.dot(hidden, w_down, preferred_element_type=jnp.float32).astype(jnp.bfloat16)


def local_wide(tokens, w_gate, w_up, w_down, block_counts, block_rows, row_gates):
    sources = lax.axis_size("exp")
    own_index = lax.axis_index("exp")
    token_count = tokens.shape[0]
    model_width = tokens.shape[1]
    experts = block_rows.shape[0]
    slot_count = block_rows.shape[1]
    per_expert = sources // experts
    my_expert = own_index // per_expert
    position = jnp.arange(slot_count, dtype=jnp.int32)
    is_live = (position[None, :] < block_counts[:, None] * BLOCK) & (block_rows >= 0)
    source = jnp.where(is_live, block_rows // token_count, sources)
    matches = (source[:, :, None] == jnp.arange(sources, dtype=jnp.int32)[None, None, :]).astype(
        jnp.int32
    )
    order_rank = jnp.sum(jnp.cumsum(matches, axis=1) * matches, axis=2) - 1
    is_mine = is_live & (source == own_index)
    slot_target = jnp.where(
        is_mine, jnp.arange(experts, dtype=jnp.int32)[:, None] * CAP + order_rank, experts * CAP
    )
    local_values = jnp.where(is_mine, block_rows - own_index * token_count, token_count)
    local_row = (
        jnp.full((experts * CAP + 1,), token_count, jnp.int32)
        .at[slot_target.ravel()]
        .set(local_values.ravel())[: experts * CAP]
    )
    gate_mine = (
        jnp.zeros((experts * CAP + 1,), jnp.float32)
        .at[slot_target.ravel()]
        .set(jnp.where(is_mine, row_gates, 0.0).ravel())[: experts * CAP]
    )
    live_mine = lax.dynamic_index_in_dim(is_live, my_expert, 0, keepdims=False)
    rows_mine = lax.dynamic_index_in_dim(block_rows, my_expert, 0, keepdims=False)
    source_mine = lax.dynamic_index_in_dim(source, my_expert, 0, keepdims=False)
    rank_mine = lax.dynamic_index_in_dim(order_rank, my_expert, 0, keepdims=False)
    back_index = jnp.where(live_mine, source_mine * CAP + rank_mine, sources * CAP)
    blank_row = jnp.zeros((1, model_width), jnp.bfloat16)
    everyone = lax.all_gather(tokens, "exp", axis=0, tiled=True)
    row_pool = jnp.concatenate([everyone, blank_row], axis=0)
    routed = row_pool[jnp.where(live_mine, rows_mine, sources * token_count)]
    partial_rows = expert_block(routed, w_gate, w_up, w_down)
    outbound = (
        jnp.zeros((sources * CAP + 1, model_width), jnp.bfloat16).at[back_index].set(partial_rows)
    )
    outbound = outbound[: sources * CAP].reshape(sources, CAP, model_width)
    returned = lax.all_to_all(outbound, "exp", split_axis=0, concat_axis=0, tiled=True)
    summed = jnp.sum(
        returned.reshape(experts, per_expert, CAP, model_width), axis=1, dtype=jnp.float32
    )
    weighted = (summed * gate_mine.reshape(experts, CAP, 1)).reshape(experts * CAP, model_width)
    selector = (local_row[:, None] == jnp.arange(token_count, dtype=jnp.int32)[None, :]).astype(
        jnp.float32
    )
    gathered_sum = jnp.einsum("st,sd->td", selector, weighted, precision=lax.Precision.HIGHEST)
    share = lax.psum_scatter(gathered_sum, "hid", scatter_dimension=1, tiled=True)
    return share.astype(jnp.bfloat16)


def solution(mesh):
    small = mesh.shape["exp"] == SOURCES and mesh.shape["hid"] == 2

    def chosen(*args):
        return (local if small and args[5].shape[0] * 2 == SOURCES else local_wide)(*args)

    return jax.shard_map(
        chosen,
        mesh=mesh,
        in_specs=(
            P(("grp", "exp"), None),
            P(None, ("exp", "hid")),
            P(None, ("exp", "hid")),
            P(("exp", "hid"), None),
            P("grp"),
            P("grp", None),
            P("grp", None),
        ),
        out_specs=P(("grp", "exp"), "hid"),
        check_vma=False,
    )
```

```python
import functools

import jax
import jax.numpy as jnp
from jax import lax
from jax.experimental import pallas as pl
from jax.experimental.pallas import tpu as pltpu
from jax.sharding import PartitionSpec as P

BLOCK = 128
CAP = 3
TILE = 512
MIB = 1 << 20
ORDER = (0, 1, 6, 7, 2, 3, 4, 5)
SOURCES = len(ORDER)
GATE = 5_000_000_000
UP = 2_000_000_000
AHEAD = 20_000_000_000
HBM = pl.BlockSpec(memory_space=pltpu.HBM)
VMEM = pl.BlockSpec(memory_space=pltpu.VMEM)
SMEM = pl.BlockSpec(memory_space=pltpu.SMEM)


def in_hbm(x):
    return pltpu.with_memory_space_constraint(x, pltpu.HBM)


def in_smem(x):
    return pltpu.with_memory_space_constraint(x, pltpu.SMEM)


def in_vmem(x):
    return pltpu.with_memory_space_constraint(x, pltpu.VMEM)


def first_kernel(place_ref):
    place_ref[0] = lax.axis_index("hid")
    place_ref[1] = lax.axis_index("exp")


def first():
    return pl.pallas_call(
        first_kernel,
        out_shape=pltpu.SMEM((2,), jnp.int32),
        out_specs=SMEM,
        compiler_params=pltpu.CompilerParams(vmem_limit_bytes=2 * MIB),
        cost_estimate=pl.CostEstimate(flops=AHEAD, bytes_accessed=0, transcendentals=0),
    )()


def routed_gates(own, per_expert, count, counts_ref, rows_ref, gates_ref):
    experts, slots = rows_ref.shape
    expert = own // per_expert
    mine = lax.broadcasted_iota(jnp.int32, (experts, slots), 0) == expert
    rows = jnp.sum(jnp.where(mine, rows_ref[...], 0), axis=0, keepdims=True)
    gates = jnp.sum(jnp.where(mine, gates_ref[...], 0.0), axis=0, keepdims=True)
    position = lax.broadcasted_iota(jnp.int32, (1, slots), 1)
    here = lax.broadcasted_iota(jnp.int32, counts_ref.shape, 1) == expert
    blocks = jnp.sum(jnp.where(here, counts_ref[...], 0), axis=1, keepdims=True)
    rows = jnp.where(position < blocks * BLOCK, rows, -1)
    line = lax.broadcasted_iota(jnp.int32, (SOURCES * count, slots), 0)
    block = line // count
    source = jnp.zeros_like(line)
    for at, k in enumerate(ORDER):
        source = jnp.where(block == at, own ^ k, source)
    token = source * count + lax.rem(line, count)
    return jnp.sum(jnp.where(rows == token, gates, 0.0), axis=1, keepdims=True)


def stack_kernel(*refs):
    for at, ref in enumerate(refs[:-1]):
        refs[-1][at] = ref[...]


def stack(pieces):
    return pl.pallas_call(
        stack_kernel,
        out_shape=jax.ShapeDtypeStruct((len(pieces), *pieces[0].shape), pieces[0].dtype),
        in_specs=[VMEM] * len(pieces),
        out_specs=VMEM,
        compiler_params=pltpu.CompilerParams(vmem_limit_bytes=2 * MIB),
    )(*pieces)


def gate_kernel(
    per_expert,
    place_ref,
    counts_ref,
    tokens_ref,
    mine_ref,
    got_ref,
    rows_ref,
    gates_ref,
    wg_ref,
    x_ref,
    act_ref,
    g_ref,
    wide,
):
    sets, count, _ = mine_ref.shape
    g = routed_gates(place_ref[1], per_expert, count, counts_ref, rows_ref, gates_ref)
    g_ref[...] = jnp.broadcast_to(g, g_ref.shape)
    for j in range(sets):
        rows = pl.ds(j * count, count)
        wide[place_ref[0], rows, :] = mine_ref[j].astype(jnp.float32)
        wide[1 - place_ref[0], rows, :] = got_ref[j].astype(jnp.float32)
    wide[0, pl.ds(0, count), :] = tokens_ref[...].astype(jnp.float32)
    x_ref[...] = wide[...].reshape(x_ref.shape).astype(jnp.bfloat16)

    for n in range(wg_ref.shape[1] // TILE):
        cols = pl.ds(n * TILE, TILE)
        gate = jnp.dot(x_ref[...], wg_ref[:, cols], preferred_element_type=jnp.float32)
        act_ref[:, cols] = gate / (1.0 + jnp.exp(-gate))


def gate_rows(place, counts, tokens, mine, got, block_rows, row_gates, wg):
    total = 2 * mine.shape[0] * mine.shape[1]
    depth, width = wg.shape
    return pl.pallas_call(
        functools.partial(gate_kernel, SOURCES // block_rows.shape[0]),
        out_shape=(
            jax.ShapeDtypeStruct((total, depth), jnp.bfloat16),
            jax.ShapeDtypeStruct((total, width), jnp.float32),
            jax.ShapeDtypeStruct((total, 128), jnp.float32),
        ),
        in_specs=[SMEM] + [VMEM] * 7,
        out_specs=(VMEM,) * 3,
        scratch_shapes=[pltpu.VMEM((2, total // 2, depth), jnp.float32)],
        compiler_params=pltpu.CompilerParams(vmem_limit_bytes=2 * MIB),
        cost_estimate=pl.CostEstimate(flops=GATE, bytes_accessed=0, transcendentals=total * width),
    )(in_smem(place), counts.reshape(1, -1), tokens, mine, got, block_rows, row_gates, in_vmem(wg))


def up_kernel(x_ref, act_ref, wu_ref, h_out):
    for n in range(wu_ref.shape[1] // TILE):
        cols = pl.ds(n * TILE, TILE)
        up = jnp.dot(x_ref[...], wu_ref[:, cols], preferred_element_type=jnp.float32)
        h_out[:, cols] = (act_ref[:, cols] * up).astype(jnp.bfloat16)


def hidden_rows(x, act, wu):
    return pl.pallas_call(
        up_kernel,
        out_shape=jax.ShapeDtypeStruct(act.shape, jnp.bfloat16),
        in_specs=[VMEM] * 3,
        out_specs=VMEM,
        compiler_params=pltpu.CompilerParams(vmem_limit_bytes=2 * MIB),
        cost_estimate=pl.CostEstimate(flops=UP, bytes_accessed=0, transcendentals=0),
    )(x, act, in_vmem(wu))


def down_kernel(other, place_ref, h_ref, wd_ref, out_ref):
    half = wd_ref.shape[1] // 2
    side = place_ref[0]
    base = (1 - side if other else side) * half
    for n in range(half // TILE):
        cols = pl.ds(pl.multiple_of(base + n * TILE, TILE), TILE)
        part = jnp.dot(h_ref[...], wd_ref[:, cols], preferred_element_type=jnp.float32)
        out_ref[:, pl.ds(n * TILE, TILE)] = part.astype(out_ref.dtype)


def down_half(place, hidden, wd, other, dtype):
    rows, depth = hidden.shape
    half = wd.shape[1] // 2
    return pl.pallas_call(
        functools.partial(down_kernel, other),
        out_shape=jax.ShapeDtypeStruct((rows, half), dtype),
        in_specs=[SMEM, VMEM, VMEM],
        out_specs=VMEM,
        compiler_params=pltpu.CompilerParams(vmem_limit_bytes=2 * MIB),
        cost_estimate=pl.CostEstimate(flops=2 * rows * depth * half, bytes_accessed=0, transcendentals=0),
    )(in_smem(place), hidden, in_vmem(wd))


def near_kernel(g_ref, keep_ref, got_ref, even_ref, odd_ref):
    both = (keep_ref[...] + got_ref[...].astype(jnp.float32)) * g_ref[:, :1]
    _, count, _ = odd_ref.shape
    for at, k in enumerate(ORDER):
        out_ref = (even_ref, odd_ref)[k % 2]
        out_ref[k // 2] = both[at * count : (at + 1) * count].astype(out_ref.dtype)


def near(g, keep, got):
    rows, width = keep.shape
    shape = (SOURCES // 2, rows // SOURCES, width)
    return pl.pallas_call(
        near_kernel,
        out_shape=(jax.ShapeDtypeStruct(shape, jnp.float32), jax.ShapeDtypeStruct(shape, jnp.bfloat16)),
        in_specs=[VMEM] * 3,
        out_specs=(VMEM, VMEM),
        compiler_params=pltpu.CompilerParams(vmem_limit_bytes=2 * MIB),
    )(g, keep, got)


def far_kernel(even_ref, got_ref, *out_refs):
    for j, out_ref in enumerate(out_refs):
        out_ref[...] = (even_ref[j] + got_ref[j].astype(jnp.float32)).astype(out_ref.dtype)


def far(even, got):
    sets, count, width = even.shape
    return pl.pallas_call(
        far_kernel,
        out_shape=(jax.ShapeDtypeStruct((count, width), jnp.float32),)
        + (jax.ShapeDtypeStruct((count, width), jnp.bfloat16),) * (sets - 1),
        in_specs=[VMEM, VMEM],
        out_specs=(VMEM,) * sets,
        compiler_params=pltpu.CompilerParams(vmem_limit_bytes=2 * MIB),
    )(even, got)


def sum_kernel(own_ref, *refs):
    total = own_ref[...]
    for ref in refs[:-1]:
        total = total + ref[...].astype(jnp.float32)
    refs[-1][...] = total.astype(jnp.bfloat16)


def final_sum(own, got):
    return pl.pallas_call(
        sum_kernel,
        out_shape=jax.ShapeDtypeStruct(own.shape, jnp.bfloat16),
        in_specs=[VMEM] * (1 + len(got)),
        out_specs=VMEM,
        compiler_params=pltpu.CompilerParams(vmem_limit_bytes=2 * MIB),
    )(own, *got)


def swapped(x, k):
    return lax.ppermute(x, "exp", [(i, i ^ k) for i in range(SOURCES)])


def fetched(x, first, second):
    pairs = []
    for side, k in enumerate((first, second)):
        if k is not None:
            pairs += [(2 * i + side, 2 * (i ^ k) + side) for i in range(SOURCES)]
    return lax.ppermute(x, ("exp", "hid"), pairs)


def swap_cores(x):
    return lax.ppermute(x, "hid", [(0, 1), (1, 0)])


def local(tokens, w_gate, w_up, w_down, block_counts, block_rows, row_gates):
    place = first()
    tokens, place, counts = lax.optimization_barrier((tokens, place, block_counts))
    half = SOURCES // 2
    pieces = [fetched(tokens, None, ORDER[half])]
    pieces += [fetched(tokens, ORDER[b], ORDER[half + b]) for b in range(1, half)]
    mine = stack(pieces)
    got = swap_cores(mine)
    x, act, g = gate_rows(place, counts, tokens, mine, got, block_rows, row_gates, w_gate)
    hidden = hidden_rows(x, act, w_up)
    send = down_half(place, hidden, w_down, True, jnp.bfloat16)
    keep = down_half(place, hidden, w_down, False, jnp.float32)
    even, odd = near(g, keep, swap_cores(send))
    own, *parts = far(even, swapped(odd, 1))
    return final_sum(own, [swapped(parts[j - 1], 2 * j) for j in range(half - 1, 0, -1)])


def expert_block(segment, w_gate, w_up, w_down):
    gate_act = jnp.dot(segment, w_gate, preferred_element_type=jnp.float32)
    up_act = jnp.dot(segment, w_up, preferred_element_type=jnp.float32)
    hidden = (jax.nn.silu(gate_act) * up_act).astype(jnp.bfloat16)
    return jnp.dot(hidden, w_down, preferred_element_type=jnp.float32).astype(jnp.bfloat16)


def local_wide(tokens, w_gate, w_up, w_down, block_counts, block_rows, row_gates):
    sources = lax.axis_size("exp")
    own_index = lax.axis_index("exp")
    token_count = tokens.shape[0]
    model_width = tokens.shape[1]
    experts = block_rows.shape[0]
    slot_count = block_rows.shape[1]
    per_expert = sources // experts
    my_expert = own_index // per_expert
    position = jnp.arange(slot_count, dtype=jnp.int32)
    is_live = (position[None, :] < block_counts[:, None] * BLOCK) & (block_rows >= 0)
    source = jnp.where(is_live, block_rows // token_count, sources)
    matches = (source[:, :, None] == jnp.arange(sources, dtype=jnp.int32)[None, None, :]).astype(
        jnp.int32
    )
    order_rank = jnp.sum(jnp.cumsum(matches, axis=1) * matches, axis=2) - 1
    is_mine = is_live & (source == own_index)
    slot_target = jnp.where(
        is_mine, jnp.arange(experts, dtype=jnp.int32)[:, None] * CAP + order_rank, experts * CAP
    )
    local_values = jnp.where(is_mine, block_rows - own_index * token_count, token_count)
    local_row = (
        jnp.full((experts * CAP + 1,), token_count, jnp.int32)
        .at[slot_target.ravel()]
        .set(local_values.ravel())[: experts * CAP]
    )
    gate_mine = (
        jnp.zeros((experts * CAP + 1,), jnp.float32)
        .at[slot_target.ravel()]
        .set(jnp.where(is_mine, row_gates, 0.0).ravel())[: experts * CAP]
    )
    live_mine = lax.dynamic_index_in_dim(is_live, my_expert, 0, keepdims=False)
    rows_mine = lax.dynamic_index_in_dim(block_rows, my_expert, 0, keepdims=False)
    source_mine = lax.dynamic_index_in_dim(source, my_expert, 0, keepdims=False)
    rank_mine = lax.dynamic_index_in_dim(order_rank, my_expert, 0, keepdims=False)
    back_index = jnp.where(live_mine, source_mine * CAP + rank_mine, sources * CAP)
    blank_row = jnp.zeros((1, model_width), jnp.bfloat16)
    everyone = lax.all_gather(tokens, "exp", axis=0, tiled=True)
    row_pool = jnp.concatenate([everyone, blank_row], axis=0)
    routed = row_pool[jnp.where(live_mine, rows_mine, sources * token_count)]
    partial_rows = expert_block(routed, w_gate, w_up, w_down)
    outbound = (
        jnp.zeros((sources * CAP + 1, model_width), jnp.bfloat16).at[back_index].set(partial_rows)
    )
    outbound = outbound[: sources * CAP].reshape(sources, CAP, model_width)
    returned = lax.all_to_all(outbound, "exp", split_axis=0, concat_axis=0, tiled=True)
    summed = jnp.sum(
        returned.reshape(experts, per_expert, CAP, model_width), axis=1, dtype=jnp.float32
    )
    weighted = (summed * gate_mine.reshape(experts, CAP, 1)).reshape(experts * CAP, model_width)
    selector = (local_row[:, None] == jnp.arange(token_count, dtype=jnp.int32)[None, :]).astype(
        jnp.float32
    )
    gathered_sum = jnp.einsum("st,sd->td", selector, weighted, precision=lax.Precision.HIGHEST)
    share = lax.psum_scatter(gathered_sum, "hid", scatter_dimension=1, tiled=True)
    return share.astype(jnp.bfloat16)


def solution(mesh):
    small = mesh.shape["exp"] == SOURCES and mesh.shape["hid"] == 2

    def chosen(*args):
        return (local if small and args[5].shape[0] * 2 == SOURCES else local_wide)(*args)

    return jax.shard_map(
        chosen,
        mesh=mesh,
        in_specs=(
            P(("grp", "exp"), None),
            P(None, ("exp", "hid")),
            P(None, ("exp", "hid")),
            P(("exp", "hid"), None),
            P("grp"),
            P("grp", None),
            P("grp", None),
        ),
        out_specs=P(("grp", "exp"), "hid"),
        check_vma=False,
    )
```

```python
import functools

import jax
import jax.numpy as jnp
from jax import lax
from jax.experimental import pallas as pl
from jax.experimental.pallas import tpu as pltpu
from jax.sharding import PartitionSpec as P

BLOCK = 128
CAP = 3
TILE = 512
MIB = 1 << 20
ORDER = (0, 1, 6, 7, 2, 3, 4, 5)
SOURCES = len(ORDER)
GATE = 5_000_000_000
UP = 2_000_000_000
AHEAD = 20_000_000_000
HBM = pl.BlockSpec(memory_space=pltpu.HBM)
VMEM = pl.BlockSpec(memory_space=pltpu.VMEM)
SMEM = pl.BlockSpec(memory_space=pltpu.SMEM)


def in_hbm(x):
    return pltpu.with_memory_space_constraint(x, pltpu.HBM)


def in_smem(x):
    return pltpu.with_memory_space_constraint(x, pltpu.SMEM)


def in_vmem(x):
    return pltpu.with_memory_space_constraint(x, pltpu.VMEM)


def first_kernel(place_ref):
    place_ref[0] = lax.axis_index("hid")
    place_ref[1] = lax.axis_index("exp")


def first():
    return pl.pallas_call(
        first_kernel,
        out_shape=pltpu.SMEM((2,), jnp.int32),
        out_specs=SMEM,
        compiler_params=pltpu.CompilerParams(vmem_limit_bytes=2 * MIB),
        cost_estimate=pl.CostEstimate(flops=AHEAD, bytes_accessed=0, transcendentals=0),
    )()


def routed_gates(own, per_expert, count, counts_ref, rows_ref, gates_ref):
    experts, slots = rows_ref.shape
    expert = own // per_expert
    mine = lax.broadcasted_iota(jnp.int32, (experts, slots), 0) == expert
    rows = jnp.sum(jnp.where(mine, rows_ref[...], 0), axis=0, keepdims=True)
    gates = jnp.sum(jnp.where(mine, gates_ref[...], 0.0), axis=0, keepdims=True)
    position = lax.broadcasted_iota(jnp.int32, (1, slots), 1)
    here = lax.broadcasted_iota(jnp.int32, counts_ref.shape, 1) == expert
    blocks = jnp.sum(jnp.where(here, counts_ref[...], 0), axis=1, keepdims=True)
    rows = jnp.where(position < blocks * BLOCK, rows, -1)
    line = lax.broadcasted_iota(jnp.int32, (SOURCES * count, slots), 0)
    block = line // count
    source = jnp.zeros_like(line)
    for at, k in enumerate(ORDER):
        source = jnp.where(block == at, own ^ k, source)
    token = source * count + lax.rem(line, count)
    return jnp.sum(jnp.where(rows == token, gates, 0.0), axis=1, keepdims=True)


def stack_kernel(*refs):
    for at, ref in enumerate(refs[:-1]):
        refs[-1][at] = ref[...]


def stack(pieces):
    return pl.pallas_call(
        stack_kernel,
        out_shape=jax.ShapeDtypeStruct((len(pieces), *pieces[0].shape), pieces[0].dtype),
        in_specs=[VMEM] * len(pieces),
        out_specs=VMEM,
        compiler_params=pltpu.CompilerParams(vmem_limit_bytes=2 * MIB),
    )(*pieces)


def gate_kernel(
    per_expert,
    place_ref,
    counts_ref,
    tokens_ref,
    mine_ref,
    got_ref,
    rows_ref,
    gates_ref,
    wg_ref,
    x_ref,
    act_ref,
    g_ref,
    wide,
):
    sets, count, _ = mine_ref.shape
    g = routed_gates(place_ref[1], per_expert, count, counts_ref, rows_ref, gates_ref)
    g_ref[...] = jnp.broadcast_to(g, g_ref.shape)
    for j in range(sets):
        rows = pl.ds(j * count, count)
        wide[place_ref[0], rows, :] = mine_ref[j].astype(jnp.float32)
        wide[1 - place_ref[0], rows, :] = got_ref[j].astype(jnp.float32)
    wide[0, pl.ds(0, count), :] = tokens_ref[...].astype(jnp.float32)
    x_ref[...] = wide[...].reshape(x_ref.shape).astype(jnp.bfloat16)

    for n in range(wg_ref.shape[1] // TILE):
        cols = pl.ds(n * TILE, TILE)
        gate = jnp.dot(x_ref[...], wg_ref[:, cols], preferred_element_type=jnp.float32)
        act_ref[:, cols] = gate / (1.0 + jnp.exp(-gate))


def gate_rows(place, counts, tokens, mine, got, block_rows, row_gates, wg):
    total = 2 * mine.shape[0] * mine.shape[1]
    depth, width = wg.shape
    return pl.pallas_call(
        functools.partial(gate_kernel, SOURCES // block_rows.shape[0]),
        out_shape=(
            jax.ShapeDtypeStruct((total, depth), jnp.bfloat16),
            jax.ShapeDtypeStruct((total, width), jnp.float32),
            jax.ShapeDtypeStruct((total, 128), jnp.float32),
        ),
        in_specs=[SMEM] + [VMEM] * 7,
        out_specs=(VMEM,) * 3,
        scratch_shapes=[pltpu.VMEM((2, total // 2, depth), jnp.float32)],
        compiler_params=pltpu.CompilerParams(vmem_limit_bytes=2 * MIB),
        cost_estimate=pl.CostEstimate(flops=GATE, bytes_accessed=0, transcendentals=total * width),
    )(in_smem(place), counts.reshape(1, -1), tokens, mine, got, block_rows, row_gates, in_vmem(wg))


def up_kernel(x_ref, act_ref, wu_ref, h_out):
    for n in range(wu_ref.shape[1] // TILE):
        cols = pl.ds(n * TILE, TILE)
        up = jnp.dot(x_ref[...], wu_ref[:, cols], preferred_element_type=jnp.float32)
        h_out[:, cols] = (act_ref[:, cols] * up).astype(jnp.bfloat16)


def hidden_rows(x, act, wu):
    return pl.pallas_call(
        up_kernel,
        out_shape=jax.ShapeDtypeStruct(act.shape, jnp.bfloat16),
        in_specs=[VMEM] * 3,
        out_specs=VMEM,
        compiler_params=pltpu.CompilerParams(vmem_limit_bytes=2 * MIB),
        cost_estimate=pl.CostEstimate(flops=UP, bytes_accessed=0, transcendentals=0),
    )(x, act, in_vmem(wu))


def down_kernel(other, place_ref, h_ref, wd_ref, out_ref):
    half = wd_ref.shape[1] // 2
    side = place_ref[0]
    base = (1 - side if other else side) * half
    for n in range(half // TILE):
        cols = pl.ds(pl.multiple_of(base + n * TILE, TILE), TILE)
        part = jnp.dot(h_ref[...], wd_ref[:, cols], preferred_element_type=jnp.float32)
        out_ref[:, pl.ds(n * TILE, TILE)] = part.astype(out_ref.dtype)


def down_half(place, hidden, wd, other, dtype):
    rows, depth = hidden.shape
    half = wd.shape[1] // 2
    return pl.pallas_call(
        functools.partial(down_kernel, other),
        out_shape=jax.ShapeDtypeStruct((rows, half), dtype),
        in_specs=[SMEM, VMEM, VMEM],
        out_specs=VMEM,
        compiler_params=pltpu.CompilerParams(vmem_limit_bytes=2 * MIB),
        cost_estimate=pl.CostEstimate(flops=2 * rows * depth * half, bytes_accessed=0, transcendentals=0),
    )(in_smem(place), hidden, in_vmem(wd))


def near_kernel(g_ref, keep_ref, got_ref, own_ref, *out_refs):
    both = (keep_ref[...] + got_ref[...].astype(jnp.float32)) * g_ref[:, :1]
    pair, count, _ = own_ref.shape
    group = SOURCES // pair
    for at, k in enumerate(ORDER):
        out_ref = (own_ref, *out_refs)[k % group]
        out_ref[k // group] = both[at * count : (at + 1) * count].astype(out_ref.dtype)


def near(g, keep, got):
    rows, width = keep.shape
    group = SOURCES // 2
    shape = (2, rows // SOURCES, width)
    return pl.pallas_call(
        near_kernel,
        out_shape=(jax.ShapeDtypeStruct(shape, jnp.float32),)
        + (jax.ShapeDtypeStruct(shape, jnp.bfloat16),) * (group - 1),
        in_specs=[VMEM] * 3,
        out_specs=(VMEM,) * group,
        compiler_params=pltpu.CompilerParams(vmem_limit_bytes=2 * MIB),
    )(g, keep, got)


def far_kernel(*refs):
    *part_refs, own_ref, next_ref = refs
    for i, out_ref in enumerate((own_ref, next_ref)):
        total = part_refs[0][i]
        for part_ref in part_refs[1:]:
            total = total + part_ref[i].astype(jnp.float32)
        out_ref[...] = total.astype(out_ref.dtype)


def far(parts):
    shape = parts[0].shape[1:]
    return pl.pallas_call(
        far_kernel,
        out_shape=(jax.ShapeDtypeStruct(shape, jnp.float32), jax.ShapeDtypeStruct(shape, jnp.bfloat16)),
        in_specs=[VMEM] * len(parts),
        out_specs=(VMEM, VMEM),
        compiler_params=pltpu.CompilerParams(vmem_limit_bytes=2 * MIB),
    )(*parts)


def sum_kernel(own_ref, got_ref, out_ref):
    out_ref[...] = (own_ref[...] + got_ref[...].astype(jnp.float32)).astype(out_ref.dtype)


def final_sum(own, got):
    return pl.pallas_call(
        sum_kernel,
        out_shape=jax.ShapeDtypeStruct(own.shape, jnp.bfloat16),
        in_specs=[VMEM, VMEM],
        out_specs=VMEM,
        compiler_params=pltpu.CompilerParams(vmem_limit_bytes=2 * MIB),
    )(own, got)


def swapped(x, k):
    return lax.ppermute(x, "exp", [(i, i ^ k) for i in range(SOURCES)])


def fetched(x, first, second):
    return lax.ppermute(
        x,
        ("exp", "hid"),
        [(2 * i + 1 - side, 2 * (i ^ k) + side) for side, k in enumerate((first, second)) for i in range(SOURCES)],
    )


def fetched_by_one(x, k):
    return lax.ppermute(x, ("exp", "hid"), [(2 * i + 1, 2 * (i ^ k) + 1) for i in range(SOURCES)])


def swap_cores(x):
    return lax.ppermute(x, "hid", [(0, 1), (1, 0)])


def local(tokens, w_gate, w_up, w_down, block_counts, block_rows, row_gates):
    place = first()
    tokens, place, counts = lax.optimization_barrier((tokens, place, block_counts))
    half = SOURCES // 2
    pieces = [fetched_by_one(tokens, ORDER[half])]
    pieces += [fetched(tokens, ORDER[b], ORDER[half + b]) for b in range(1, half)]
    mine = stack(pieces)
    got = swap_cores(mine)
    x, act, g = gate_rows(place, counts, tokens, mine, got, block_rows, row_gates, w_gate)
    hidden = hidden_rows(x, act, w_up)
    send = down_half(place, hidden, w_down, True, jnp.bfloat16)
    keep = down_half(place, hidden, w_down, False, jnp.float32)
    own, *parts = near(g, keep, swap_cores(send))
    returned = [swapped(parts[j - 1], j) for j in range(half - 1, 0, -1)]
    own, other = far([own, *returned])
    return final_sum(own, swapped(other, half))


def expert_block(segment, w_gate, w_up, w_down):
    gate_act = jnp.dot(segment, w_gate, preferred_element_type=jnp.float32)
    up_act = jnp.dot(segment, w_up, preferred_element_type=jnp.float32)
    hidden = (jax.nn.silu(gate_act) * up_act).astype(jnp.bfloat16)
    return jnp.dot(hidden, w_down, preferred_element_type=jnp.float32).astype(jnp.bfloat16)


def local_wide(tokens, w_gate, w_up, w_down, block_counts, block_rows, row_gates):
    sources = lax.axis_size("exp")
    own_index = lax.axis_index("exp")
    token_count = tokens.shape[0]
    model_width = tokens.shape[1]
    experts = block_rows.shape[0]
    slot_count = block_rows.shape[1]
    per_expert = sources // experts
    my_expert = own_index // per_expert
    position = jnp.arange(slot_count, dtype=jnp.int32)
    is_live = (position[None, :] < block_counts[:, None] * BLOCK) & (block_rows >= 0)
    source = jnp.where(is_live, block_rows // token_count, sources)
    matches = (source[:, :, None] == jnp.arange(sources, dtype=jnp.int32)[None, None, :]).astype(
        jnp.int32
    )
    order_rank = jnp.sum(jnp.cumsum(matches, axis=1) * matches, axis=2) - 1
    is_mine = is_live & (source == own_index)
    slot_target = jnp.where(
        is_mine, jnp.arange(experts, dtype=jnp.int32)[:, None] * CAP + order_rank, experts * CAP
    )
    local_values = jnp.where(is_mine, block_rows - own_index * token_count, token_count)
    local_row = (
        jnp.full((experts * CAP + 1,), token_count, jnp.int32)
        .at[slot_target.ravel()]
        .set(local_values.ravel())[: experts * CAP]
    )
    gate_mine = (
        jnp.zeros((experts * CAP + 1,), jnp.float32)
        .at[slot_target.ravel()]
        .set(jnp.where(is_mine, row_gates, 0.0).ravel())[: experts * CAP]
    )
    live_mine = lax.dynamic_index_in_dim(is_live, my_expert, 0, keepdims=False)
    rows_mine = lax.dynamic_index_in_dim(block_rows, my_expert, 0, keepdims=False)
    source_mine = lax.dynamic_index_in_dim(source, my_expert, 0, keepdims=False)
    rank_mine = lax.dynamic_index_in_dim(order_rank, my_expert, 0, keepdims=False)
    back_index = jnp.where(live_mine, source_mine * CAP + rank_mine, sources * CAP)
    blank_row = jnp.zeros((1, model_width), jnp.bfloat16)
    everyone = lax.all_gather(tokens, "exp", axis=0, tiled=True)
    row_pool = jnp.concatenate([everyone, blank_row], axis=0)
    routed = row_pool[jnp.where(live_mine, rows_mine, sources * token_count)]
    partial_rows = expert_block(routed, w_gate, w_up, w_down)
    outbound = (
        jnp.zeros((sources * CAP + 1, model_width), jnp.bfloat16).at[back_index].set(partial_rows)
    )
    outbound = outbound[: sources * CAP].reshape(sources, CAP, model_width)
    returned = lax.all_to_all(outbound, "exp", split_axis=0, concat_axis=0, tiled=True)
    summed = jnp.sum(
        returned.reshape(experts, per_expert, CAP, model_width), axis=1, dtype=jnp.float32
    )
    weighted = (summed * gate_mine.reshape(experts, CAP, 1)).reshape(experts * CAP, model_width)
    selector = (local_row[:, None] == jnp.arange(token_count, dtype=jnp.int32)[None, :]).astype(
        jnp.float32
    )
    gathered_sum = jnp.einsum("st,sd->td", selector, weighted, precision=lax.Precision.HIGHEST)
    share = lax.psum_scatter(gathered_sum, "hid", scatter_dimension=1, tiled=True)
    return share.astype(jnp.bfloat16)


def solution(mesh):
    small = mesh.shape["exp"] == SOURCES and mesh.shape["hid"] == 2

    def chosen(*args):
        return (local if small and args[5].shape[0] * 2 == SOURCES else local_wide)(*args)

    return jax.shard_map(
        chosen,
        mesh=mesh,
        in_specs=(
            P(("grp", "exp"), None),
            P(None, ("exp", "hid")),
            P(None, ("exp", "hid")),
            P(("exp", "hid"), None),
            P("grp"),
            P("grp", None),
            P("grp", None),
        ),
        out_specs=P(("grp", "exp"), "hid"),
        check_vma=False,
    )
```

```python
import functools

import jax
import jax.numpy as jnp
from jax import lax
from jax.experimental import pallas as pl
from jax.experimental.pallas import tpu as pltpu
from jax.sharding import PartitionSpec as P

BLOCK = 128
CAP = 3
TILE = 512
MIB = 1 << 20
ORDER = (0, 1, 6, 7, 2, 3, 4, 5)
SOURCES = len(ORDER)
GATE = 5_000_000_000
UP = 2_000_000_000
AHEAD = 20_000_000_000
HBM = pl.BlockSpec(memory_space=pltpu.HBM)
VMEM = pl.BlockSpec(memory_space=pltpu.VMEM)
SMEM = pl.BlockSpec(memory_space=pltpu.SMEM)


def in_hbm(x):
    return pltpu.with_memory_space_constraint(x, pltpu.HBM)


def in_smem(x):
    return pltpu.with_memory_space_constraint(x, pltpu.SMEM)


def in_vmem(x):
    return pltpu.with_memory_space_constraint(x, pltpu.VMEM)


def first_kernel(place_ref):
    place_ref[0] = lax.axis_index("hid")
    place_ref[1] = lax.axis_index("exp")


def first():
    return pl.pallas_call(
        first_kernel,
        out_shape=pltpu.SMEM((2,), jnp.int32),
        out_specs=SMEM,
        compiler_params=pltpu.CompilerParams(vmem_limit_bytes=2 * MIB),
        cost_estimate=pl.CostEstimate(flops=AHEAD, bytes_accessed=0, transcendentals=0),
    )()


def routed_gates(own, per_expert, count, counts_ref, rows_ref, gates_ref):
    experts, slots = rows_ref.shape
    expert = own // per_expert
    mine = lax.broadcasted_iota(jnp.int32, (experts, slots), 0) == expert
    rows = jnp.sum(jnp.where(mine, rows_ref[...], 0), axis=0, keepdims=True)
    gates = jnp.sum(jnp.where(mine, gates_ref[...], 0.0), axis=0, keepdims=True)
    position = lax.broadcasted_iota(jnp.int32, (1, slots), 1)
    here = lax.broadcasted_iota(jnp.int32, counts_ref.shape, 1) == expert
    blocks = jnp.sum(jnp.where(here, counts_ref[...], 0), axis=1, keepdims=True)
    rows = jnp.where(position < blocks * BLOCK, rows, -1)
    line = lax.broadcasted_iota(jnp.int32, (SOURCES * count, slots), 0)
    block = line // count
    source = jnp.zeros_like(line)
    for at, k in enumerate(ORDER):
        source = jnp.where(block == at, own ^ k, source)
    token = source * count + lax.rem(line, count)
    return jnp.sum(jnp.where(rows == token, gates, 0.0), axis=1, keepdims=True)


def stack_kernel(*refs):
    for at, ref in enumerate(refs[:-1]):
        refs[-1][at] = ref[...]


def stack(pieces):
    return pl.pallas_call(
        stack_kernel,
        out_shape=jax.ShapeDtypeStruct((len(pieces), *pieces[0].shape), pieces[0].dtype),
        in_specs=[VMEM] * len(pieces),
        out_specs=VMEM,
        compiler_params=pltpu.CompilerParams(vmem_limit_bytes=2 * MIB),
    )(*pieces)


def gate_kernel(
    per_expert,
    place_ref,
    counts_ref,
    tokens_ref,
    mine_ref,
    got_ref,
    rows_ref,
    gates_ref,
    wg_ref,
    x_ref,
    act_ref,
    g_ref,
    wide,
):
    sets, count, _ = mine_ref.shape
    g = routed_gates(place_ref[1], per_expert, count, counts_ref, rows_ref, gates_ref)
    g_ref[...] = jnp.broadcast_to(g, g_ref.shape)
    for j in range(sets):
        rows = pl.ds(j * count, count)
        wide[place_ref[0], rows, :] = mine_ref[j].astype(jnp.float32)
        wide[1 - place_ref[0], rows, :] = got_ref[j].astype(jnp.float32)
    wide[0, pl.ds(0, count), :] = tokens_ref[...].astype(jnp.float32)
    x_ref[...] = wide[...].reshape(x_ref.shape).astype(jnp.bfloat16)

    for n in range(wg_ref.shape[1] // TILE):
        cols = pl.ds(n * TILE, TILE)
        gate = jnp.dot(x_ref[...], wg_ref[:, cols], preferred_element_type=jnp.float32)
        act_ref[:, cols] = gate / (1.0 + jnp.exp(-gate))


def gate_rows(place, counts, tokens, mine, got, block_rows, row_gates, wg):
    total = 2 * mine.shape[0] * mine.shape[1]
    depth, width = wg.shape
    return pl.pallas_call(
        functools.partial(gate_kernel, SOURCES // block_rows.shape[0]),
        out_shape=(
            jax.ShapeDtypeStruct((total, depth), jnp.bfloat16),
            jax.ShapeDtypeStruct((total, width), jnp.float32),
            jax.ShapeDtypeStruct((total, 128), jnp.float32),
        ),
        in_specs=[SMEM] + [VMEM] * 7,
        out_specs=(VMEM,) * 3,
        scratch_shapes=[pltpu.VMEM((2, total // 2, depth), jnp.float32)],
        compiler_params=pltpu.CompilerParams(vmem_limit_bytes=2 * MIB),
        cost_estimate=pl.CostEstimate(flops=GATE, bytes_accessed=0, transcendentals=total * width),
    )(in_smem(place), counts.reshape(1, -1), tokens, mine, got, block_rows, row_gates, in_vmem(wg))


def up_kernel(x_ref, act_ref, wu_ref, h_out):
    for n in range(wu_ref.shape[1] // TILE):
        cols = pl.ds(n * TILE, TILE)
        up = jnp.dot(x_ref[...], wu_ref[:, cols], preferred_element_type=jnp.float32)
        h_out[:, cols] = (act_ref[:, cols] * up).astype(jnp.bfloat16)


def hidden_rows(x, act, wu):
    return pl.pallas_call(
        up_kernel,
        out_shape=jax.ShapeDtypeStruct(act.shape, jnp.bfloat16),
        in_specs=[VMEM] * 3,
        out_specs=VMEM,
        compiler_params=pltpu.CompilerParams(vmem_limit_bytes=2 * MIB),
        cost_estimate=pl.CostEstimate(flops=UP, bytes_accessed=0, transcendentals=0),
    )(x, act, in_vmem(wu))


def down_kernel(other, place_ref, h_ref, wd_ref, out_ref):
    half = wd_ref.shape[1] // 2
    side = place_ref[0]
    base = (1 - side if other else side) * half
    for n in range(half // TILE):
        cols = pl.ds(pl.multiple_of(base + n * TILE, TILE), TILE)
        part = jnp.dot(h_ref[...], wd_ref[:, cols], preferred_element_type=jnp.float32)
        out_ref[:, pl.ds(n * TILE, TILE)] = part.astype(out_ref.dtype)


def down_half(place, hidden, wd, other, dtype):
    rows, depth = hidden.shape
    half = wd.shape[1] // 2
    return pl.pallas_call(
        functools.partial(down_kernel, other),
        out_shape=jax.ShapeDtypeStruct((rows, half), dtype),
        in_specs=[SMEM, VMEM, VMEM],
        out_specs=VMEM,
        compiler_params=pltpu.CompilerParams(vmem_limit_bytes=2 * MIB),
        cost_estimate=pl.CostEstimate(flops=2 * rows * depth * half, bytes_accessed=0, transcendentals=0),
    )(in_smem(place), hidden, in_vmem(wd))


def near_kernel(g_ref, keep_ref, got_ref, own_ref, *out_refs):
    both = (keep_ref[...] + got_ref[...].astype(jnp.float32)) * g_ref[:, :1]
    pair, count, _ = own_ref.shape
    group = SOURCES // pair
    for at, k in enumerate(ORDER):
        out_ref = (own_ref, *out_refs)[k % group]
        out_ref[k // group] = both[at * count : (at + 1) * count].astype(out_ref.dtype)


def near(g, keep, got):
    rows, width = keep.shape
    group = SOURCES // 2
    shape = (2, rows // SOURCES, width)
    return pl.pallas_call(
        near_kernel,
        out_shape=(jax.ShapeDtypeStruct(shape, jnp.float32),)
        + (jax.ShapeDtypeStruct(shape, jnp.bfloat16),) * (group - 1),
        in_specs=[VMEM] * 3,
        out_specs=(VMEM,) * group,
        compiler_params=pltpu.CompilerParams(vmem_limit_bytes=2 * MIB),
    )(g, keep, got)


def far_kernel(*refs):
    *part_refs, own_ref, next_ref = refs
    for i, out_ref in enumerate((own_ref, next_ref)):
        total = part_refs[0][i]
        for part_ref in part_refs[1:]:
            total = total + part_ref[i].astype(jnp.float32)
        out_ref[...] = total.astype(out_ref.dtype)


def far(parts):
    shape = parts[0].shape[1:]
    return pl.pallas_call(
        far_kernel,
        out_shape=(jax.ShapeDtypeStruct(shape, jnp.float32), jax.ShapeDtypeStruct(shape, jnp.bfloat16)),
        in_specs=[VMEM] * len(parts),
        out_specs=(VMEM, VMEM),
        compiler_params=pltpu.CompilerParams(vmem_limit_bytes=2 * MIB),
    )(*parts)


def sum_kernel(own_ref, got_ref, out_ref):
    out_ref[...] = (own_ref[...] + got_ref[...].astype(jnp.float32)).astype(out_ref.dtype)


def final_sum(own, got):
    return pl.pallas_call(
        sum_kernel,
        out_shape=jax.ShapeDtypeStruct(own.shape, jnp.bfloat16),
        in_specs=[VMEM, VMEM],
        out_specs=VMEM,
        compiler_params=pltpu.CompilerParams(vmem_limit_bytes=2 * MIB),
    )(own, got)


def swapped(x, k):
    return lax.ppermute(x, "exp", [(i, i ^ k) for i in range(SOURCES)])


def fetched(x, first, second):
    return lax.ppermute(
        x,
        ("exp", "hid"),
        [(2 * i + 1 - side, 2 * (i ^ k) + side) for side, k in enumerate((first, second)) for i in range(SOURCES)],
    )


def swap_cores(x):
    return lax.ppermute(x, "hid", [(0, 1), (1, 0)])


def local(tokens, w_gate, w_up, w_down, block_counts, block_rows, row_gates):
    place = first()
    tokens, place, counts = lax.optimization_barrier((tokens, place, block_counts))
    half = SOURCES // 2
    pieces = [fetched(tokens, ORDER[half], ORDER[half])]
    pieces += [fetched(tokens, ORDER[b], ORDER[half + b]) for b in range(1, half)]
    mine = stack(pieces)
    got = swap_cores(mine)
    x, act, g = gate_rows(place, counts, tokens, mine, got, block_rows, row_gates, w_gate)
    hidden = hidden_rows(x, act, w_up)
    send = down_half(place, hidden, w_down, True, jnp.bfloat16)
    keep = down_half(place, hidden, w_down, False, jnp.float32)
    own, *parts = near(g, keep, swap_cores(send))
    returned = [swapped(parts[j - 1], j) for j in range(half - 1, 0, -1)]
    own, other = far([own, *returned])
    return final_sum(own, swapped(other, half))


def expert_block(segment, w_gate, w_up, w_down):
    gate_act = jnp.dot(segment, w_gate, preferred_element_type=jnp.float32)
    up_act = jnp.dot(segment, w_up, preferred_element_type=jnp.float32)
    hidden = (jax.nn.silu(gate_act) * up_act).astype(jnp.bfloat16)
    return jnp.dot(hidden, w_down, preferred_element_type=jnp.float32).astype(jnp.bfloat16)


def local_wide(tokens, w_gate, w_up, w_down, block_counts, block_rows, row_gates):
    sources = lax.axis_size("exp")
    own_index = lax.axis_index("exp")
    token_count = tokens.shape[0]
    model_width = tokens.shape[1]
    experts = block_rows.shape[0]
    slot_count = block_rows.shape[1]
    per_expert = sources // experts
    my_expert = own_index // per_expert
    position = jnp.arange(slot_count, dtype=jnp.int32)
    is_live = (position[None, :] < block_counts[:, None] * BLOCK) & (block_rows >= 0)
    source = jnp.where(is_live, block_rows // token_count, sources)
    matches = (source[:, :, None] == jnp.arange(sources, dtype=jnp.int32)[None, None, :]).astype(
        jnp.int32
    )
    order_rank = jnp.sum(jnp.cumsum(matches, axis=1) * matches, axis=2) - 1
    is_mine = is_live & (source == own_index)
    slot_target = jnp.where(
        is_mine, jnp.arange(experts, dtype=jnp.int32)[:, None] * CAP + order_rank, experts * CAP
    )
    local_values = jnp.where(is_mine, block_rows - own_index * token_count, token_count)
    local_row = (
        jnp.full((experts * CAP + 1,), token_count, jnp.int32)
        .at[slot_target.ravel()]
        .set(local_values.ravel())[: experts * CAP]
    )
    gate_mine = (
        jnp.zeros((experts * CAP + 1,), jnp.float32)
        .at[slot_target.ravel()]
        .set(jnp.where(is_mine, row_gates, 0.0).ravel())[: experts * CAP]
    )
    live_mine = lax.dynamic_index_in_dim(is_live, my_expert, 0, keepdims=False)
    rows_mine = lax.dynamic_index_in_dim(block_rows, my_expert, 0, keepdims=False)
    source_mine = lax.dynamic_index_in_dim(source, my_expert, 0, keepdims=False)
    rank_mine = lax.dynamic_index_in_dim(order_rank, my_expert, 0, keepdims=False)
    back_index = jnp.where(live_mine, source_mine * CAP + rank_mine, sources * CAP)
    blank_row = jnp.zeros((1, model_width), jnp.bfloat16)
    everyone = lax.all_gather(tokens, "exp", axis=0, tiled=True)
    row_pool = jnp.concatenate([everyone, blank_row], axis=0)
    routed = row_pool[jnp.where(live_mine, rows_mine, sources * token_count)]
    partial_rows = expert_block(routed, w_gate, w_up, w_down)
    outbound = (
        jnp.zeros((sources * CAP + 1, model_width), jnp.bfloat16).at[back_index].set(partial_rows)
    )
    outbound = outbound[: sources * CAP].reshape(sources, CAP, model_width)
    returned = lax.all_to_all(outbound, "exp", split_axis=0, concat_axis=0, tiled=True)
    summed = jnp.sum(
        returned.reshape(experts, per_expert, CAP, model_width), axis=1, dtype=jnp.float32
    )
    weighted = (summed * gate_mine.reshape(experts, CAP, 1)).reshape(experts * CAP, model_width)
    selector = (local_row[:, None] == jnp.arange(token_count, dtype=jnp.int32)[None, :]).astype(
        jnp.float32
    )
    gathered_sum = jnp.einsum("st,sd->td", selector, weighted, precision=lax.Precision.HIGHEST)
    share = lax.psum_scatter(gathered_sum, "hid", scatter_dimension=1, tiled=True)
    return share.astype(jnp.bfloat16)


def solution(mesh):
    small = mesh.shape["exp"] == SOURCES and mesh.shape["hid"] == 2

    def chosen(*args):
        return (local if small and args[5].shape[0] * 2 == SOURCES else local_wide)(*args)

    return jax.shard_map(
        chosen,
        mesh=mesh,
        in_specs=(
            P(("grp", "exp"), None),
            P(None, ("exp", "hid")),
            P(None, ("exp", "hid")),
            P(("exp", "hid"), None),
            P("grp"),
            P("grp", None),
            P("grp", None),
        ),
        out_specs=P(("grp", "exp"), "hid"),
        check_vma=False,
    )
```

```python
import functools

import jax
import jax.numpy as jnp
from jax import lax
from jax.experimental import pallas as pl
from jax.experimental.pallas import tpu as pltpu
from jax.sharding import PartitionSpec as P

BLOCK = 128
CAP = 3
TILE = 512
MIB = 1 << 20
ORDER = (0, 1, 6, 7, 2, 3, 4, 5)
SOURCES = len(ORDER)
GATE = 5_000_000_000
UP = 2_000_000_000
AHEAD = 20_000_000_000
HBM = pl.BlockSpec(memory_space=pltpu.HBM)
VMEM = pl.BlockSpec(memory_space=pltpu.VMEM)
SMEM = pl.BlockSpec(memory_space=pltpu.SMEM)


def in_hbm(x):
    return pltpu.with_memory_space_constraint(x, pltpu.HBM)


def in_smem(x):
    return pltpu.with_memory_space_constraint(x, pltpu.SMEM)


def in_vmem(x):
    return pltpu.with_memory_space_constraint(x, pltpu.VMEM)


def turned(i):
    return (1 + i + i // 2) % 2


def first_kernel(place_ref):
    side, own = lax.axis_index("hid"), lax.axis_index("exp")
    place_ref[0] = side
    place_ref[1] = own
    place_ref[2] = turned(own)
    place_ref[3] = lax.rem(side + turned(own), 2)


def first():
    return pl.pallas_call(
        first_kernel,
        out_shape=pltpu.SMEM((4,), jnp.int32),
        out_specs=SMEM,
        compiler_params=pltpu.CompilerParams(vmem_limit_bytes=2 * MIB),
        cost_estimate=pl.CostEstimate(flops=AHEAD, bytes_accessed=0, transcendentals=0),
    )()


def routed_gates(own, per_expert, count, counts_ref, rows_ref, gates_ref):
    experts, slots = rows_ref.shape
    expert = own // per_expert
    mine = lax.broadcasted_iota(jnp.int32, (experts, slots), 0) == expert
    rows = jnp.sum(jnp.where(mine, rows_ref[...], 0), axis=0, keepdims=True)
    gates = jnp.sum(jnp.where(mine, gates_ref[...], 0.0), axis=0, keepdims=True)
    position = lax.broadcasted_iota(jnp.int32, (1, slots), 1)
    here = lax.broadcasted_iota(jnp.int32, counts_ref.shape, 1) == expert
    blocks = jnp.sum(jnp.where(here, counts_ref[...], 0), axis=1, keepdims=True)
    rows = jnp.where(position < blocks * BLOCK, rows, -1)
    line = lax.broadcasted_iota(jnp.int32, (SOURCES * count, slots), 0)
    block = line // count
    source = jnp.zeros_like(line)
    for at, k in enumerate(ORDER):
        source = jnp.where(block == at, own ^ k, source)
    token = source * count + lax.rem(line, count)
    return jnp.sum(jnp.where(rows == token, gates, 0.0), axis=1, keepdims=True)


def stack_kernel(*refs):
    for at, ref in enumerate(refs[:-1]):
        refs[-1][at] = ref[...]


def stack(pieces):
    return pl.pallas_call(
        stack_kernel,
        out_shape=jax.ShapeDtypeStruct((len(pieces), *pieces[0].shape), pieces[0].dtype),
        in_specs=[VMEM] * len(pieces),
        out_specs=VMEM,
        compiler_params=pltpu.CompilerParams(vmem_limit_bytes=2 * MIB),
    )(*pieces)


def gate_kernel(
    per_expert,
    place_ref,
    counts_ref,
    tokens_ref,
    mine_ref,
    got_ref,
    rows_ref,
    gates_ref,
    wg_ref,
    x_ref,
    act_ref,
    g_ref,
    wide,
):
    sets, count, _ = mine_ref.shape
    g = routed_gates(place_ref[1], per_expert, count, counts_ref, rows_ref, gates_ref)
    g_ref[...] = jnp.broadcast_to(g, g_ref.shape)
    for j in range(sets):
        rows = pl.ds(j * count, count)
        wide[place_ref[0], rows, :] = mine_ref[j].astype(jnp.float32)
        wide[1 - place_ref[0], rows, :] = got_ref[j].astype(jnp.float32)
    wide[0, pl.ds(0, count), :] = tokens_ref[...].astype(jnp.float32)
    x_ref[...] = wide[...].reshape(x_ref.shape).astype(jnp.bfloat16)

    for n in range(wg_ref.shape[1] // TILE):
        cols = pl.ds(n * TILE, TILE)
        gate = jnp.dot(x_ref[...], wg_ref[:, cols], preferred_element_type=jnp.float32)
        act_ref[:, cols] = gate / (1.0 + jnp.exp(-gate))


def gate_rows(place, counts, tokens, mine, got, block_rows, row_gates, wg):
    total = 2 * mine.shape[0] * mine.shape[1]
    depth, width = wg.shape
    return pl.pallas_call(
        functools.partial(gate_kernel, SOURCES // block_rows.shape[0]),
        out_shape=(
            jax.ShapeDtypeStruct((total, depth), jnp.bfloat16),
            jax.ShapeDtypeStruct((total, width), jnp.float32),
            jax.ShapeDtypeStruct((total, 128), jnp.float32),
        ),
        in_specs=[SMEM] + [VMEM] * 7,
        out_specs=(VMEM,) * 3,
        scratch_shapes=[pltpu.VMEM((2, total // 2, depth), jnp.float32)],
        compiler_params=pltpu.CompilerParams(vmem_limit_bytes=2 * MIB),
        cost_estimate=pl.CostEstimate(flops=GATE, bytes_accessed=0, transcendentals=total * width),
    )(in_smem(place), counts.reshape(1, -1), tokens, mine, got, block_rows, row_gates, in_vmem(wg))


def up_kernel(x_ref, act_ref, wu_ref, h_out):
    for n in range(wu_ref.shape[1] // TILE):
        cols = pl.ds(n * TILE, TILE)
        up = jnp.dot(x_ref[...], wu_ref[:, cols], preferred_element_type=jnp.float32)
        h_out[:, cols] = (act_ref[:, cols] * up).astype(jnp.bfloat16)


def hidden_rows(x, act, wu):
    return pl.pallas_call(
        up_kernel,
        out_shape=jax.ShapeDtypeStruct(act.shape, jnp.bfloat16),
        in_specs=[VMEM] * 3,
        out_specs=VMEM,
        compiler_params=pltpu.CompilerParams(vmem_limit_bytes=2 * MIB),
        cost_estimate=pl.CostEstimate(flops=UP, bytes_accessed=0, transcendentals=0),
    )(x, act, in_vmem(wu))


def down_kernel(other, place_ref, h_ref, wd_ref, out_ref):
    half = wd_ref.shape[1] // 2
    mine = place_ref[3]
    base = (1 - mine if other else mine) * half
    for n in range(half // TILE):
        cols = pl.ds(pl.multiple_of(base + n * TILE, TILE), TILE)
        part = jnp.dot(h_ref[...], wd_ref[:, cols], preferred_element_type=jnp.float32)
        out_ref[:, pl.ds(n * TILE, TILE)] = part.astype(out_ref.dtype)


def down_half(place, hidden, wd, other, dtype):
    rows, depth = hidden.shape
    half = wd.shape[1] // 2
    return pl.pallas_call(
        functools.partial(down_kernel, other),
        out_shape=jax.ShapeDtypeStruct((rows, half), dtype),
        in_specs=[SMEM, VMEM, VMEM],
        out_specs=VMEM,
        compiler_params=pltpu.CompilerParams(vmem_limit_bytes=2 * MIB),
        cost_estimate=pl.CostEstimate(flops=2 * rows * depth * half, bytes_accessed=0, transcendentals=0),
    )(in_smem(place), hidden, in_vmem(wd))


def near_kernel(g_ref, keep_ref, got_ref, own_ref, *out_refs):
    both = (keep_ref[...] + got_ref[...].astype(jnp.float32)) * g_ref[:, :1]
    pair, count, _ = own_ref.shape
    group = SOURCES // pair
    for at, k in enumerate(ORDER):
        out_ref = (own_ref, *out_refs)[k % group]
        out_ref[k // group] = both[at * count : (at + 1) * count].astype(out_ref.dtype)


def near(g, keep, got):
    rows, width = keep.shape
    group = SOURCES // 2
    shape = (2, rows // SOURCES, width)
    return pl.pallas_call(
        near_kernel,
        out_shape=(jax.ShapeDtypeStruct(shape, jnp.float32),)
        + (jax.ShapeDtypeStruct(shape, jnp.bfloat16),) * (group - 1),
        in_specs=[VMEM] * 3,
        out_specs=(VMEM,) * group,
        compiler_params=pltpu.CompilerParams(vmem_limit_bytes=2 * MIB),
    )(g, keep, got)


def far_kernel(*refs):
    *part_refs, own_ref, next_ref = refs
    for i, out_ref in enumerate((own_ref, next_ref)):
        total = part_refs[0][i]
        for part_ref in part_refs[1:]:
            total = total + part_ref[i].astype(jnp.float32)
        out_ref[...] = total.astype(out_ref.dtype)


def far(parts):
    shape = parts[0].shape[1:]
    return pl.pallas_call(
        far_kernel,
        out_shape=(jax.ShapeDtypeStruct(shape, jnp.float32), jax.ShapeDtypeStruct(shape, jnp.bfloat16)),
        in_specs=[VMEM] * len(parts),
        out_specs=(VMEM, VMEM),
        compiler_params=pltpu.CompilerParams(vmem_limit_bytes=2 * MIB),
    )(*parts)


def sum_kernel(place_ref, own_ref, got_ref, turned_ref, out_ref):
    own = jnp.where(place_ref[2] == 1, turned_ref[...], own_ref[...])
    out_ref[...] = (own + got_ref[...].astype(jnp.float32)).astype(out_ref.dtype)


def final_sum(place, own, got, other_core):
    return pl.pallas_call(
        sum_kernel,
        out_shape=jax.ShapeDtypeStruct(own.shape, jnp.bfloat16),
        in_specs=[SMEM] + [VMEM] * 3,
        out_specs=VMEM,
        compiler_params=pltpu.CompilerParams(vmem_limit_bytes=2 * MIB),
    )(in_smem(place), own, got, other_core)


def swapped(x, k):
    pairs = [
        (2 * i + side, 2 * (i ^ k) + (side + turned(i) + turned(i ^ k)) % 2) for i in range(SOURCES) for side in range(2)
    ]
    return lax.ppermute(x, ("exp", "hid"), pairs)


def sent_home(x, k):
    pairs = [(2 * i + side, 2 * (i ^ k) + (side + turned(i)) % 2) for i in range(SOURCES) for side in range(2)]
    return lax.ppermute(x, ("exp", "hid"), pairs)


def fetched(x, first, second):
    return lax.ppermute(
        x,
        ("exp", "hid"),
        [(2 * i + 1 - side, 2 * (i ^ k) + side) for side, k in enumerate((first, second)) for i in range(SOURCES)],
    )


def swap_cores(x):
    return lax.ppermute(x, "hid", [(0, 1), (1, 0)])


def local(tokens, w_gate, w_up, w_down, block_counts, block_rows, row_gates):
    place = first()
    tokens, place, counts = lax.optimization_barrier((tokens, place, block_counts))
    half = SOURCES // 2
    pieces = [fetched(tokens, ORDER[half], ORDER[half])]
    pieces += [fetched(tokens, ORDER[b], ORDER[half + b]) for b in range(1, half)]
    mine = stack(pieces)
    got = swap_cores(mine)
    x, act, g = gate_rows(place, counts, tokens, mine, got, block_rows, row_gates, w_gate)
    hidden = hidden_rows(x, act, w_up)
    send = down_half(place, hidden, w_down, True, jnp.bfloat16)
    keep = down_half(place, hidden, w_down, False, jnp.float32)
    own, *parts = near(g, keep, swap_cores(send))
    returned = [swapped(parts[j - 1], j) for j in range(half - 1, 0, -1)]
    own, other = far([own, *returned])
    return final_sum(place, own, sent_home(other, half), swap_cores(own))


def expert_block(segment, w_gate, w_up, w_down):
    gate_act = jnp.dot(segment, w_gate, preferred_element_type=jnp.float32)
    up_act = jnp.dot(segment, w_up, preferred_element_type=jnp.float32)
    hidden = (jax.nn.silu(gate_act) * up_act).astype(jnp.bfloat16)
    return jnp.dot(hidden, w_down, preferred_element_type=jnp.float32).astype(jnp.bfloat16)


def local_wide(tokens, w_gate, w_up, w_down, block_counts, block_rows, row_gates):
    sources = lax.axis_size("exp")
    own_index = lax.axis_index("exp")
    token_count = tokens.shape[0]
    model_width = tokens.shape[1]
    experts = block_rows.shape[0]
    slot_count = block_rows.shape[1]
    per_expert = sources // experts
    my_expert = own_index // per_expert
    position = jnp.arange(slot_count, dtype=jnp.int32)
    is_live = (position[None, :] < block_counts[:, None] * BLOCK) & (block_rows >= 0)
    source = jnp.where(is_live, block_rows // token_count, sources)
    matches = (source[:, :, None] == jnp.arange(sources, dtype=jnp.int32)[None, None, :]).astype(
        jnp.int32
    )
    order_rank = jnp.sum(jnp.cumsum(matches, axis=1) * matches, axis=2) - 1
    is_mine = is_live & (source == own_index)
    slot_target = jnp.where(
        is_mine, jnp.arange(experts, dtype=jnp.int32)[:, None] * CAP + order_rank, experts * CAP
    )
    local_values = jnp.where(is_mine, block_rows - own_index * token_count, token_count)
    local_row = (
        jnp.full((experts * CAP + 1,), token_count, jnp.int32)
        .at[slot_target.ravel()]
        .set(local_values.ravel())[: experts * CAP]
    )
    gate_mine = (
        jnp.zeros((experts * CAP + 1,), jnp.float32)
        .at[slot_target.ravel()]
        .set(jnp.where(is_mine, row_gates, 0.0).ravel())[: experts * CAP]
    )
    live_mine = lax.dynamic_index_in_dim(is_live, my_expert, 0, keepdims=False)
    rows_mine = lax.dynamic_index_in_dim(block_rows, my_expert, 0, keepdims=False)
    source_mine = lax.dynamic_index_in_dim(source, my_expert, 0, keepdims=False)
    rank_mine = lax.dynamic_index_in_dim(order_rank, my_expert, 0, keepdims=False)
    back_index = jnp.where(live_mine, source_mine * CAP + rank_mine, sources * CAP)
    blank_row = jnp.zeros((1, model_width), jnp.bfloat16)
    everyone = lax.all_gather(tokens, "exp", axis=0, tiled=True)
    row_pool = jnp.concatenate([everyone, blank_row], axis=0)
    routed = row_pool[jnp.where(live_mine, rows_mine, sources * token_count)]
    partial_rows = expert_block(routed, w_gate, w_up, w_down)
    outbound = (
        jnp.zeros((sources * CAP + 1, model_width), jnp.bfloat16).at[back_index].set(partial_rows)
    )
    outbound = outbound[: sources * CAP].reshape(sources, CAP, model_width)
    returned = lax.all_to_all(outbound, "exp", split_axis=0, concat_axis=0, tiled=True)
    summed = jnp.sum(
        returned.reshape(experts, per_expert, CAP, model_width), axis=1, dtype=jnp.float32
    )
    weighted = (summed * gate_mine.reshape(experts, CAP, 1)).reshape(experts * CAP, model_width)
    selector = (local_row[:, None] == jnp.arange(token_count, dtype=jnp.int32)[None, :]).astype(
        jnp.float32
    )
    gathered_sum = jnp.einsum("st,sd->td", selector, weighted, precision=lax.Precision.HIGHEST)
    share = lax.psum_scatter(gathered_sum, "hid", scatter_dimension=1, tiled=True)
    return share.astype(jnp.bfloat16)


def solution(mesh):
    small = mesh.shape["exp"] == SOURCES and mesh.shape["hid"] == 2

    def chosen(*args):
        return (local if small and args[5].shape[0] * 2 == SOURCES else local_wide)(*args)

    return jax.shard_map(
        chosen,
        mesh=mesh,
        in_specs=(
            P(("grp", "exp"), None),
            P(None, ("exp", "hid")),
            P(None, ("exp", "hid")),
            P(("exp", "hid"), None),
            P("grp"),
            P("grp", None),
            P("grp", None),
        ),
        out_specs=P(("grp", "exp"), "hid"),
        check_vma=False,
    )
```

```python
import functools

import jax
import jax.numpy as jnp
from jax import lax
from jax.experimental import pallas as pl
from jax.experimental.pallas import tpu as pltpu
from jax.sharding import PartitionSpec as P

BLOCK = 128
CAP = 3
TILE = 512
MIB = 1 << 20
ORDER = (0, 1, 6, 7, 2, 3, 4, 5)
SOURCES = len(ORDER)
GATE = 5_000_000_000
UP = 2_000_000_000
AHEAD = 20_000_000_000
HBM = pl.BlockSpec(memory_space=pltpu.HBM)
VMEM = pl.BlockSpec(memory_space=pltpu.VMEM)
SMEM = pl.BlockSpec(memory_space=pltpu.SMEM)


def in_hbm(x):
    return pltpu.with_memory_space_constraint(x, pltpu.HBM)


def in_smem(x):
    return pltpu.with_memory_space_constraint(x, pltpu.SMEM)


def in_vmem(x):
    return pltpu.with_memory_space_constraint(x, pltpu.VMEM)


def turned(i):
    return (1 + i) % 2


def first_kernel(place_ref):
    side, own = lax.axis_index("hid"), lax.axis_index("exp")
    place_ref[0] = side
    place_ref[1] = own
    place_ref[2] = turned(own)
    place_ref[3] = lax.rem(side + turned(own), 2)


def first():
    return pl.pallas_call(
        first_kernel,
        out_shape=pltpu.SMEM((4,), jnp.int32),
        out_specs=SMEM,
        compiler_params=pltpu.CompilerParams(vmem_limit_bytes=2 * MIB),
        cost_estimate=pl.CostEstimate(flops=AHEAD, bytes_accessed=0, transcendentals=0),
    )()


def routed_gates(own, per_expert, count, counts_ref, rows_ref, gates_ref):
    experts, slots = rows_ref.shape
    expert = own // per_expert
    mine = lax.broadcasted_iota(jnp.int32, (experts, slots), 0) == expert
    rows = jnp.sum(jnp.where(mine, rows_ref[...], 0), axis=0, keepdims=True)
    gates = jnp.sum(jnp.where(mine, gates_ref[...], 0.0), axis=0, keepdims=True)
    position = lax.broadcasted_iota(jnp.int32, (1, slots), 1)
    here = lax.broadcasted_iota(jnp.int32, counts_ref.shape, 1) == expert
    blocks = jnp.sum(jnp.where(here, counts_ref[...], 0), axis=1, keepdims=True)
    rows = jnp.where(position < blocks * BLOCK, rows, -1)
    line = lax.broadcasted_iota(jnp.int32, (SOURCES * count, slots), 0)
    block = line // count
    source = jnp.zeros_like(line)
    for at, k in enumerate(ORDER):
        source = jnp.where(block == at, own ^ k, source)
    token = source * count + lax.rem(line, count)
    return jnp.sum(jnp.where(rows == token, gates, 0.0), axis=1, keepdims=True)


def stack_kernel(*refs):
    for at, ref in enumerate(refs[:-1]):
        refs[-1][at] = ref[...]


def stack(pieces):
    return pl.pallas_call(
        stack_kernel,
        out_shape=jax.ShapeDtypeStruct((len(pieces), *pieces[0].shape), pieces[0].dtype),
        in_specs=[VMEM] * len(pieces),
        out_specs=VMEM,
        compiler_params=pltpu.CompilerParams(vmem_limit_bytes=2 * MIB),
    )(*pieces)


def gate_kernel(
    per_expert,
    place_ref,
    counts_ref,
    tokens_ref,
    mine_ref,
    got_ref,
    rows_ref,
    gates_ref,
    wg_ref,
    x_ref,
    act_ref,
    g_ref,
    wide,
):
    sets, count, _ = mine_ref.shape
    g = routed_gates(place_ref[1], per_expert, count, counts_ref, rows_ref, gates_ref)
    g_ref[...] = jnp.broadcast_to(g, g_ref.shape)
    for j in range(sets):
        rows = pl.ds(j * count, count)
        wide[place_ref[0], rows, :] = mine_ref[j].astype(jnp.float32)
        wide[1 - place_ref[0], rows, :] = got_ref[j].astype(jnp.float32)
    wide[0, pl.ds(0, count), :] = tokens_ref[...].astype(jnp.float32)
    x_ref[...] = wide[...].reshape(x_ref.shape).astype(jnp.bfloat16)

    for n in range(wg_ref.shape[1] // TILE):
        cols = pl.ds(n * TILE, TILE)
        gate = jnp.dot(x_ref[...], wg_ref[:, cols], preferred_element_type=jnp.float32)
        act_ref[:, cols] = gate / (1.0 + jnp.exp(-gate))


def gate_rows(place, counts, tokens, mine, got, block_rows, row_gates, wg):
    total = 2 * mine.shape[0] * mine.shape[1]
    depth, width = wg.shape
    return pl.pallas_call(
        functools.partial(gate_kernel, SOURCES // block_rows.shape[0]),
        out_shape=(
            jax.ShapeDtypeStruct((total, depth), jnp.bfloat16),
            jax.ShapeDtypeStruct((total, width), jnp.float32),
            jax.ShapeDtypeStruct((total, 128), jnp.float32),
        ),
        in_specs=[SMEM] + [VMEM] * 7,
        out_specs=(VMEM,) * 3,
        scratch_shapes=[pltpu.VMEM((2, total // 2, depth), jnp.float32)],
        compiler_params=pltpu.CompilerParams(vmem_limit_bytes=2 * MIB),
        cost_estimate=pl.CostEstimate(flops=GATE, bytes_accessed=0, transcendentals=total * width),
    )(in_smem(place), counts.reshape(1, -1), tokens, mine, got, block_rows, row_gates, in_vmem(wg))


def up_kernel(x_ref, act_ref, wu_ref, h_out):
    for n in range(wu_ref.shape[1] // TILE):
        cols = pl.ds(n * TILE, TILE)
        up = jnp.dot(x_ref[...], wu_ref[:, cols], preferred_element_type=jnp.float32)
        h_out[:, cols] = (act_ref[:, cols] * up).astype(jnp.bfloat16)


def hidden_rows(x, act, wu):
    return pl.pallas_call(
        up_kernel,
        out_shape=jax.ShapeDtypeStruct(act.shape, jnp.bfloat16),
        in_specs=[VMEM] * 3,
        out_specs=VMEM,
        compiler_params=pltpu.CompilerParams(vmem_limit_bytes=2 * MIB),
        cost_estimate=pl.CostEstimate(flops=UP, bytes_accessed=0, transcendentals=0),
    )(x, act, in_vmem(wu))


def down_kernel(other, place_ref, h_ref, wd_ref, out_ref):
    half = wd_ref.shape[1] // 2
    mine = place_ref[3]
    base = (1 - mine if other else mine) * half
    for n in range(half // TILE):
        cols = pl.ds(pl.multiple_of(base + n * TILE, TILE), TILE)
        part = jnp.dot(h_ref[...], wd_ref[:, cols], preferred_element_type=jnp.float32)
        out_ref[:, pl.ds(n * TILE, TILE)] = part.astype(out_ref.dtype)


def down_half(place, hidden, wd, other, dtype):
    rows, depth = hidden.shape
    half = wd.shape[1] // 2
    return pl.pallas_call(
        functools.partial(down_kernel, other),
        out_shape=jax.ShapeDtypeStruct((rows, half), dtype),
        in_specs=[SMEM, VMEM, VMEM],
        out_specs=VMEM,
        compiler_params=pltpu.CompilerParams(vmem_limit_bytes=2 * MIB),
        cost_estimate=pl.CostEstimate(flops=2 * rows * depth * half, bytes_accessed=0, transcendentals=0),
    )(in_smem(place), hidden, in_vmem(wd))


def near_kernel(g_ref, keep_ref, got_ref, own_ref, *out_refs):
    both = (keep_ref[...] + got_ref[...].astype(jnp.float32)) * g_ref[:, :1]
    pair, count, _ = own_ref.shape
    group = SOURCES // pair
    for at, k in enumerate(ORDER):
        out_ref = (own_ref, *out_refs)[k % group]
        out_ref[k // group] = both[at * count : (at + 1) * count].astype(out_ref.dtype)


def near(g, keep, got):
    rows, width = keep.shape
    group = SOURCES // 2
    shape = (2, rows // SOURCES, width)
    return pl.pallas_call(
        near_kernel,
        out_shape=(jax.ShapeDtypeStruct(shape, jnp.float32),)
        + (jax.ShapeDtypeStruct(shape, jnp.bfloat16),) * (group - 1),
        in_specs=[VMEM] * 3,
        out_specs=(VMEM,) * group,
        compiler_params=pltpu.CompilerParams(vmem_limit_bytes=2 * MIB),
    )(g, keep, got)


def far_kernel(*refs):
    *part_refs, own_ref, turn_ref, next_ref = refs
    for i, out_refs in enumerate(((own_ref, turn_ref), (next_ref,))):
        total = part_refs[0][i]
        for part_ref in part_refs[1:]:
            total = total + part_ref[i].astype(jnp.float32)
        for out_ref in out_refs:
            out_ref[...] = total.astype(out_ref.dtype)


def far(parts):
    shape = parts[0].shape[1:]
    return pl.pallas_call(
        far_kernel,
        out_shape=(jax.ShapeDtypeStruct(shape, jnp.float32),) + (jax.ShapeDtypeStruct(shape, jnp.bfloat16),) * 2,
        in_specs=[VMEM] * len(parts),
        out_specs=(VMEM,) * 3,
        compiler_params=pltpu.CompilerParams(vmem_limit_bytes=2 * MIB),
    )(*parts)


def sum_kernel(place_ref, own_ref, got_ref, turned_ref, out_ref):
    own = jnp.where(place_ref[2] == 1, turned_ref[...].astype(jnp.float32), own_ref[...])
    out_ref[...] = (own + got_ref[...].astype(jnp.float32)).astype(out_ref.dtype)


def final_sum(place, own, got, other_core):
    return pl.pallas_call(
        sum_kernel,
        out_shape=jax.ShapeDtypeStruct(own.shape, jnp.bfloat16),
        in_specs=[SMEM] + [VMEM] * 3,
        out_specs=VMEM,
        compiler_params=pltpu.CompilerParams(vmem_limit_bytes=2 * MIB),
    )(in_smem(place), own, got, other_core)


def swapped(x, k):
    pairs = [
        (2 * i + side, 2 * (i ^ k) + (side + turned(i) + turned(i ^ k)) % 2) for i in range(SOURCES) for side in range(2)
    ]
    return lax.ppermute(x, ("exp", "hid"), pairs)


def sent_home(x, k):
    pairs = [(2 * i + side, 2 * (i ^ k) + (side + turned(i)) % 2) for i in range(SOURCES) for side in range(2)]
    return lax.ppermute(x, ("exp", "hid"), pairs)


def fetched(x, first, second):
    return lax.ppermute(
        x,
        ("exp", "hid"),
        [(2 * i + 1 - side, 2 * (i ^ k) + side) for side, k in enumerate((first, second)) for i in range(SOURCES)],
    )


def swap_cores(x):
    return lax.ppermute(x, "hid", [(0, 1), (1, 0)])


def local(tokens, w_gate, w_up, w_down, block_counts, block_rows, row_gates):
    place = first()
    tokens, place, counts = lax.optimization_barrier((tokens, place, block_counts))
    half = SOURCES // 2
    pieces = [fetched(tokens, ORDER[half], ORDER[half])]
    pieces += [fetched(tokens, ORDER[b], ORDER[half + b]) for b in range(1, half)]
    mine = stack(pieces)
    got = swap_cores(mine)
    x, act, g = gate_rows(place, counts, tokens, mine, got, block_rows, row_gates, w_gate)
    hidden = hidden_rows(x, act, w_up)
    send = down_half(place, hidden, w_down, True, jnp.bfloat16)
    keep = down_half(place, hidden, w_down, False, jnp.float32)
    own, *parts = near(g, keep, swap_cores(send))
    returned = [swapped(parts[j - 1], j) for j in range(half - 1, 0, -1)]
    own, turn, other = far([own, *returned])
    return final_sum(place, own, sent_home(other, half), swap_cores(turn))


def expert_block(segment, w_gate, w_up, w_down):
    gate_act = jnp.dot(segment, w_gate, preferred_element_type=jnp.float32)
    up_act = jnp.dot(segment, w_up, preferred_element_type=jnp.float32)
    hidden = (jax.nn.silu(gate_act) * up_act).astype(jnp.bfloat16)
    return jnp.dot(hidden, w_down, preferred_element_type=jnp.float32).astype(jnp.bfloat16)


def local_wide(tokens, w_gate, w_up, w_down, block_counts, block_rows, row_gates):
    sources = lax.axis_size("exp")
    own_index = lax.axis_index("exp")
    token_count = tokens.shape[0]
    model_width = tokens.shape[1]
    experts = block_rows.shape[0]
    slot_count = block_rows.shape[1]
    per_expert = sources // experts
    my_expert = own_index // per_expert
    position = jnp.arange(slot_count, dtype=jnp.int32)
    is_live = (position[None, :] < block_counts[:, None] * BLOCK) & (block_rows >= 0)
    source = jnp.where(is_live, block_rows // token_count, sources)
    matches = (source[:, :, None] == jnp.arange(sources, dtype=jnp.int32)[None, None, :]).astype(
        jnp.int32
    )
    order_rank = jnp.sum(jnp.cumsum(matches, axis=1) * matches, axis=2) - 1
    is_mine = is_live & (source == own_index)
    slot_target = jnp.where(
        is_mine, jnp.arange(experts, dtype=jnp.int32)[:, None] * CAP + order_rank, experts * CAP
    )
    local_values = jnp.where(is_mine, block_rows - own_index * token_count, token_count)
    local_row = (
        jnp.full((experts * CAP + 1,), token_count, jnp.int32)
        .at[slot_target.ravel()]
        .set(local_values.ravel())[: experts * CAP]
    )
    gate_mine = (
        jnp.zeros((experts * CAP + 1,), jnp.float32)
        .at[slot_target.ravel()]
        .set(jnp.where(is_mine, row_gates, 0.0).ravel())[: experts * CAP]
    )
    live_mine = lax.dynamic_index_in_dim(is_live, my_expert, 0, keepdims=False)
    rows_mine = lax.dynamic_index_in_dim(block_rows, my_expert, 0, keepdims=False)
    source_mine = lax.dynamic_index_in_dim(source, my_expert, 0, keepdims=False)
    rank_mine = lax.dynamic_index_in_dim(order_rank, my_expert, 0, keepdims=False)
    back_index = jnp.where(live_mine, source_mine * CAP + rank_mine, sources * CAP)
    blank_row = jnp.zeros((1, model_width), jnp.bfloat16)
    everyone = lax.all_gather(tokens, "exp", axis=0, tiled=True)
    row_pool = jnp.concatenate([everyone, blank_row], axis=0)
    routed = row_pool[jnp.where(live_mine, rows_mine, sources * token_count)]
    partial_rows = expert_block(routed, w_gate, w_up, w_down)
    outbound = (
        jnp.zeros((sources * CAP + 1, model_width), jnp.bfloat16).at[back_index].set(partial_rows)
    )
    outbound = outbound[: sources * CAP].reshape(sources, CAP, model_width)
    returned = lax.all_to_all(outbound, "exp", split_axis=0, concat_axis=0, tiled=True)
    summed = jnp.sum(
        returned.reshape(experts, per_expert, CAP, model_width), axis=1, dtype=jnp.float32
    )
    weighted = (summed * gate_mine.reshape(experts, CAP, 1)).reshape(experts * CAP, model_width)
    selector = (local_row[:, None] == jnp.arange(token_count, dtype=jnp.int32)[None, :]).astype(
        jnp.float32
    )
    gathered_sum = jnp.einsum("st,sd->td", selector, weighted, precision=lax.Precision.HIGHEST)
    share = lax.psum_scatter(gathered_sum, "hid", scatter_dimension=1, tiled=True)
    return share.astype(jnp.bfloat16)


def solution(mesh):
    small = mesh.shape["exp"] == SOURCES and mesh.shape["hid"] == 2

    def chosen(*args):
        return (local if small and args[5].shape[0] * 2 == SOURCES else local_wide)(*args)

    return jax.shard_map(
        chosen,
        mesh=mesh,
        in_specs=(
            P(("grp", "exp"), None),
            P(None, ("exp", "hid")),
            P(None, ("exp", "hid")),
            P(("exp", "hid"), None),
            P("grp"),
            P("grp", None),
            P("grp", None),
        ),
        out_specs=P(("grp", "exp"), "hid"),
        check_vma=False,
    )
```

```python
import functools

import jax
import jax.numpy as jnp
from jax import lax
from jax.experimental import pallas as pl
from jax.experimental.pallas import tpu as pltpu
from jax.sharding import PartitionSpec as P

BLOCK = 128
CAP = 3
TILE = 512
MIB = 1 << 20
ORDER = (0, 6, 7, 1, 2, 4, 5, 3)
SOURCES = len(ORDER)
GATE = 5_000_000_000
UP = 2_000_000_000
AHEAD = 20_000_000_000
HBM = pl.BlockSpec(memory_space=pltpu.HBM)
VMEM = pl.BlockSpec(memory_space=pltpu.VMEM)
SMEM = pl.BlockSpec(memory_space=pltpu.SMEM)


def in_hbm(x):
    return pltpu.with_memory_space_constraint(x, pltpu.HBM)


def in_smem(x):
    return pltpu.with_memory_space_constraint(x, pltpu.SMEM)


def in_vmem(x):
    return pltpu.with_memory_space_constraint(x, pltpu.VMEM)


def turned(i):
    return (1 + i) % 2


def first_kernel(place_ref):
    side, own = lax.axis_index("hid"), lax.axis_index("exp")
    place_ref[0] = side
    place_ref[1] = own
    place_ref[2] = turned(own)
    place_ref[3] = lax.rem(side + turned(own), 2)


def first():
    return pl.pallas_call(
        first_kernel,
        out_shape=pltpu.SMEM((4,), jnp.int32),
        out_specs=SMEM,
        compiler_params=pltpu.CompilerParams(vmem_limit_bytes=2 * MIB),
        cost_estimate=pl.CostEstimate(flops=AHEAD, bytes_accessed=0, transcendentals=0),
    )()


def routed_gates(own, per_expert, count, counts_ref, rows_ref, gates_ref):
    experts, slots = rows_ref.shape
    expert = own // per_expert
    mine = lax.broadcasted_iota(jnp.int32, (experts, slots), 0) == expert
    rows = jnp.sum(jnp.where(mine, rows_ref[...], 0), axis=0, keepdims=True)
    gates = jnp.sum(jnp.where(mine, gates_ref[...], 0.0), axis=0, keepdims=True)
    position = lax.broadcasted_iota(jnp.int32, (1, slots), 1)
    here = lax.broadcasted_iota(jnp.int32, counts_ref.shape, 1) == expert
    blocks = jnp.sum(jnp.where(here, counts_ref[...], 0), axis=1, keepdims=True)
    rows = jnp.where(position < blocks * BLOCK, rows, -1)
    line = lax.broadcasted_iota(jnp.int32, (SOURCES * count, slots), 0)
    block = line // count
    source = jnp.zeros_like(line)
    for at, k in enumerate(ORDER):
        source = jnp.where(block == at, own ^ k, source)
    token = source * count + lax.rem(line, count)
    return jnp.sum(jnp.where(rows == token, gates, 0.0), axis=1, keepdims=True)


def stack_kernel(*refs):
    for at, ref in enumerate(refs[:-1]):
        refs[-1][at] = ref[...]


def stack(pieces):
    return pl.pallas_call(
        stack_kernel,
        out_shape=jax.ShapeDtypeStruct((len(pieces), *pieces[0].shape), pieces[0].dtype),
        in_specs=[VMEM] * len(pieces),
        out_specs=VMEM,
        compiler_params=pltpu.CompilerParams(vmem_limit_bytes=2 * MIB),
    )(*pieces)


def gate_kernel(
    per_expert,
    place_ref,
    counts_ref,
    tokens_ref,
    mine_ref,
    got_ref,
    rows_ref,
    gates_ref,
    wg_ref,
    x_ref,
    act_ref,
    g_ref,
    wide,
):
    sets, count, _ = mine_ref.shape
    g = routed_gates(place_ref[1], per_expert, count, counts_ref, rows_ref, gates_ref)
    g_ref[...] = jnp.broadcast_to(g, g_ref.shape)
    for j in range(sets):
        rows = pl.ds(j * count, count)
        wide[place_ref[0], rows, :] = mine_ref[j].astype(jnp.float32)
        wide[1 - place_ref[0], rows, :] = got_ref[j].astype(jnp.float32)
    wide[0, pl.ds(0, count), :] = tokens_ref[...].astype(jnp.float32)
    x_ref[...] = wide[...].reshape(x_ref.shape).astype(jnp.bfloat16)

    for n in range(wg_ref.shape[1] // TILE):
        cols = pl.ds(n * TILE, TILE)
        gate = jnp.dot(x_ref[...], wg_ref[:, cols], preferred_element_type=jnp.float32)
        act_ref[:, cols] = gate / (1.0 + jnp.exp(-gate))


def gate_rows(place, counts, tokens, mine, got, block_rows, row_gates, wg):
    total = 2 * mine.shape[0] * mine.shape[1]
    depth, width = wg.shape
    return pl.pallas_call(
        functools.partial(gate_kernel, SOURCES // block_rows.shape[0]),
        out_shape=(
            jax.ShapeDtypeStruct((total, depth), jnp.bfloat16),
            jax.ShapeDtypeStruct((total, width), jnp.float32),
            jax.ShapeDtypeStruct((total, 128), jnp.float32),
        ),
        in_specs=[SMEM] + [VMEM] * 7,
        out_specs=(VMEM,) * 3,
        scratch_shapes=[pltpu.VMEM((2, total // 2, depth), jnp.float32)],
        compiler_params=pltpu.CompilerParams(vmem_limit_bytes=2 * MIB),
        cost_estimate=pl.CostEstimate(flops=GATE, bytes_accessed=0, transcendentals=total * width),
    )(in_smem(place), counts.reshape(1, -1), tokens, mine, got, block_rows, row_gates, in_vmem(wg))


def up_kernel(x_ref, act_ref, wu_ref, h_out):
    for n in range(wu_ref.shape[1] // TILE):
        cols = pl.ds(n * TILE, TILE)
        up = jnp.dot(x_ref[...], wu_ref[:, cols], preferred_element_type=jnp.float32)
        h_out[:, cols] = (act_ref[:, cols] * up).astype(jnp.bfloat16)


def hidden_rows(x, act, wu):
    return pl.pallas_call(
        up_kernel,
        out_shape=jax.ShapeDtypeStruct(act.shape, jnp.bfloat16),
        in_specs=[VMEM] * 3,
        out_specs=VMEM,
        compiler_params=pltpu.CompilerParams(vmem_limit_bytes=2 * MIB),
        cost_estimate=pl.CostEstimate(flops=UP, bytes_accessed=0, transcendentals=0),
    )(x, act, in_vmem(wu))


def down_kernel(other, place_ref, h_ref, wd_ref, out_ref):
    half = wd_ref.shape[1] // 2
    mine = place_ref[3]
    base = (1 - mine if other else mine) * half
    for n in range(half // TILE):
        cols = pl.ds(pl.multiple_of(base + n * TILE, TILE), TILE)
        part = jnp.dot(h_ref[...], wd_ref[:, cols], preferred_element_type=jnp.float32)
        out_ref[:, pl.ds(n * TILE, TILE)] = part.astype(out_ref.dtype)


def down_half(place, hidden, wd, other, dtype):
    rows, depth = hidden.shape
    half = wd.shape[1] // 2
    return pl.pallas_call(
        functools.partial(down_kernel, other),
        out_shape=jax.ShapeDtypeStruct((rows, half), dtype),
        in_specs=[SMEM, VMEM, VMEM],
        out_specs=VMEM,
        compiler_params=pltpu.CompilerParams(vmem_limit_bytes=2 * MIB),
        cost_estimate=pl.CostEstimate(flops=2 * rows * depth * half, bytes_accessed=0, transcendentals=0),
    )(in_smem(place), hidden, in_vmem(wd))


def near_kernel(g_ref, keep_ref, got_ref, own_ref, *out_refs):
    both = (keep_ref[...] + got_ref[...].astype(jnp.float32)) * g_ref[:, :1]
    pair, count, _ = own_ref.shape
    group = SOURCES // pair
    for at, k in enumerate(ORDER):
        out_ref = (own_ref, *out_refs)[k % group]
        out_ref[k // group] = both[at * count : (at + 1) * count].astype(out_ref.dtype)


def near(g, keep, got):
    rows, width = keep.shape
    group = SOURCES // 2
    shape = (2, rows // SOURCES, width)
    return pl.pallas_call(
        near_kernel,
        out_shape=(jax.ShapeDtypeStruct(shape, jnp.float32),)
        + (jax.ShapeDtypeStruct(shape, jnp.bfloat16),) * (group - 1),
        in_specs=[VMEM] * 3,
        out_specs=(VMEM,) * group,
        compiler_params=pltpu.CompilerParams(vmem_limit_bytes=2 * MIB),
    )(g, keep, got)


def far_kernel(*refs):
    *part_refs, own_ref, turn_ref, next_ref = refs
    for i, out_refs in enumerate(((own_ref, turn_ref), (next_ref,))):
        total = part_refs[0][i]
        for part_ref in part_refs[1:]:
            total = total + part_ref[i].astype(jnp.float32)
        for out_ref in out_refs:
            out_ref[...] = total.astype(out_ref.dtype)


def far(parts):
    shape = parts[0].shape[1:]
    return pl.pallas_call(
        far_kernel,
        out_shape=(jax.ShapeDtypeStruct(shape, jnp.float32),) + (jax.ShapeDtypeStruct(shape, jnp.bfloat16),) * 2,
        in_specs=[VMEM] * len(parts),
        out_specs=(VMEM,) * 3,
        compiler_params=pltpu.CompilerParams(vmem_limit_bytes=2 * MIB),
    )(*parts)


def sum_kernel(place_ref, own_ref, got_ref, turned_ref, out_ref):
    own = jnp.where(place_ref[2] == 1, turned_ref[...].astype(jnp.float32), own_ref[...])
    out_ref[...] = (own + got_ref[...].astype(jnp.float32)).astype(out_ref.dtype)


def final_sum(place, own, got, other_core):
    return pl.pallas_call(
        sum_kernel,
        out_shape=jax.ShapeDtypeStruct(own.shape, jnp.bfloat16),
        in_specs=[SMEM] + [VMEM] * 3,
        out_specs=VMEM,
        compiler_params=pltpu.CompilerParams(vmem_limit_bytes=2 * MIB),
    )(in_smem(place), own, got, other_core)


def swapped(x, k):
    pairs = [
        (2 * i + side, 2 * (i ^ k) + (side + turned(i) + turned(i ^ k)) % 2) for i in range(SOURCES) for side in range(2)
    ]
    return lax.ppermute(x, ("exp", "hid"), pairs)


def sent_home(x, k):
    pairs = [(2 * i + side, 2 * (i ^ k) + (side + turned(i)) % 2) for i in range(SOURCES) for side in range(2)]
    return lax.ppermute(x, ("exp", "hid"), pairs)


def fetched(x, first, second):
    return lax.ppermute(
        x,
        ("exp", "hid"),
        [(2 * i + 1 - side, 2 * (i ^ k) + side) for side, k in enumerate((first, second)) for i in range(SOURCES)],
    )


def swap_cores(x):
    return lax.ppermute(x, "hid", [(0, 1), (1, 0)])


def local(tokens, w_gate, w_up, w_down, block_counts, block_rows, row_gates):
    place = first()
    tokens, place, counts = lax.optimization_barrier((tokens, place, block_counts))
    half = SOURCES // 2
    pieces = [fetched(tokens, ORDER[half], ORDER[half])]
    pieces += [fetched(tokens, ORDER[b], ORDER[half + b]) for b in range(1, half)]
    mine = stack(pieces)
    got = swap_cores(mine)
    x, act, g = gate_rows(place, counts, tokens, mine, got, block_rows, row_gates, w_gate)
    hidden = hidden_rows(x, act, w_up)
    send = down_half(place, hidden, w_down, True, jnp.bfloat16)
    keep = down_half(place, hidden, w_down, False, jnp.float32)
    own, *parts = near(g, keep, swap_cores(send))
    returned = [swapped(parts[j - 1], j) for j in range(half - 1, 0, -1)]
    own, turn, other = far([own, *returned])
    return final_sum(place, own, sent_home(other, half), swap_cores(turn))


def expert_block(segment, w_gate, w_up, w_down):
    gate_act = jnp.dot(segment, w_gate, preferred_element_type=jnp.float32)
    up_act = jnp.dot(segment, w_up, preferred_element_type=jnp.float32)
    hidden = (jax.nn.silu(gate_act) * up_act).astype(jnp.bfloat16)
    return jnp.dot(hidden, w_down, preferred_element_type=jnp.float32).astype(jnp.bfloat16)


def local_wide(tokens, w_gate, w_up, w_down, block_counts, block_rows, row_gates):
    sources = lax.axis_size("exp")
    own_index = lax.axis_index("exp")
    token_count = tokens.shape[0]
    model_width = tokens.shape[1]
    experts = block_rows.shape[0]
    slot_count = block_rows.shape[1]
    per_expert = sources // experts
    my_expert = own_index // per_expert
    position = jnp.arange(slot_count, dtype=jnp.int32)
    is_live = (position[None, :] < block_counts[:, None] * BLOCK) & (block_rows >= 0)
    source = jnp.where(is_live, block_rows // token_count, sources)
    matches = (source[:, :, None] == jnp.arange(sources, dtype=jnp.int32)[None, None, :]).astype(
        jnp.int32
    )
    order_rank = jnp.sum(jnp.cumsum(matches, axis=1) * matches, axis=2) - 1
    is_mine = is_live & (source == own_index)
    slot_target = jnp.where(
        is_mine, jnp.arange(experts, dtype=jnp.int32)[:, None] * CAP + order_rank, experts * CAP
    )
    local_values = jnp.where(is_mine, block_rows - own_index * token_count, token_count)
    local_row = (
        jnp.full((experts * CAP + 1,), token_count, jnp.int32)
        .at[slot_target.ravel()]
        .set(local_values.ravel())[: experts * CAP]
    )
    gate_mine = (
        jnp.zeros((experts * CAP + 1,), jnp.float32)
        .at[slot_target.ravel()]
        .set(jnp.where(is_mine, row_gates, 0.0).ravel())[: experts * CAP]
    )
    live_mine = lax.dynamic_index_in_dim(is_live, my_expert, 0, keepdims=False)
    rows_mine = lax.dynamic_index_in_dim(block_rows, my_expert, 0, keepdims=False)
    source_mine = lax.dynamic_index_in_dim(source, my_expert, 0, keepdims=False)
    rank_mine = lax.dynamic_index_in_dim(order_rank, my_expert, 0, keepdims=False)
    back_index = jnp.where(live_mine, source_mine * CAP + rank_mine, sources * CAP)
    blank_row = jnp.zeros((1, model_width), jnp.bfloat16)
    everyone = lax.all_gather(tokens, "exp", axis=0, tiled=True)
    row_pool = jnp.concatenate([everyone, blank_row], axis=0)
    routed = row_pool[jnp.where(live_mine, rows_mine, sources * token_count)]
    partial_rows = expert_block(routed, w_gate, w_up, w_down)
    outbound = (
        jnp.zeros((sources * CAP + 1, model_width), jnp.bfloat16).at[back_index].set(partial_rows)
    )
    outbound = outbound[: sources * CAP].reshape(sources, CAP, model_width)
    returned = lax.all_to_all(outbound, "exp", split_axis=0, concat_axis=0, tiled=True)
    summed = jnp.sum(
        returned.reshape(experts, per_expert, CAP, model_width), axis=1, dtype=jnp.float32
    )
    weighted = (summed * gate_mine.reshape(experts, CAP, 1)).reshape(experts * CAP, model_width)
    selector = (local_row[:, None] == jnp.arange(token_count, dtype=jnp.int32)[None, :]).astype(
        jnp.float32
    )
    gathered_sum = jnp.einsum("st,sd->td", selector, weighted, precision=lax.Precision.HIGHEST)
    share = lax.psum_scatter(gathered_sum, "hid", scatter_dimension=1, tiled=True)
    return share.astype(jnp.bfloat16)


def solution(mesh):
    small = mesh.shape["exp"] == SOURCES and mesh.shape["hid"] == 2

    def chosen(*args):
        return (local if small and args[5].shape[0] * 2 == SOURCES else local_wide)(*args)

    return jax.shard_map(
        chosen,
        mesh=mesh,
        in_specs=(
            P(("grp", "exp"), None),
            P(None, ("exp", "hid")),
            P(None, ("exp", "hid")),
            P(("exp", "hid"), None),
            P("grp"),
            P("grp", None),
            P("grp", None),
        ),
        out_specs=P(("grp", "exp"), "hid"),
        check_vma=False,
    )
```

```python
import functools

import jax
import jax.numpy as jnp
from jax import lax
from jax.experimental import pallas as pl
from jax.experimental.pallas import tpu as pltpu
from jax.sharding import PartitionSpec as P

BLOCK = 128
CAP = 3
TILE = 512
MIB = 1 << 20
ORDER = (0, 3, 7, 5, 2, 1, 6, 4)
SOURCES = len(ORDER)
GATE = 5_000_000_000
UP = 2_000_000_000
AHEAD = 20_000_000_000
HBM = pl.BlockSpec(memory_space=pltpu.HBM)
VMEM = pl.BlockSpec(memory_space=pltpu.VMEM)
SMEM = pl.BlockSpec(memory_space=pltpu.SMEM)


def in_hbm(x):
    return pltpu.with_memory_space_constraint(x, pltpu.HBM)


def in_smem(x):
    return pltpu.with_memory_space_constraint(x, pltpu.SMEM)


def in_vmem(x):
    return pltpu.with_memory_space_constraint(x, pltpu.VMEM)


def turned(i):
    return (1 + i) % 2


def first_kernel(place_ref):
    side, own = lax.axis_index("hid"), lax.axis_index("exp")
    place_ref[0] = side
    place_ref[1] = own
    place_ref[2] = turned(own)
    place_ref[3] = lax.rem(side + turned(own), 2)


def first():
    return pl.pallas_call(
        first_kernel,
        out_shape=pltpu.SMEM((4,), jnp.int32),
        out_specs=SMEM,
        compiler_params=pltpu.CompilerParams(vmem_limit_bytes=2 * MIB),
        cost_estimate=pl.CostEstimate(flops=AHEAD, bytes_accessed=0, transcendentals=0),
    )()


def routed_gates(own, per_expert, count, counts_ref, rows_ref, gates_ref):
    experts, slots = rows_ref.shape
    expert = own // per_expert
    mine = lax.broadcasted_iota(jnp.int32, (experts, slots), 0) == expert
    rows = jnp.sum(jnp.where(mine, rows_ref[...], 0), axis=0, keepdims=True)
    gates = jnp.sum(jnp.where(mine, gates_ref[...], 0.0), axis=0, keepdims=True)
    position = lax.broadcasted_iota(jnp.int32, (1, slots), 1)
    here = lax.broadcasted_iota(jnp.int32, counts_ref.shape, 1) == expert
    blocks = jnp.sum(jnp.where(here, counts_ref[...], 0), axis=1, keepdims=True)
    rows = jnp.where(position < blocks * BLOCK, rows, -1)
    line = lax.broadcasted_iota(jnp.int32, (SOURCES * count, slots), 0)
    block = line // count
    source = jnp.zeros_like(line)
    for at, k in enumerate(ORDER):
        source = jnp.where(block == at, own ^ k, source)
    token = source * count + lax.rem(line, count)
    return jnp.sum(jnp.where(rows == token, gates, 0.0), axis=1, keepdims=True)


def stack_kernel(*refs):
    for at, ref in enumerate(refs[:-1]):
        refs[-1][at] = ref[...]


def stack(pieces):
    return pl.pallas_call(
        stack_kernel,
        out_shape=jax.ShapeDtypeStruct((len(pieces), *pieces[0].shape), pieces[0].dtype),
        in_specs=[VMEM] * len(pieces),
        out_specs=VMEM,
        compiler_params=pltpu.CompilerParams(vmem_limit_bytes=2 * MIB),
    )(*pieces)


def gate_kernel(
    per_expert,
    place_ref,
    counts_ref,
    tokens_ref,
    mine_ref,
    got_ref,
    rows_ref,
    gates_ref,
    wg_ref,
    x_ref,
    act_ref,
    g_ref,
    wide,
):
    sets, count, _ = mine_ref.shape
    g = routed_gates(place_ref[1], per_expert, count, counts_ref, rows_ref, gates_ref)
    g_ref[...] = jnp.broadcast_to(g, g_ref.shape)
    for j in range(sets):
        rows = pl.ds(j * count, count)
        wide[place_ref[0], rows, :] = mine_ref[j].astype(jnp.float32)
        wide[1 - place_ref[0], rows, :] = got_ref[j].astype(jnp.float32)
    wide[0, pl.ds(0, count), :] = tokens_ref[...].astype(jnp.float32)
    x_ref[...] = wide[...].reshape(x_ref.shape).astype(jnp.bfloat16)

    for n in range(wg_ref.shape[1] // TILE):
        cols = pl.ds(n * TILE, TILE)
        gate = jnp.dot(x_ref[...], wg_ref[:, cols], preferred_element_type=jnp.float32)
        act_ref[:, cols] = gate / (1.0 + jnp.exp(-gate))


def gate_rows(place, counts, tokens, mine, got, block_rows, row_gates, wg):
    total = 2 * mine.shape[0] * mine.shape[1]
    depth, width = wg.shape
    return pl.pallas_call(
        functools.partial(gate_kernel, SOURCES // block_rows.shape[0]),
        out_shape=(
            jax.ShapeDtypeStruct((total, depth), jnp.bfloat16),
            jax.ShapeDtypeStruct((total, width), jnp.float32),
            jax.ShapeDtypeStruct((total, 128), jnp.float32),
        ),
        in_specs=[SMEM] + [VMEM] * 7,
        out_specs=(VMEM,) * 3,
        scratch_shapes=[pltpu.VMEM((2, total // 2, depth), jnp.float32)],
        compiler_params=pltpu.CompilerParams(vmem_limit_bytes=2 * MIB),
        cost_estimate=pl.CostEstimate(flops=GATE, bytes_accessed=0, transcendentals=total * width),
    )(in_smem(place), counts.reshape(1, -1), tokens, mine, got, block_rows, row_gates, in_vmem(wg))


def up_kernel(x_ref, act_ref, wu_ref, h_out):
    for n in range(wu_ref.shape[1] // TILE):
        cols = pl.ds(n * TILE, TILE)
        up = jnp.dot(x_ref[...], wu_ref[:, cols], preferred_element_type=jnp.float32)
        h_out[:, cols] = (act_ref[:, cols] * up).astype(jnp.bfloat16)


def hidden_rows(x, act, wu):
    return pl.pallas_call(
        up_kernel,
        out_shape=jax.ShapeDtypeStruct(act.shape, jnp.bfloat16),
        in_specs=[VMEM] * 3,
        out_specs=VMEM,
        compiler_params=pltpu.CompilerParams(vmem_limit_bytes=2 * MIB),
        cost_estimate=pl.CostEstimate(flops=UP, bytes_accessed=0, transcendentals=0),
    )(x, act, in_vmem(wu))


def down_kernel(other, place_ref, h_ref, wd_ref, out_ref):
    half = wd_ref.shape[1] // 2
    mine = place_ref[3]
    base = (1 - mine if other else mine) * half
    for n in range(half // TILE):
        cols = pl.ds(pl.multiple_of(base + n * TILE, TILE), TILE)
        part = jnp.dot(h_ref[...], wd_ref[:, cols], preferred_element_type=jnp.float32)
        out_ref[:, pl.ds(n * TILE, TILE)] = part.astype(out_ref.dtype)


def down_half(place, hidden, wd, other, dtype):
    rows, depth = hidden.shape
    half = wd.shape[1] // 2
    return pl.pallas_call(
        functools.partial(down_kernel, other),
        out_shape=jax.ShapeDtypeStruct((rows, half), dtype),
        in_specs=[SMEM, VMEM, VMEM],
        out_specs=VMEM,
        compiler_params=pltpu.CompilerParams(vmem_limit_bytes=2 * MIB),
        cost_estimate=pl.CostEstimate(flops=2 * rows * depth * half, bytes_accessed=0, transcendentals=0),
    )(in_smem(place), hidden, in_vmem(wd))


def near_kernel(g_ref, keep_ref, got_ref, own_ref, *out_refs):
    both = (keep_ref[...] + got_ref[...].astype(jnp.float32)) * g_ref[:, :1]
    pair, count, _ = own_ref.shape
    group = SOURCES // pair
    for at, k in enumerate(ORDER):
        out_ref = (own_ref, *out_refs)[k % group]
        out_ref[k // group] = both[at * count : (at + 1) * count].astype(out_ref.dtype)


def near(g, keep, got):
    rows, width = keep.shape
    group = SOURCES // 2
    shape = (2, rows // SOURCES, width)
    return pl.pallas_call(
        near_kernel,
        out_shape=(jax.ShapeDtypeStruct(shape, jnp.float32),)
        + (jax.ShapeDtypeStruct(shape, jnp.bfloat16),) * (group - 1),
        in_specs=[VMEM] * 3,
        out_specs=(VMEM,) * group,
        compiler_params=pltpu.CompilerParams(vmem_limit_bytes=2 * MIB),
    )(g, keep, got)


def far_kernel(*refs):
    *part_refs, own_ref, turn_ref, next_ref = refs
    for i, out_refs in enumerate(((own_ref, turn_ref), (next_ref,))):
        total = part_refs[0][i]
        for part_ref in part_refs[1:]:
            total = total + part_ref[i].astype(jnp.float32)
        for out_ref in out_refs:
            out_ref[...] = total.astype(out_ref.dtype)


def far(parts):
    shape = parts[0].shape[1:]
    return pl.pallas_call(
        far_kernel,
        out_shape=(jax.ShapeDtypeStruct(shape, jnp.float32),) + (jax.ShapeDtypeStruct(shape, jnp.bfloat16),) * 2,
        in_specs=[VMEM] * len(parts),
        out_specs=(VMEM,) * 3,
        compiler_params=pltpu.CompilerParams(vmem_limit_bytes=2 * MIB),
    )(*parts)


def sum_kernel(place_ref, own_ref, got_ref, turned_ref, out_ref):
    own = jnp.where(place_ref[2] == 1, turned_ref[...].astype(jnp.float32), own_ref[...])
    out_ref[...] = (own + got_ref[...].astype(jnp.float32)).astype(out_ref.dtype)


def final_sum(place, own, got, other_core):
    return pl.pallas_call(
        sum_kernel,
        out_shape=jax.ShapeDtypeStruct(own.shape, jnp.bfloat16),
        in_specs=[SMEM] + [VMEM] * 3,
        out_specs=VMEM,
        compiler_params=pltpu.CompilerParams(vmem_limit_bytes=2 * MIB),
    )(in_smem(place), own, got, other_core)


def swapped(x, k):
    pairs = [
        (2 * i + side, 2 * (i ^ k) + (side + turned(i) + turned(i ^ k)) % 2) for i in range(SOURCES) for side in range(2)
    ]
    return lax.ppermute(x, ("exp", "hid"), pairs)


def sent_home(x, k):
    pairs = [(2 * i + side, 2 * (i ^ k) + (side + turned(i)) % 2) for i in range(SOURCES) for side in range(2)]
    return lax.ppermute(x, ("exp", "hid"), pairs)


def fetched(x, first, second):
    return lax.ppermute(
        x,
        ("exp", "hid"),
        [(2 * i + 1 - side, 2 * (i ^ k) + side) for side, k in enumerate((first, second)) for i in range(SOURCES)],
    )


def swap_cores(x):
    return lax.ppermute(x, "hid", [(0, 1), (1, 0)])


def local(tokens, w_gate, w_up, w_down, block_counts, block_rows, row_gates):
    place = first()
    tokens, place, counts = lax.optimization_barrier((tokens, place, block_counts))
    half = SOURCES // 2
    pieces = [fetched(tokens, ORDER[half], ORDER[half])]
    pieces += [fetched(tokens, ORDER[b], ORDER[half + b]) for b in range(1, half)]
    mine = stack(pieces)
    got = swap_cores(mine)
    x, act, g = gate_rows(place, counts, tokens, mine, got, block_rows, row_gates, w_gate)
    hidden = hidden_rows(x, act, w_up)
    send = down_half(place, hidden, w_down, True, jnp.bfloat16)
    keep = down_half(place, hidden, w_down, False, jnp.float32)
    own, *parts = near(g, keep, swap_cores(send))
    returned = [swapped(parts[j - 1], j) for j in range(half - 1, 0, -1)]
    own, turn, other = far([own, *returned])
    return final_sum(place, own, sent_home(other, half), swap_cores(turn))


def expert_block(segment, w_gate, w_up, w_down):
    gate_act = jnp.dot(segment, w_gate, preferred_element_type=jnp.float32)
    up_act = jnp.dot(segment, w_up, preferred_element_type=jnp.float32)
    hidden = (jax.nn.silu(gate_act) * up_act).astype(jnp.bfloat16)
    return jnp.dot(hidden, w_down, preferred_element_type=jnp.float32).astype(jnp.bfloat16)


def local_wide(tokens, w_gate, w_up, w_down, block_counts, block_rows, row_gates):
    sources = lax.axis_size("exp")
    own_index = lax.axis_index("exp")
    token_count = tokens.shape[0]
    model_width = tokens.shape[1]
    experts = block_rows.shape[0]
    slot_count = block_rows.shape[1]
    per_expert = sources // experts
    my_expert = own_index // per_expert
    position = jnp.arange(slot_count, dtype=jnp.int32)
    is_live = (position[None, :] < block_counts[:, None] * BLOCK) & (block_rows >= 0)
    source = jnp.where(is_live, block_rows // token_count, sources)
    matches = (source[:, :, None] == jnp.arange(sources, dtype=jnp.int32)[None, None, :]).astype(
        jnp.int32
    )
    order_rank = jnp.sum(jnp.cumsum(matches, axis=1) * matches, axis=2) - 1
    is_mine = is_live & (source == own_index)
    slot_target = jnp.where(
        is_mine, jnp.arange(experts, dtype=jnp.int32)[:, None] * CAP + order_rank, experts * CAP
    )
    local_values = jnp.where(is_mine, block_rows - own_index * token_count, token_count)
    local_row = (
        jnp.full((experts * CAP + 1,), token_count, jnp.int32)
        .at[slot_target.ravel()]
        .set(local_values.ravel())[: experts * CAP]
    )
    gate_mine = (
        jnp.zeros((experts * CAP + 1,), jnp.float32)
        .at[slot_target.ravel()]
        .set(jnp.where(is_mine, row_gates, 0.0).ravel())[: experts * CAP]
    )
    live_mine = lax.dynamic_index_in_dim(is_live, my_expert, 0, keepdims=False)
    rows_mine = lax.dynamic_index_in_dim(block_rows, my_expert, 0, keepdims=False)
    source_mine = lax.dynamic_index_in_dim(source, my_expert, 0, keepdims=False)
    rank_mine = lax.dynamic_index_in_dim(order_rank, my_expert, 0, keepdims=False)
    back_index = jnp.where(live_mine, source_mine * CAP + rank_mine, sources * CAP)
    blank_row = jnp.zeros((1, model_width), jnp.bfloat16)
    everyone = lax.all_gather(tokens, "exp", axis=0, tiled=True)
    row_pool = jnp.concatenate([everyone, blank_row], axis=0)
    routed = row_pool[jnp.where(live_mine, rows_mine, sources * token_count)]
    partial_rows = expert_block(routed, w_gate, w_up, w_down)
    outbound = (
        jnp.zeros((sources * CAP + 1, model_width), jnp.bfloat16).at[back_index].set(partial_rows)
    )
    outbound = outbound[: sources * CAP].reshape(sources, CAP, model_width)
    returned = lax.all_to_all(outbound, "exp", split_axis=0, concat_axis=0, tiled=True)
    summed = jnp.sum(
        returned.reshape(experts, per_expert, CAP, model_width), axis=1, dtype=jnp.float32
    )
    weighted = (summed * gate_mine.reshape(experts, CAP, 1)).reshape(experts * CAP, model_width)
    selector = (local_row[:, None] == jnp.arange(token_count, dtype=jnp.int32)[None, :]).astype(
        jnp.float32
    )
    gathered_sum = jnp.einsum("st,sd->td", selector, weighted, precision=lax.Precision.HIGHEST)
    share = lax.psum_scatter(gathered_sum, "hid", scatter_dimension=1, tiled=True)
    return share.astype(jnp.bfloat16)


def solution(mesh):
    small = mesh.shape["exp"] == SOURCES and mesh.shape["hid"] == 2

    def chosen(*args):
        return (local if small and args[5].shape[0] * 2 == SOURCES else local_wide)(*args)

    return jax.shard_map(
        chosen,
        mesh=mesh,
        in_specs=(
            P(("grp", "exp"), None),
            P(None, ("exp", "hid")),
            P(None, ("exp", "hid")),
            P(("exp", "hid"), None),
            P("grp"),
            P("grp", None),
            P("grp", None),
        ),
        out_specs=P(("grp", "exp"), "hid"),
        check_vma=False,
    )
```

```python
import functools

import jax
import jax.numpy as jnp
from jax import lax
from jax.experimental import pallas as pl
from jax.experimental.pallas import tpu as pltpu
from jax.sharding import PartitionSpec as P

BLOCK = 128
CAP = 3
TILE = 512
MIB = 1 << 20
ORDER = (0, 1, 6, 7, 2, 3, 4, 5)
SOURCES = len(ORDER)
GATE = 5_000_000_000
UP = 2_000_000_000
AHEAD = 20_000_000_000
HBM = pl.BlockSpec(memory_space=pltpu.HBM)
VMEM = pl.BlockSpec(memory_space=pltpu.VMEM)
SMEM = pl.BlockSpec(memory_space=pltpu.SMEM)


def in_hbm(x):
    return pltpu.with_memory_space_constraint(x, pltpu.HBM)


def in_smem(x):
    return pltpu.with_memory_space_constraint(x, pltpu.SMEM)


def in_vmem(x):
    return pltpu.with_memory_space_constraint(x, pltpu.VMEM)


def turned(i):
    return (1 + i + i // 2) % 2


def first_kernel(place_ref):
    side, own = lax.axis_index("hid"), lax.axis_index("exp")
    place_ref[0] = side
    place_ref[1] = own
    place_ref[2] = turned(own)
    place_ref[3] = lax.rem(side + turned(own), 2)


def first():
    return pl.pallas_call(
        first_kernel,
        out_shape=pltpu.SMEM((4,), jnp.int32),
        out_specs=SMEM,
        compiler_params=pltpu.CompilerParams(vmem_limit_bytes=2 * MIB),
        cost_estimate=pl.CostEstimate(flops=AHEAD, bytes_accessed=0, transcendentals=0),
    )()


def routed_gates(own, per_expert, count, counts_ref, rows_ref, gates_ref):
    experts, slots = rows_ref.shape
    expert = own // per_expert
    mine = lax.broadcasted_iota(jnp.int32, (experts, slots), 0) == expert
    rows = jnp.sum(jnp.where(mine, rows_ref[...], 0), axis=0, keepdims=True)
    gates = jnp.sum(jnp.where(mine, gates_ref[...], 0.0), axis=0, keepdims=True)
    position = lax.broadcasted_iota(jnp.int32, (1, slots), 1)
    here = lax.broadcasted_iota(jnp.int32, counts_ref.shape, 1) == expert
    blocks = jnp.sum(jnp.where(here, counts_ref[...], 0), axis=1, keepdims=True)
    rows = jnp.where(position < blocks * BLOCK, rows, -1)
    line = lax.broadcasted_iota(jnp.int32, (SOURCES * count, slots), 0)
    block = line // count
    source = jnp.zeros_like(line)
    for at, k in enumerate(ORDER):
        source = jnp.where(block == at, own ^ k, source)
    token = source * count + lax.rem(line, count)
    return jnp.sum(jnp.where(rows == token, gates, 0.0), axis=1, keepdims=True)


def stack_kernel(*refs):
    for at, ref in enumerate(refs[:-1]):
        refs[-1][at] = ref[...]


def stack(pieces):
    return pl.pallas_call(
        stack_kernel,
        out_shape=jax.ShapeDtypeStruct((len(pieces), *pieces[0].shape), pieces[0].dtype),
        in_specs=[VMEM] * len(pieces),
        out_specs=VMEM,
        compiler_params=pltpu.CompilerParams(vmem_limit_bytes=2 * MIB),
    )(*pieces)


def gate_kernel(
    per_expert,
    place_ref,
    counts_ref,
    tokens_ref,
    mine_ref,
    got_ref,
    rows_ref,
    gates_ref,
    wg_ref,
    x_ref,
    act_ref,
    g_ref,
    wide,
):
    sets, count, _ = mine_ref.shape
    g = routed_gates(place_ref[1], per_expert, count, counts_ref, rows_ref, gates_ref)
    g_ref[...] = jnp.broadcast_to(g, g_ref.shape)
    for j in range(sets):
        rows = pl.ds(j * count, count)
        wide[place_ref[0], rows, :] = mine_ref[j].astype(jnp.float32)
        wide[1 - place_ref[0], rows, :] = got_ref[j].astype(jnp.float32)
    wide[0, pl.ds(0, count), :] = tokens_ref[...].astype(jnp.float32)
    x_ref[...] = wide[...].reshape(x_ref.shape).astype(jnp.bfloat16)

    for n in range(wg_ref.shape[1] // TILE):
        cols = pl.ds(n * TILE, TILE)
        gate = jnp.dot(x_ref[...], wg_ref[:, cols], preferred_element_type=jnp.float32)
        act_ref[:, cols] = gate / (1.0 + jnp.exp(-gate))


def gate_rows(place, counts, tokens, mine, got, block_rows, row_gates, wg):
    total = 2 * mine.shape[0] * mine.shape[1]
    depth, width = wg.shape
    return pl.pallas_call(
        functools.partial(gate_kernel, SOURCES // block_rows.shape[0]),
        out_shape=(
            jax.ShapeDtypeStruct((total, depth), jnp.bfloat16),
            jax.ShapeDtypeStruct((total, width), jnp.float32),
            jax.ShapeDtypeStruct((total, 128), jnp.float32),
        ),
        in_specs=[SMEM] + [VMEM] * 7,
        out_specs=(VMEM,) * 3,
        scratch_shapes=[pltpu.VMEM((2, total // 2, depth), jnp.float32)],
        compiler_params=pltpu.CompilerParams(vmem_limit_bytes=2 * MIB),
        cost_estimate=pl.CostEstimate(flops=GATE, bytes_accessed=0, transcendentals=total * width),
    )(in_smem(place), counts.reshape(1, -1), tokens, mine, got, block_rows, row_gates, in_vmem(wg))


def up_kernel(x_ref, act_ref, wu_ref, h_out):
    for n in range(wu_ref.shape[1] // TILE):
        cols = pl.ds(n * TILE, TILE)
        up = jnp.dot(x_ref[...], wu_ref[:, cols], preferred_element_type=jnp.float32)
        h_out[:, cols] = (act_ref[:, cols] * up).astype(jnp.bfloat16)


def hidden_rows(x, act, wu):
    return pl.pallas_call(
        up_kernel,
        out_shape=jax.ShapeDtypeStruct(act.shape, jnp.bfloat16),
        in_specs=[VMEM] * 3,
        out_specs=VMEM,
        compiler_params=pltpu.CompilerParams(vmem_limit_bytes=2 * MIB),
        cost_estimate=pl.CostEstimate(flops=UP, bytes_accessed=0, transcendentals=0),
    )(x, act, in_vmem(wu))


def down_kernel(other, place_ref, h_ref, wd_ref, out_ref):
    half = wd_ref.shape[1] // 2
    mine = place_ref[3]
    base = (1 - mine if other else mine) * half
    for n in range(half // TILE):
        cols = pl.ds(pl.multiple_of(base + n * TILE, TILE), TILE)
        part = jnp.dot(h_ref[...], wd_ref[:, cols], preferred_element_type=jnp.float32)
        out_ref[:, pl.ds(n * TILE, TILE)] = part.astype(out_ref.dtype)


def down_half(place, hidden, wd, other, dtype):
    rows, depth = hidden.shape
    half = wd.shape[1] // 2
    return pl.pallas_call(
        functools.partial(down_kernel, other),
        out_shape=jax.ShapeDtypeStruct((rows, half), dtype),
        in_specs=[SMEM, VMEM, VMEM],
        out_specs=VMEM,
        compiler_params=pltpu.CompilerParams(vmem_limit_bytes=2 * MIB),
        cost_estimate=pl.CostEstimate(flops=2 * rows * depth * half, bytes_accessed=0, transcendentals=0),
    )(in_smem(place), hidden, in_vmem(wd))


def near_kernel(g_ref, keep_ref, got_ref, own_ref, *out_refs):
    both = (keep_ref[...] + got_ref[...].astype(jnp.float32)) * g_ref[:, :1]
    pair, count, _ = own_ref.shape
    group = SOURCES // pair
    for at, k in enumerate(ORDER):
        out_ref = (own_ref, *out_refs)[k % group]
        out_ref[k // group] = both[at * count : (at + 1) * count].astype(out_ref.dtype)


def near(g, keep, got):
    rows, width = keep.shape
    group = SOURCES // 2
    shape = (2, rows // SOURCES, width)
    return pl.pallas_call(
        near_kernel,
        out_shape=(jax.ShapeDtypeStruct(shape, jnp.float32),)
        + (jax.ShapeDtypeStruct(shape, jnp.bfloat16),) * (group - 1),
        in_specs=[VMEM] * 3,
        out_specs=(VMEM,) * group,
        compiler_params=pltpu.CompilerParams(vmem_limit_bytes=2 * MIB),
    )(g, keep, got)


def far_kernel(*refs):
    *part_refs, own_ref, turn_ref, next_ref = refs
    for i, out_refs in enumerate(((own_ref, turn_ref), (next_ref,))):
        total = part_refs[0][i]
        for part_ref in part_refs[1:]:
            total = total + part_ref[i].astype(jnp.float32)
        for out_ref in out_refs:
            out_ref[...] = total.astype(out_ref.dtype)


def far(parts):
    shape = parts[0].shape[1:]
    return pl.pallas_call(
        far_kernel,
        out_shape=(jax.ShapeDtypeStruct(shape, jnp.float32),) + (jax.ShapeDtypeStruct(shape, jnp.bfloat16),) * 2,
        in_specs=[VMEM] * len(parts),
        out_specs=(VMEM,) * 3,
        compiler_params=pltpu.CompilerParams(vmem_limit_bytes=2 * MIB),
    )(*parts)


def sum_kernel(place_ref, own_ref, got_ref, turned_ref, out_ref):
    own = jnp.where(place_ref[2] == 1, turned_ref[...].astype(jnp.float32), own_ref[...])
    out_ref[...] = (own + got_ref[...].astype(jnp.float32)).astype(out_ref.dtype)


def final_sum(place, own, got, other_core):
    return pl.pallas_call(
        sum_kernel,
        out_shape=jax.ShapeDtypeStruct(own.shape, jnp.bfloat16),
        in_specs=[SMEM] + [VMEM] * 3,
        out_specs=VMEM,
        compiler_params=pltpu.CompilerParams(vmem_limit_bytes=2 * MIB),
    )(in_smem(place), own, got, other_core)


def swapped(x, k):
    pairs = [
        (2 * i + side, 2 * (i ^ k) + (side + turned(i) + turned(i ^ k)) % 2) for i in range(SOURCES) for side in range(2)
    ]
    return lax.ppermute(x, ("exp", "hid"), pairs)


def sent_home(x, k):
    pairs = [(2 * i + side, 2 * (i ^ k) + (side + turned(i)) % 2) for i in range(SOURCES) for side in range(2)]
    return lax.ppermute(x, ("exp", "hid"), pairs)


def fetched(x, first, second):
    return lax.ppermute(
        x,
        ("exp", "hid"),
        [(2 * i + 1 - side, 2 * (i ^ k) + side) for side, k in enumerate((first, second)) for i in range(SOURCES)],
    )


def swap_cores(x):
    return lax.ppermute(x, "hid", [(0, 1), (1, 0)])


def local(tokens, w_gate, w_up, w_down, block_counts, block_rows, row_gates):
    place = first()
    tokens, place, counts = lax.optimization_barrier((tokens, place, block_counts))
    half = SOURCES // 2
    pieces = [fetched(tokens, ORDER[half], ORDER[half])]
    pieces += [fetched(tokens, ORDER[b], ORDER[half + b]) for b in range(1, half)]
    mine = stack(pieces)
    got = swap_cores(mine)
    x, act, g = gate_rows(place, counts, tokens, mine, got, block_rows, row_gates, w_gate)
    hidden = hidden_rows(x, act, w_up)
    send = down_half(place, hidden, w_down, True, jnp.bfloat16)
    keep = down_half(place, hidden, w_down, False, jnp.float32)
    own, *parts = near(g, keep, swap_cores(send))
    returned = [swapped(parts[j - 1], j) for j in range(half - 1, 0, -1)]
    own, turn, other = far([own, *returned])
    return final_sum(place, own, sent_home(other, half), swap_cores(turn))


def expert_block(segment, w_gate, w_up, w_down):
    gate_act = jnp.dot(segment, w_gate, preferred_element_type=jnp.float32)
    up_act = jnp.dot(segment, w_up, preferred_element_type=jnp.float32)
    hidden = (jax.nn.silu(gate_act) * up_act).astype(jnp.bfloat16)
    return jnp.dot(hidden, w_down, preferred_element_type=jnp.float32).astype(jnp.bfloat16)


def local_wide(tokens, w_gate, w_up, w_down, block_counts, block_rows, row_gates):
    sources = lax.axis_size("exp")
    own_index = lax.axis_index("exp")
    token_count = tokens.shape[0]
    model_width = tokens.shape[1]
    experts = block_rows.shape[0]
    slot_count = block_rows.shape[1]
    per_expert = sources // experts
    my_expert = own_index // per_expert
    position = jnp.arange(slot_count, dtype=jnp.int32)
    is_live = (position[None, :] < block_counts[:, None] * BLOCK) & (block_rows >= 0)
    source = jnp.where(is_live, block_rows // token_count, sources)
    matches = (source[:, :, None] == jnp.arange(sources, dtype=jnp.int32)[None, None, :]).astype(
        jnp.int32
    )
    order_rank = jnp.sum(jnp.cumsum(matches, axis=1) * matches, axis=2) - 1
    is_mine = is_live & (source == own_index)
    slot_target = jnp.where(
        is_mine, jnp.arange(experts, dtype=jnp.int32)[:, None] * CAP + order_rank, experts * CAP
    )
    local_values = jnp.where(is_mine, block_rows - own_index * token_count, token_count)
    local_row = (
        jnp.full((experts * CAP + 1,), token_count, jnp.int32)
        .at[slot_target.ravel()]
        .set(local_values.ravel())[: experts * CAP]
    )
    gate_mine = (
        jnp.zeros((experts * CAP + 1,), jnp.float32)
        .at[slot_target.ravel()]
        .set(jnp.where(is_mine, row_gates, 0.0).ravel())[: experts * CAP]
    )
    live_mine = lax.dynamic_index_in_dim(is_live, my_expert, 0, keepdims=False)
    rows_mine = lax.dynamic_index_in_dim(block_rows, my_expert, 0, keepdims=False)
    source_mine = lax.dynamic_index_in_dim(source, my_expert, 0, keepdims=False)
    rank_mine = lax.dynamic_index_in_dim(order_rank, my_expert, 0, keepdims=False)
    back_index = jnp.where(live_mine, source_mine * CAP + rank_mine, sources * CAP)
    blank_row = jnp.zeros((1, model_width), jnp.bfloat16)
    everyone = lax.all_gather(tokens, "exp", axis=0, tiled=True)
    row_pool = jnp.concatenate([everyone, blank_row], axis=0)
    routed = row_pool[jnp.where(live_mine, rows_mine, sources * token_count)]
    partial_rows = expert_block(routed, w_gate, w_up, w_down)
    outbound = (
        jnp.zeros((sources * CAP + 1, model_width), jnp.bfloat16).at[back_index].set(partial_rows)
    )
    outbound = outbound[: sources * CAP].reshape(sources, CAP, model_width)
    returned = lax.all_to_all(outbound, "exp", split_axis=0, concat_axis=0, tiled=True)
    summed = jnp.sum(
        returned.reshape(experts, per_expert, CAP, model_width), axis=1, dtype=jnp.float32
    )
    weighted = (summed * gate_mine.reshape(experts, CAP, 1)).reshape(experts * CAP, model_width)
    selector = (local_row[:, None] == jnp.arange(token_count, dtype=jnp.int32)[None, :]).astype(
        jnp.float32
    )
    gathered_sum = jnp.einsum("st,sd->td", selector, weighted, precision=lax.Precision.HIGHEST)
    share = lax.psum_scatter(gathered_sum, "hid", scatter_dimension=1, tiled=True)
    return share.astype(jnp.bfloat16)


def solution(mesh):
    small = mesh.shape["exp"] == SOURCES and mesh.shape["hid"] == 2

    def chosen(*args):
        return (local if small and args[5].shape[0] * 2 == SOURCES else local_wide)(*args)

    return jax.shard_map(
        chosen,
        mesh=mesh,
        in_specs=(
            P(("grp", "exp"), None),
            P(None, ("exp", "hid")),
            P(None, ("exp", "hid")),
            P(("exp", "hid"), None),
            P("grp"),
            P("grp", None),
            P("grp", None),
        ),
        out_specs=P(("grp", "exp"), "hid"),
        check_vma=False,
    )
```

```python
import functools

import jax
import jax.numpy as jnp
from jax import lax
from jax.experimental import pallas as pl
from jax.experimental.pallas import tpu as pltpu
from jax.sharding import PartitionSpec as P

BLOCK = 128
CAP = 3
TILE = 512
MIB = 1 << 20
ORDER = (0, 3, 6, 7, 2, 1, 4, 5)
SOURCES = len(ORDER)
GATE = 5_000_000_000
UP = 2_000_000_000
AHEAD = 20_000_000_000
HBM = pl.BlockSpec(memory_space=pltpu.HBM)
VMEM = pl.BlockSpec(memory_space=pltpu.VMEM)
SMEM = pl.BlockSpec(memory_space=pltpu.SMEM)


def in_hbm(x):
    return pltpu.with_memory_space_constraint(x, pltpu.HBM)


def in_smem(x):
    return pltpu.with_memory_space_constraint(x, pltpu.SMEM)


def in_vmem(x):
    return pltpu.with_memory_space_constraint(x, pltpu.VMEM)


def turned(i):
    return (1 + i + i // 2) % 2


def first_kernel(place_ref):
    side, own = lax.axis_index("hid"), lax.axis_index("exp")
    place_ref[0] = side
    place_ref[1] = own
    place_ref[2] = turned(own)
    place_ref[3] = lax.rem(side + turned(own), 2)


def first():
    return pl.pallas_call(
        first_kernel,
        out_shape=pltpu.SMEM((4,), jnp.int32),
        out_specs=SMEM,
        compiler_params=pltpu.CompilerParams(vmem_limit_bytes=2 * MIB),
        cost_estimate=pl.CostEstimate(flops=AHEAD, bytes_accessed=0, transcendentals=0),
    )()


def routed_gates(own, per_expert, count, counts_ref, rows_ref, gates_ref):
    experts, slots = rows_ref.shape
    expert = own // per_expert
    mine = lax.broadcasted_iota(jnp.int32, (experts, slots), 0) == expert
    rows = jnp.sum(jnp.where(mine, rows_ref[...], 0), axis=0, keepdims=True)
    gates = jnp.sum(jnp.where(mine, gates_ref[...], 0.0), axis=0, keepdims=True)
    position = lax.broadcasted_iota(jnp.int32, (1, slots), 1)
    here = lax.broadcasted_iota(jnp.int32, counts_ref.shape, 1) == expert
    blocks = jnp.sum(jnp.where(here, counts_ref[...], 0), axis=1, keepdims=True)
    rows = jnp.where(position < blocks * BLOCK, rows, -1)
    line = lax.broadcasted_iota(jnp.int32, (SOURCES * count, slots), 0)
    block = line // count
    source = jnp.zeros_like(line)
    for at, k in enumerate(ORDER):
        source = jnp.where(block == at, own ^ k, source)
    token = source * count + lax.rem(line, count)
    return jnp.sum(jnp.where(rows == token, gates, 0.0), axis=1, keepdims=True)


def stack_kernel(*refs):
    for at, ref in enumerate(refs[:-1]):
        refs[-1][at] = ref[...]


def stack(pieces):
    return pl.pallas_call(
        stack_kernel,
        out_shape=jax.ShapeDtypeStruct((len(pieces), *pieces[0].shape), pieces[0].dtype),
        in_specs=[VMEM] * len(pieces),
        out_specs=VMEM,
        compiler_params=pltpu.CompilerParams(vmem_limit_bytes=2 * MIB),
    )(*pieces)


def gate_kernel(
    per_expert,
    place_ref,
    counts_ref,
    tokens_ref,
    mine_ref,
    got_ref,
    rows_ref,
    gates_ref,
    wg_ref,
    x_ref,
    act_ref,
    g_ref,
    wide,
):
    sets, count, _ = mine_ref.shape
    g = routed_gates(place_ref[1], per_expert, count, counts_ref, rows_ref, gates_ref)
    g_ref[...] = jnp.broadcast_to(g, g_ref.shape)
    for j in range(sets):
        rows = pl.ds(j * count, count)
        wide[place_ref[0], rows, :] = mine_ref[j].astype(jnp.float32)
        wide[1 - place_ref[0], rows, :] = got_ref[j].astype(jnp.float32)
    wide[0, pl.ds(0, count), :] = tokens_ref[...].astype(jnp.float32)
    x_ref[...] = wide[...].reshape(x_ref.shape).astype(jnp.bfloat16)

    for n in range(wg_ref.shape[1] // TILE):
        cols = pl.ds(n * TILE, TILE)
        gate = jnp.dot(x_ref[...], wg_ref[:, cols], preferred_element_type=jnp.float32)
        act_ref[:, cols] = gate / (1.0 + jnp.exp(-gate))


def gate_rows(place, counts, tokens, mine, got, block_rows, row_gates, wg):
    total = 2 * mine.shape[0] * mine.shape[1]
    depth, width = wg.shape
    return pl.pallas_call(
        functools.partial(gate_kernel, SOURCES // block_rows.shape[0]),
        out_shape=(
            jax.ShapeDtypeStruct((total, depth), jnp.bfloat16),
            jax.ShapeDtypeStruct((total, width), jnp.float32),
            jax.ShapeDtypeStruct((total, 128), jnp.float32),
        ),
        in_specs=[SMEM] + [VMEM] * 7,
        out_specs=(VMEM,) * 3,
        scratch_shapes=[pltpu.VMEM((2, total // 2, depth), jnp.float32)],
        compiler_params=pltpu.CompilerParams(vmem_limit_bytes=2 * MIB),
        cost_estimate=pl.CostEstimate(flops=GATE, bytes_accessed=0, transcendentals=total * width),
    )(in_smem(place), counts.reshape(1, -1), tokens, mine, got, block_rows, row_gates, in_vmem(wg))


def up_kernel(x_ref, act_ref, wu_ref, h_out):
    for n in range(wu_ref.shape[1] // TILE):
        cols = pl.ds(n * TILE, TILE)
        up = jnp.dot(x_ref[...], wu_ref[:, cols], preferred_element_type=jnp.float32)
        h_out[:, cols] = (act_ref[:, cols] * up).astype(jnp.bfloat16)


def hidden_rows(x, act, wu):
    return pl.pallas_call(
        up_kernel,
        out_shape=jax.ShapeDtypeStruct(act.shape, jnp.bfloat16),
        in_specs=[VMEM] * 3,
        out_specs=VMEM,
        compiler_params=pltpu.CompilerParams(vmem_limit_bytes=2 * MIB),
        cost_estimate=pl.CostEstimate(flops=UP, bytes_accessed=0, transcendentals=0),
    )(x, act, in_vmem(wu))


def down_kernel(other, place_ref, h_ref, wd_ref, out_ref):
    half = wd_ref.shape[1] // 2
    mine = place_ref[3]
    base = (1 - mine if other else mine) * half
    for n in range(half // TILE):
        cols = pl.ds(pl.multiple_of(base + n * TILE, TILE), TILE)
        part = jnp.dot(h_ref[...], wd_ref[:, cols], preferred_element_type=jnp.float32)
        out_ref[:, pl.ds(n * TILE, TILE)] = part.astype(out_ref.dtype)


def down_half(place, hidden, wd, other, dtype):
    rows, depth = hidden.shape
    half = wd.shape[1] // 2
    return pl.pallas_call(
        functools.partial(down_kernel, other),
        out_shape=jax.ShapeDtypeStruct((rows, half), dtype),
        in_specs=[SMEM, VMEM, VMEM],
        out_specs=VMEM,
        compiler_params=pltpu.CompilerParams(vmem_limit_bytes=2 * MIB),
        cost_estimate=pl.CostEstimate(flops=2 * rows * depth * half, bytes_accessed=0, transcendentals=0),
    )(in_smem(place), hidden, in_vmem(wd))


def near_kernel(g_ref, keep_ref, got_ref, own_ref, *out_refs):
    both = (keep_ref[...] + got_ref[...].astype(jnp.float32)) * g_ref[:, :1]
    pair, count, _ = own_ref.shape
    group = SOURCES // pair
    for at, k in enumerate(ORDER):
        out_ref = (own_ref, *out_refs)[k % group]
        out_ref[k // group] = both[at * count : (at + 1) * count].astype(out_ref.dtype)


def near(g, keep, got):
    rows, width = keep.shape
    group = SOURCES // 2
    shape = (2, rows // SOURCES, width)
    return pl.pallas_call(
        near_kernel,
        out_shape=(jax.ShapeDtypeStruct(shape, jnp.float32),)
        + (jax.ShapeDtypeStruct(shape, jnp.bfloat16),) * (group - 1),
        in_specs=[VMEM] * 3,
        out_specs=(VMEM,) * group,
        compiler_params=pltpu.CompilerParams(vmem_limit_bytes=2 * MIB),
    )(g, keep, got)


def far_kernel(*refs):
    *part_refs, own_ref, turn_ref, next_ref = refs
    for i, out_refs in enumerate(((own_ref, turn_ref), (next_ref,))):
        total = part_refs[0][i]
        for part_ref in part_refs[1:]:
            total = total + part_ref[i].astype(jnp.float32)
        for out_ref in out_refs:
            out_ref[...] = total.astype(out_ref.dtype)


def far(parts):
    shape = parts[0].shape[1:]
    return pl.pallas_call(
        far_kernel,
        out_shape=(jax.ShapeDtypeStruct(shape, jnp.float32),) + (jax.ShapeDtypeStruct(shape, jnp.bfloat16),) * 2,
        in_specs=[VMEM] * len(parts),
        out_specs=(VMEM,) * 3,
        compiler_params=pltpu.CompilerParams(vmem_limit_bytes=2 * MIB),
    )(*parts)


def sum_kernel(place_ref, own_ref, got_ref, turned_ref, out_ref):
    own = jnp.where(place_ref[2] == 1, turned_ref[...].astype(jnp.float32), own_ref[...])
    out_ref[...] = (own + got_ref[...].astype(jnp.float32)).astype(out_ref.dtype)


def final_sum(place, own, got, other_core):
    return pl.pallas_call(
        sum_kernel,
        out_shape=jax.ShapeDtypeStruct(own.shape, jnp.bfloat16),
        in_specs=[SMEM] + [VMEM] * 3,
        out_specs=VMEM,
        compiler_params=pltpu.CompilerParams(vmem_limit_bytes=2 * MIB),
    )(in_smem(place), own, got, other_core)


def swapped(x, k):
    pairs = [
        (2 * i + side, 2 * (i ^ k) + (side + turned(i) + turned(i ^ k)) % 2) for i in range(SOURCES) for side in range(2)
    ]
    return lax.ppermute(x, ("exp", "hid"), pairs)


def sent_home(x, k):
    pairs = [(2 * i + side, 2 * (i ^ k) + (side + turned(i)) % 2) for i in range(SOURCES) for side in range(2)]
    return lax.ppermute(x, ("exp", "hid"), pairs)


def fetched(x, first, second):
    return lax.ppermute(
        x,
        ("exp", "hid"),
        [(2 * i + 1 - side, 2 * (i ^ k) + side) for side, k in enumerate((first, second)) for i in range(SOURCES)],
    )


def swap_cores(x):
    return lax.ppermute(x, "hid", [(0, 1), (1, 0)])


def local(tokens, w_gate, w_up, w_down, block_counts, block_rows, row_gates):
    place = first()
    tokens, place, counts = lax.optimization_barrier((tokens, place, block_counts))
    half = SOURCES // 2
    pieces = [fetched(tokens, ORDER[half], ORDER[half])]
    pieces += [fetched(tokens, ORDER[b], ORDER[half + b]) for b in range(1, half)]
    mine = stack(pieces)
    got = swap_cores(mine)
    x, act, g = gate_rows(place, counts, tokens, mine, got, block_rows, row_gates, w_gate)
    hidden = hidden_rows(x, act, w_up)
    send = down_half(place, hidden, w_down, True, jnp.bfloat16)
    keep = down_half(place, hidden, w_down, False, jnp.float32)
    own, *parts = near(g, keep, swap_cores(send))
    returned = [swapped(parts[j - 1], j) for j in range(half - 1, 0, -1)]
    own, turn, other = far([own, *returned])
    return final_sum(place, own, sent_home(other, half), swap_cores(turn))


def expert_block(segment, w_gate, w_up, w_down):
    gate_act = jnp.dot(segment, w_gate, preferred_element_type=jnp.float32)
    up_act = jnp.dot(segment, w_up, preferred_element_type=jnp.float32)
    hidden = (jax.nn.silu(gate_act) * up_act).astype(jnp.bfloat16)
    return jnp.dot(hidden, w_down, preferred_element_type=jnp.float32).astype(jnp.bfloat16)


def local_wide(tokens, w_gate, w_up, w_down, block_counts, block_rows, row_gates):
    sources = lax.axis_size("exp")
    own_index = lax.axis_index("exp")
    token_count = tokens.shape[0]
    model_width = tokens.shape[1]
    experts = block_rows.shape[0]
    slot_count = block_rows.shape[1]
    per_expert = sources // experts
    my_expert = own_index // per_expert
    position = jnp.arange(slot_count, dtype=jnp.int32)
    is_live = (position[None, :] < block_counts[:, None] * BLOCK) & (block_rows >= 0)
    source = jnp.where(is_live, block_rows // token_count, sources)
    matches = (source[:, :, None] == jnp.arange(sources, dtype=jnp.int32)[None, None, :]).astype(
        jnp.int32
    )
    order_rank = jnp.sum(jnp.cumsum(matches, axis=1) * matches, axis=2) - 1
    is_mine = is_live & (source == own_index)
    slot_target = jnp.where(
        is_mine, jnp.arange(experts, dtype=jnp.int32)[:, None] * CAP + order_rank, experts * CAP
    )
    local_values = jnp.where(is_mine, block_rows - own_index * token_count, token_count)
    local_row = (
        jnp.full((experts * CAP + 1,), token_count, jnp.int32)
        .at[slot_target.ravel()]
        .set(local_values.ravel())[: experts * CAP]
    )
    gate_mine = (
        jnp.zeros((experts * CAP + 1,), jnp.float32)
        .at[slot_target.ravel()]
        .set(jnp.where(is_mine, row_gates, 0.0).ravel())[: experts * CAP]
    )
    live_mine = lax.dynamic_index_in_dim(is_live, my_expert, 0, keepdims=False)
    rows_mine = lax.dynamic_index_in_dim(block_rows, my_expert, 0, keepdims=False)
    source_mine = lax.dynamic_index_in_dim(source, my_expert, 0, keepdims=False)
    rank_mine = lax.dynamic_index_in_dim(order_rank, my_expert, 0, keepdims=False)
    back_index = jnp.where(live_mine, source_mine * CAP + rank_mine, sources * CAP)
    blank_row = jnp.zeros((1, model_width), jnp.bfloat16)
    everyone = lax.all_gather(tokens, "exp", axis=0, tiled=True)
    row_pool = jnp.concatenate([everyone, blank_row], axis=0)
    routed = row_pool[jnp.where(live_mine, rows_mine, sources * token_count)]
    partial_rows = expert_block(routed, w_gate, w_up, w_down)
    outbound = (
        jnp.zeros((sources * CAP + 1, model_width), jnp.bfloat16).at[back_index].set(partial_rows)
    )
    outbound = outbound[: sources * CAP].reshape(sources, CAP, model_width)
    returned = lax.all_to_all(outbound, "exp", split_axis=0, concat_axis=0, tiled=True)
    summed = jnp.sum(
        returned.reshape(experts, per_expert, CAP, model_width), axis=1, dtype=jnp.float32
    )
    weighted = (summed * gate_mine.reshape(experts, CAP, 1)).reshape(experts * CAP, model_width)
    selector = (local_row[:, None] == jnp.arange(token_count, dtype=jnp.int32)[None, :]).astype(
        jnp.float32
    )
    gathered_sum = jnp.einsum("st,sd->td", selector, weighted, precision=lax.Precision.HIGHEST)
    share = lax.psum_scatter(gathered_sum, "hid", scatter_dimension=1, tiled=True)
    return share.astype(jnp.bfloat16)


def solution(mesh):
    small = mesh.shape["exp"] == SOURCES and mesh.shape["hid"] == 2

    def chosen(*args):
        return (local if small and args[5].shape[0] * 2 == SOURCES else local_wide)(*args)

    return jax.shard_map(
        chosen,
        mesh=mesh,
        in_specs=(
            P(("grp", "exp"), None),
            P(None, ("exp", "hid")),
            P(None, ("exp", "hid")),
            P(("exp", "hid"), None),
            P("grp"),
            P("grp", None),
            P("grp", None),
        ),
        out_specs=P(("grp", "exp"), "hid"),
        check_vma=False,
    )
```
